256 devices in a mesh: seq: 32 (over y, x, core), ch: 8 (over z).
Axes of the slice: x: 4, y: 4, z: 8, core: 2. Of those that a mesh axis runs over, the one named last changes fastest.
Arguments:
- hidden_in: bfloat16 [8192, 32768], P('ch', 'seq'), may hold values from -6 to 6
- w_in: bfloat16 [8192, 384], P('ch'), may hold values from -0.0625 to 0.0625
- short_taps: float32 [3, 384], P(None, 'ch'), may hold values from -4 to 4
- rates: float32 [128, 16], P('ch'), may hold values from 1.5258789e-05 to 0.05
- residues: float32 [128, 16], P('ch'), may hold values from -3 to 3
- skip_gain: float32 [128], P('ch'), may hold values from -3 to 3
- w_out: bfloat16 [8192, 128], P('ch'), may hold values from -0.5 to 0.5
Outputs:
- mixed: bfloat16 [8192, 32768], P('ch', 'seq')
The draws below stay inside these ranges and needn't reach their ends.
All inputs are finite; a program needn't handle non-finite values.
Results may differ from the reference program's by a relative error of at most 0.0075.
Values may be sent and summed in bfloat16 or wider, within the bound.
A program may use at most 64 MiB of HBM per device.

```python
import math
import jax
import jax.numpy as jnp
from jax import lax

D = 8192
CH = 128
MODES = 16
TOKENS = 32768


def level_of(key, extent, split, smallest, high):
    factor_of, own = 1.0, jax.random.fold_in(key, 6)
    for position, shards_of in split:
        draws = jnp.exp(jax.random.uniform(jax.random.fold_in(own, position), (shards_of,), jnp.float32, smallest / len(split), high / len(split)))
        factor_of = factor_of * jnp.repeat(draws, extent[position] // shards_of).reshape([-1 if axis == position else 1 for axis in range(len(extent))])
    return factor_of


def gaussian(own_key, extent, spread, bound, cuts=(), dtype=jnp.bfloat16):
    values = jax.random.normal(own_key, extent, jnp.float32) * spread
    if len(cuts) > 0:
        values = level_of(own_key, extent, cuts, -0.22, 0.18) * values
    return jnp.clip(values, min=-bound, max=bound).astype(dtype)


def setup_inputs(seed: int = 0) -> dict:
    key_of = jax.random.split(jax.random.key(seed), 8)
    hidden_in = gaussian(key_of[0], (D, TOKENS), 1.0, 6.0, ((0, 8), (1, 32)))
    w_in = gaussian(key_of[1], (D, 3 * CH), D ** -0.5, 0.0625, ((0, 8),))
    short_taps = gaussian(key_of[2], (3, 3 * CH), 0.6, 4.0, ((1, 8),), jnp.float32)
    rates = jnp.clip(jnp.exp(math.log(0.05) - 8.094623 * jax.random.uniform(key_of[3], (CH, MODES), jnp.float32) ** level_of(key_of[3], (CH, MODES), ((0, 8),), -0.2, 0.2)), 1.52587890625e-05, 0.05)
    residues = gaussian(key_of[4], (CH, MODES), 0.5, 3.0, ((0, 8),), jnp.float32)
    skip_gain = gaussian(key_of[5], (CH,), 0.5, 3.0, ((0, 8),), jnp.float32)
    w_out = gaussian(key_of[6], (D, CH), CH ** -0.5, 0.5, ((0, 8),))
    return dict(hidden_in=hidden_in, w_in=w_in, short_taps=short_taps, rates=rates, residues=residues, skip_gain=skip_gain, w_out=w_out)


def reference(hidden_in, w_in, short_taps, rates, residues, skip_gain, w_out):
    featurized = jnp.dot(w_in.T, hidden_in, preferred_element_type=jnp.float32).astype(jnp.bfloat16)
    widened = featurized.astype(jnp.float32)
    padded = jnp.pad(widened, ((0, 0), (2, 0)))
    short = short_taps[0][:, None] * padded[:, 2:] + short_taps[1][:, None] * padded[:, 1:-1] + short_taps[2][:, None] * padded[:, :-2]
    grouped = short.reshape(CH, 3, TOKENS)
    query = grouped[:, 0]
    driven_low = lax.optimization_barrier((grouped[:, 1] * grouped[:, 2]).astype(jnp.bfloat16))
    driven = driven_low.astype(jnp.float32)
    positions = jnp.arange(TOKENS).astype(jnp.float32)
    decay = jnp.exp(-rates[:, :, None] * positions[None, None, :])
    impulse = lax.optimization_barrier(jnp.sum((residues * jnp.sqrt(rates))[:, :, None] * decay, axis=1))
    length_all = 2 * TOKENS
    spectrum = jnp.fft.rfft(driven, n=length_all, axis=1) * jnp.fft.rfft(impulse, n=length_all, axis=1)
    long_conv = jnp.fft.irfft(spectrum, n=length_all, axis=1)[:, :TOKENS].astype(jnp.float32)
    gated = (query * (long_conv + skip_gain[:, None] * driven)).astype(jnp.bfloat16)
    return jnp.dot(w_out, gated, preferred_element_type=jnp.float32).astype(jnp.bfloat16)
```

```python
import functools

import jax
import jax.numpy as jnp
from jax import lax
from jax.experimental import pallas as pl
from jax.experimental.pallas import tpu as pltpu
from jax.sharding import PartitionSpec as P

MESH = pl.DeviceIdType.MESH
f32 = jnp.float32
bf16 = jnp.bfloat16
HIGH = lax.Precision.HIGHEST
NT = (((1,), (1,)), ((), ()))
NN = (((1,), (0,)), ((), ()))
CL = 128
ROW = 8


def mm(a, b, dims=NN, precision=None):
    return lax.dot_general(a, b, dims, precision=precision, preferred_element_type=f32)


def halves(x):
    hi = x.astype(bf16)
    return hi, (x - hi.astype(f32)).astype(bf16)


def iota(shape, dim):
    return lax.broadcasted_iota(jnp.int32, shape, dim)


def conv_kernel(
    n_seq,
    n_ch,
    hid,
    w_ref,
    taps_ref,
    rates_ref,
    res_ref,
    skip_ref,
    out_ref,
    hidv,
    wt,
    part,
    kv_s,
    kv_r,
    q_s,
    q_r,
    tot,
    halo_s,
    halo_r,
    gath,
    st0,
    st1,
    st2,
    par,
    e_hl,
    p_hl,
    tcat,
    dscr,
    yscr,
    xscr,
    load_sem,
    kv_ss,
    kv_rs,
    q_ss,
    q_rs,
    halo_ss,
    halo_rs,
    st1_ss,
    st1_rs,
    st2_ss,
    st2_rs,
    ag_ss,
    ag_rs,
):
    p = lax.axis_index("seq")
    z = lax.axis_index("ch")
    depth, length = hid.shape
    rows = w_ref.shape[1]
    per = rows // n_ch
    cs = per // 3
    nm = rates_ref.shape[1]
    st = cs * nm
    half = length // 2
    nk = length // CL
    quarter = length // 4
    row_y = p // ROW
    r = p % ROW
    n_y = n_seq // ROW

    def zz(k):
        return lax.rem(z + (k + n_ch), n_ch)

    ring = (zz(1), zz(-1))

    loads = []
    for i in (3, 2, 1, 0):
        cp = pltpu.make_async_copy(
            hid.at[:, pl.ds(i * quarter, quarter)],
            hidv.at[:, pl.ds(i * quarter, quarter)],
            load_sem.at[i],
        )
        cp.start()
        loads.append((i, cp))

    mates = [row_y * ROW + lax.rem(r + k, ROW) for k in range(1, ROW)]
    peers = [lax.rem(row_y + k, n_y) * ROW + r for k in range(1, n_y)]
    after = lax.rem(p + 1, n_seq)
    before = lax.rem(p + n_seq - 1, n_seq)
    barrier = pltpu.get_barrier_semaphore()
    for s in ring:
        pl.semaphore_signal(barrier, inc=1, device_id=(p, s), device_id_type=MESH)
    for s in mates + peers + [before]:
        pl.semaphore_signal(barrier, inc=1, device_id=(s, z), device_id_type=MESH)

    new = iota((rows, rows), 0)
    blk = (new * 1366) >> 16
    comp = (new - blk * per) >> 4
    old = blk * per + 3 * (new & (cs - 1)) + jnp.where(comp == 2, 0, comp + 1)
    perm = jnp.where(old == iota((rows, rows), 1), 1.0, 0.0).astype(bf16)
    wt[...] = mm(perm, w_ref[...], NT).astype(bf16)

    sends = []

    def remote(src, dst, ssem, rsem, dev):
        cp = pltpu.make_async_remote_copy(
            src_ref=src,
            dst_ref=dst,
            send_sem=ssem,
            recv_sem=rsem,
            device_id=dev,
            device_id_type=MESH,
        )
        cp.start()
        sends.append(cp)

    def arrived(dst, ssem, rsem):
        pltpu.make_async_remote_copy(
            src_ref=dst,
            dst_ref=dst,
            send_sem=ssem,
            recv_sem=rsem,
            device_id=(p, ring[0]),
            device_id_type=MESH,
        ).wait_recv()

    bufs = {
        "kv": (kv_s, kv_r, kv_ss, kv_rs, 0, 2 * cs),
        "q": (q_s, q_r, q_ss, q_rs, 2 * cs, cs),
    }
    toks = (pl.ds(0, half), pl.ds(half, half))

    def own(kind, h, d, dist):
        row0, n = bufs[kind][4:]
        dest = zz(dist if d == 0 else -dist)
        return part[dest, row0 : row0 + n, toks[h]]

    def send(kind, h, d, hop, value):
        sbuf, rbuf, ss, rs = bufs[kind][:4]
        sbuf[d, hop, h] = value.astype(bf16)
        remote(
            sbuf.at[d, hop, h], rbuf.at[d, hop, h], ss.at[d, hop, h], rs.at[d, hop, h], (p, ring[d])
        )

    def first(kind, h):
        long = 0 if h == 1 else 1
        send(kind, h, long, 0, own(kind, h, long, 4))
        send(kind, h, 1 - long, 1, own(kind, h, 1 - long, 3))

    def take(kind, h, d, hop):
        _, rbuf, ss, rs, row0, n = bufs[kind]
        arrived(rbuf.at[d, hop, h], ss.at[d, hop, h], rs.at[d, hop, h])
        got = rbuf[d, hop, h].astype(f32)
        if hop < 3:
            send(kind, h, d, hop + 1, got + own(kind, h, d, 3 - hop))
        elif (d == 0) == (h == 1):
            tot[row0 : row0 + n, toks[h]] = tot[row0 : row0 + n, toks[h]] + got
        else:
            tot[row0 : row0 + n, toks[h]] = part[z, row0 : row0 + n, toks[h]] + got

    def stage(kind, s, h):
        long = 0 if h == 1 else 1
        if s < 4:
            take(kind, h, 1 - long, s)
        take(kind, h, long, s - 1)

    for n, (i, cp) in enumerate(loads):
        cp.wait()
        tok = pl.ds(i * quarter, quarter)
        part[:, :, tok] = mm(wt[...], hidv[:, tok]).reshape(n_ch, per, quarter)
        if n == 1:
            pl.semaphore_wait(barrier, 3 + len(mates) + len(peers))
            first("kv", 1)
        if n == 3:
            first("kv", 0)

    lane_st = iota((cs, st), 1)
    mine = (lane_st >> 4) == iota((cs, st), 0)
    rep = jnp.where((iota((nm, st), 1) & (nm - 1)) == iota((nm, st), 0), 1.0, 0.0)

    def as_row(x):
        return jnp.sum(jnp.where(mine, mm(x, rep, precision=HIGH), 0.0), axis=0, keepdims=True)

    lam = as_row(rates_ref[...])
    gain = as_row(res_ref[...] * jnp.sqrt(rates_ref[...]))
    steps = iota((CL, st), 0).astype(f32)
    e_hi, e_lo = halves(jnp.exp(-lam * (CL - 1 - steps)))
    e_hl[0] = e_hi
    e_hl[1] = e_lo
    p_hi, p_lo = halves(gain * jnp.exp(-lam * (steps + 1.0)))
    p_hl[0] = p_hi
    p_hl[1] = p_lo

    stage("kv", 1, 1)
    stage("kv", 1, 0)
    first("q", 1)
    first("q", 0)

    spread = jnp.where(mine, gain, 0.0)
    taps0 = mm(spread, jnp.exp(-lam * steps), NT, HIGH)
    causal = iota((CL, CL), 1) >= iota((CL, CL), 0)

    def lay_out(c0, c1):
        for c in range(c0, c1):
            line = jnp.broadcast_to(taps0[c : c + 1, :], (CL, CL))
            tri = jnp.where(causal, pltpu.roll(line, 0, 1, stride=1, stride_axis=0), 0.0)
            hi, lo = halves(tri)
            tcat[c, 0:CL] = hi
            tcat[c, CL : 2 * CL] = lo

    lay_out(0, 8)
    lane_per = iota((cs, per), 1)
    row_per = iota((cs, per), 0)
    for i in range(3):
        line = jnp.broadcast_to(taps_ref[i : i + 1, :], (cs, per))
        for j in range(3):
            picked = jnp.where(lane_per == 3 * row_per + j, line, 0.0)
            par[3 * i + j] = jnp.broadcast_to(jnp.sum(picked, axis=1, keepdims=True), (cs, CL))
    skip_line = jnp.broadcast_to(skip_ref[...], (cs, cs))
    skip_col = jnp.sum(
        jnp.where(iota((cs, cs), 0) == iota((cs, cs), 1), skip_line, 0.0), axis=1, keepdims=True
    )

    stage("kv", 2, 1)
    stage("kv", 2, 0)
    stage("q", 1, 1)
    stage("q", 1, 0)
    lay_out(8, 16)
    decay_k = [jnp.exp(-lam * float(CL * k)) for k in range(nk)]
    rf = r.astype(f32)
    block = lam * float(length)
    w_own = jnp.exp(-block * (ROW - 1 - rf))
    w_before = [
        jnp.where(r >= k, jnp.exp(-block * float(k - 1)), 0.0) for k in range(1, ROW)
    ]
    w_row = [
        jnp.exp(-block * (ROW - 1 - lax.rem(r + ROW - k, ROW).astype(f32))) for k in range(1, ROW)
    ]
    w_rows = [
        jnp.where(row_y >= k, jnp.exp(-block * (rf + float(ROW * (k - 1)))), 0.0)
        for k in range(1, n_y)
    ]
    stage("kv", 3, 1)
    stage("kv", 3, 0)
    stage("q", 2, 1)
    stage("q", 2, 0)
    stage("kv", 4, 1)

    def tail(kind, i, row0, n):
        halo_s[row0 : row0 + n] = tot[row0 : row0 + n, length - CL : length].astype(bf16)
        remote(
            halo_s.at[pl.ds(row0, n)],
            halo_r.at[pl.ds(row0, n)],
            halo_ss.at[i],
            halo_rs.at[i],
            (after, z),
        )

    def tail_in(i, row0, n):
        arrived(halo_r.at[pl.ds(row0, n)], halo_ss.at[i], halo_rs.at[i])

    tail("kv", 0, 0, 2 * cs)
    stage("kv", 4, 0)

    def short(row0, j):
        edge = jnp.where(p > 0, halo_r[row0 : row0 + cs].astype(f32), 0.0)
        x = tot[row0 : row0 + cs]
        ext = jnp.concatenate([edge, x], axis=1)
        one = pltpu.roll(ext, 1, 1)[:, CL:]
        two = pltpu.roll(ext, 2, 1)[:, CL:]
        t = [par[3 * i + j][:, 0:1] for i in range(3)]
        return t[0] * x + t[1] * one + t[2] * two

    tail_in(0, 0, 2 * cs)
    driven = (short(0, 1) * short(cs, 2)).astype(bf16)
    stacked = jnp.concatenate([driven[:, CL * k : CL * (k + 1)] for k in range(nk)], axis=0)
    dscr[...] = stacked.astype(f32)
    states = mm(stacked, e_hl[0]) + mm(stacked, e_hl[1])
    carry = jnp.zeros((cs, st), f32)
    for k in range(nk):
        xscr[cs * k : cs * (k + 1)] = carry
        carry = decay_k[1] * carry + jnp.where(mine, states[cs * k : cs * (k + 1)], 0.0)
    total = jnp.sum(carry, axis=0, keepdims=True)
    st0[0] = total
    for k in range(1, ROW):
        remote(
            st0.at[0], st1.at[k - 1], st1_ss.at[k - 1], st1_rs.at[k - 1], (mates[k - 1], z)
        )

    stage("q", 3, 1)
    stage("q", 3, 0)
    for c in range(cs):
        line = dscr[pl.ds(c, nk, stride=cs), :].astype(bf16)
        yscr[pl.ds(c, nk, stride=cs), :] = mm(jnp.concatenate([line, line], axis=1), tcat[c])

    into = jnp.zeros((1, st), f32)
    whole = w_own * total
    for k in range(1, ROW):
        arrived(st1.at[k - 1], st1_ss.at[k - 1], st1_rs.at[k - 1])
        got = st1[k - 1]
        into = into + w_before[k - 1] * got
        whole = whole + w_row[k - 1] * got
    st0[1] = whole
    for k in range(1, n_y):
        remote(
            st0.at[1], st2.at[k - 1], st2_ss.at[k - 1], st2_rs.at[k - 1], (peers[k - 1], z)
        )
    stage("q", 4, 1)
    tail("q", 1, 2 * cs, cs)
    stage("q", 4, 0)
    tail_in(1, 2 * cs, cs)
    query = short(2 * cs, 0)
    for k in range(1, n_y):
        arrived(st2.at[k - 1], st2_ss.at[k - 1], st2_rs.at[k - 1])
        into = into + w_rows[k - 1] * st2[k - 1]
    wide = jnp.where(mine, into, 0.0)
    x = jnp.concatenate(
        [xscr[cs * k : cs * (k + 1)] + decay_k[k] * wide for k in range(nk)], axis=0
    )
    x_hi, x_lo = halves(x)
    y = yscr[...] + mm(x_hi, p_hl[0], NT) + mm(x_lo, p_hl[0], NT) + mm(x_hi, p_hl[1], NT)
    for k in range(nk):
        sl = slice(cs * k, cs * (k + 1))
        tok = slice(CL * k, CL * (k + 1))
        value = query[:, tok] * (y[sl] + skip_col * dscr[sl])
        gath[z, :, tok] = value.astype(bf16)

    def pass_on(src, h, d, hop):
        ref = gath.at[src, :, toks[h]]
        remote(ref, ref, ag_ss.at[d, hop, h], ag_rs.at[d, hop, h], (p, ring[d]))

    for h in (0, 1):
        for d in (0, 1):
            pass_on(z, h, d, 0)
    out_ref[z] = gath[z]
    for hop in range(4):
        for h in (0, 1):
            for d in (0, 1):
                if hop == 3 and (d == 0) != (h == 1):
                    continue
                src = zz(-hop - 1 if d == 0 else hop + 1)
                arrived(gath.at[src, :, toks[h]], ag_ss.at[d, hop, h], ag_rs.at[d, hop, h])
                if hop < 2 or (hop == 2 and (d == 0) == (h == 1)):
                    pass_on(src, h, d, hop + 1)
                out_ref[src, :, toks[h]] = gath[src, :, toks[h]]
    for cp in sends:
        cp.wait_send()


def solution(mesh):
    n_seq, n_ch = mesh.shape["seq"], mesh.shape["ch"]

    def body(hidden_in, w_in, short_taps, rates, residues, skip_gain, w_out):
        depth, length = hidden_in.shape
        rows = w_in.shape[1]
        per = rows // n_ch
        cs = per // 3
        st = cs * rates.shape[1]
        half = length // 2
        nk = length // CL
        n_y = n_seq // ROW
        vmem = pl.BlockSpec(memory_space=pltpu.VMEM)
        dma = pltpu.SemaphoreType.DMA
        gathered = pl.pallas_call(
            functools.partial(conv_kernel, n_seq, n_ch),
            out_shape=jax.ShapeDtypeStruct((n_ch, cs, length), bf16),
            in_specs=[pl.BlockSpec(memory_space=pl.ANY)] + [vmem] * 5,
            out_specs=vmem,
            scratch_shapes=[
                pltpu.VMEM((depth, length), bf16),
                pltpu.VMEM((rows, depth), bf16),
                pltpu.VMEM((n_ch, per, length), f32),
                pltpu.VMEM((2, 4, 2, 2 * cs, half), bf16),
                pltpu.VMEM((2, 4, 2, 2 * cs, half), bf16),
                pltpu.VMEM((2, 4, 2, cs, half), bf16),
                pltpu.VMEM((2, 4, 2, cs, half), bf16),
                pltpu.VMEM((per, length), f32),
                pltpu.VMEM((per, CL), bf16),
                pltpu.VMEM((per, CL), bf16),
                pltpu.VMEM((n_ch, cs, length), bf16),
                pltpu.VMEM((2, 1, st), f32),
                pltpu.VMEM((ROW - 1, 1, st), f32),
                pltpu.VMEM((n_y - 1, 1, st), f32),
                pltpu.VMEM((9, cs, CL), f32),
                pltpu.VMEM((2, CL, st), bf16),
                pltpu.VMEM((2, CL, st), bf16),
                pltpu.VMEM((cs, 2 * CL, CL), bf16),
                pltpu.VMEM((nk * cs, CL), f32),
                pltpu.VMEM((nk * cs, CL), f32),
                pltpu.VMEM((nk * cs, st), f32),
                dma((4,)),
                dma((2, 4, 2)),
                dma((2, 4, 2)),
                dma((2, 4, 2)),
                dma((2, 4, 2)),
                dma((2,)),
                dma((2,)),
                dma((ROW - 1,)),
                dma((ROW - 1,)),
                dma((n_y - 1,)),
                dma((n_y - 1,)),
                dma((2, 4, 2)),
                dma((2, 4, 2)),
            ],
            compiler_params=pltpu.CompilerParams(
                collective_id=0, has_side_effects=True, vmem_limit_bytes=40 * 1024 * 1024
            ),
        )(hidden_in, w_in, short_taps, rates, residues, skip_gain.reshape(1, cs))
        mixed = jnp.dot(w_out, gathered.reshape(n_ch * cs, length), preferred_element_type=f32)
        return mixed.astype(bf16)

    in_specs = (
        P("ch", "seq"),
        P("ch", None),
        P(None, "ch"),
        P("ch", None),
        P("ch", None),
        P("ch"),
        P("ch", None),
    )
    return jax.shard_map(
        body, mesh=mesh, in_specs=in_specs, out_specs=P("ch", "seq"), check_vma=False
    )
```

```python
import functools

import jax
import jax.numpy as jnp
from jax import lax
from jax.experimental import pallas as pl
from jax.experimental.pallas import tpu as pltpu
from jax.sharding import PartitionSpec as P

MESH = pl.DeviceIdType.MESH
f32 = jnp.float32
bf16 = jnp.bfloat16
HIGH = lax.Precision.HIGHEST
NT = (((1,), (1,)), ((), ()))
NN = (((1,), (0,)), ((), ()))
CL = 128
ROW = 8


def mm(a, b, dims=NN, precision=None):
    return lax.dot_general(a, b, dims, precision=precision, preferred_element_type=f32)


def halves(x):
    hi = x.astype(bf16)
    return hi, (x - hi.astype(f32)).astype(bf16)


def iota(shape, dim):
    return lax.broadcasted_iota(jnp.int32, shape, dim)


def conv_kernel(
    n_seq,
    n_ch,
    hid,
    w_in,
    taps_in,
    rates_in,
    res_in,
    skip_in,
    out_ref,
    w_ref,
    taps_ref,
    rates_ref,
    res_ref,
    skip_ref,
    hidv,
    wt,
    part,
    kv_s,
    kv_r,
    q_s,
    q_r,
    tot,
    halo_s,
    halo_r,
    gath,
    st0,
    st1,
    st2,
    par,
    e_hl,
    p_hl,
    tcat,
    dscr,
    yscr,
    xscr,
    load_sem,
    small_sem,
    kv_ss,
    kv_rs,
    q_ss,
    q_rs,
    halo_ss,
    halo_rs,
    st1_ss,
    st1_rs,
    st2_ss,
    st2_rs,
    ag_ss,
    ag_rs,
):
    p = lax.axis_index("seq")
    z = lax.axis_index("ch")
    depth, length = hid.shape
    rows = w_ref.shape[1]
    per = rows // n_ch
    cs = per // 3
    nm = rates_ref.shape[1]
    st = cs * nm
    half = length // 2
    nk = length // CL
    quarter = length // 4
    row_y = p // ROW
    r = p % ROW
    n_y = n_seq // ROW

    def zz(k):
        return lax.rem(z + (k + n_ch), n_ch)

    ring = (zz(1), zz(-1))
    sends = []
    pending = {}

    smalls = []
    pairs = ((w_in, w_ref), (rates_in, rates_ref), (res_in, res_ref), (taps_in, taps_ref), (skip_in, skip_ref))
    for i, (src, dst) in enumerate(pairs):
        cp = pltpu.make_async_copy(src, dst, small_sem.at[i])
        smalls.append(cp)
    smalls[0].start()
    loads = []
    for i in (3, 2, 1, 0):
        cp = pltpu.make_async_copy(
            hid.at[:, pl.ds(i * quarter, quarter)],
            hidv.at[:, pl.ds(i * quarter, quarter)],
            load_sem.at[i],
        )
        cp.start()
        loads.append((i, cp))
    for cp in smalls[1:]:
        cp.start()

    mates = [row_y * ROW + lax.rem(r + k, ROW) for k in range(1, ROW)]
    peers = [lax.rem(row_y + k, n_y) * ROW + r for k in range(1, n_y)]
    after = lax.rem(p + 1, n_seq)
    before = lax.rem(p + n_seq - 1, n_seq)
    barrier = pltpu.get_barrier_semaphore()
    for s in ring + (zz(2), zz(-2)):
        pl.semaphore_signal(barrier, inc=1, device_id=(p, s), device_id_type=MESH)
    for s in mates + peers + [before]:
        pl.semaphore_signal(barrier, inc=1, device_id=(s, z), device_id_type=MESH)

    new = iota((rows, rows), 0)
    blk = (new * 1366) >> 16
    comp = (new - blk * per) >> 4
    old = blk * per + 3 * (new & (cs - 1)) + jnp.where(comp == 2, 0, comp + 1)
    perm = jnp.where(old == iota((rows, rows), 1), 1.0, 0.0).astype(bf16)
    smalls[0].wait()
    wt[...] = mm(perm, w_ref[...], NT).astype(bf16)

    def remote(key, src, dst, ssem, rsem, dev):
        cp = pltpu.make_async_remote_copy(
            src_ref=src,
            dst_ref=dst,
            send_sem=ssem,
            recv_sem=rsem,
            device_id=dev,
            device_id_type=MESH,
        )
        cp.start()
        sends.append(cp)
        pending[key] = (dst, ssem, rsem)

    def arrived(key, dst, ssem, rsem):
        pending.pop(key)
        pltpu.make_async_remote_copy(
            src_ref=dst,
            dst_ref=dst,
            send_sem=ssem,
            recv_sem=rsem,
            device_id=(p, ring[0]),
            device_id_type=MESH,
        ).wait_recv()

    bufs = {
        "kv": (kv_s, kv_r, kv_ss, kv_rs, 0, 2 * cs),
        "q": (q_s, q_r, q_ss, q_rs, 2 * cs, cs),
    }
    toks = (pl.ds(0, half), pl.ds(half, half))

    def own(kind, h, d, dist):
        row0, n = bufs[kind][4:]
        dest = zz(dist if d == 0 else -dist)
        return part[dest, row0 : row0 + n, toks[h]]

    def send(kind, h, d, hop, value):
        sbuf, rbuf, ss, rs = bufs[kind][:4]
        sbuf[d, hop, h] = value.astype(bf16)
        remote(
            (kind, d, hop, h),
            sbuf.at[d, hop, h],
            rbuf.at[d, hop, h],
            ss.at[d, hop, h],
            rs.at[d, hop, h],
            (p, ring[d]),
        )

    def first(kind, h):
        long = 0 if h == 1 else 1
        send(kind, h, long, 0, own(kind, h, long, 4))
        send(kind, h, 1 - long, 1, own(kind, h, 1 - long, 3))

    def take(kind, h, d, hop):
        _, rbuf, ss, rs, row0, n = bufs[kind]
        arrived((kind, d, hop, h), rbuf.at[d, hop, h], ss.at[d, hop, h], rs.at[d, hop, h])
        got = rbuf[d, hop, h].astype(f32)
        if hop < 3:
            send(kind, h, d, hop + 1, got + own(kind, h, d, 3 - hop))
        elif (d == 0) == (h == 1):
            tot[row0 : row0 + n, toks[h]] = tot[row0 : row0 + n, toks[h]] + got
        else:
            tot[row0 : row0 + n, toks[h]] = part[z, row0 : row0 + n, toks[h]] + got

    def stage(kind, s, h):
        long = 0 if h == 1 else 1
        if s < 4:
            take(kind, h, 1 - long, s)
        take(kind, h, long, s - 1)

    for n, (i, cp) in enumerate(loads):
        cp.wait()
        tok = pl.ds(i * quarter, quarter)
        part[:, :, tok] = mm(wt[...], hidv[:, tok]).reshape(n_ch, per, quarter)
        if n == 1:
            pl.semaphore_wait(barrier, 5 + len(mates) + len(peers))
            first("kv", 1)
        if n == 3:
            first("kv", 0)

    lane_st = iota((cs, st), 1)
    mine = (lane_st >> 4) == iota((cs, st), 0)
    rep = jnp.where((iota((nm, st), 1) & (nm - 1)) == iota((nm, st), 0), 1.0, 0.0)

    def as_row(x):
        return jnp.sum(jnp.where(mine, mm(x, rep, precision=HIGH), 0.0), axis=0, keepdims=True)

    for cp in smalls[1:]:
        cp.wait()
    lam = as_row(rates_ref[...])
    gain = as_row(res_ref[...] * jnp.sqrt(rates_ref[...]))
    steps = iota((CL, st), 0).astype(f32)
    e_hi, e_lo = halves(jnp.exp(-lam * (CL - 1 - steps)))
    e_hl[0] = e_hi
    e_hl[1] = e_lo
    p_hi, p_lo = halves(gain * jnp.exp(-lam * (steps + 1.0)))
    p_hl[0] = p_hi
    p_hl[1] = p_lo

    stage("kv", 1, 1)
    stage("kv", 1, 0)
    first("q", 1)
    first("q", 0)

    spread = jnp.where(mine, gain, 0.0)
    taps0 = mm(spread, jnp.exp(-lam * steps), NT, HIGH)
    causal = iota((CL, CL), 1) >= iota((CL, CL), 0)

    def lay_out(c0, c1):
        for c in range(c0, c1):
            line = jnp.broadcast_to(taps0[c : c + 1, :], (CL, CL))
            tri = jnp.where(causal, pltpu.roll(line, 0, 1, stride=1, stride_axis=0), 0.0)
            hi, lo = halves(tri)
            tcat[c, 0:CL] = hi
            tcat[c, CL : 2 * CL] = lo

    lay_out(0, 8)
    lane_per = iota((cs, per), 1)
    row_per = iota((cs, per), 0)
    for i in range(3):
        line = jnp.broadcast_to(taps_ref[i : i + 1, :], (cs, per))
        for j in range(3):
            picked = jnp.where(lane_per == 3 * row_per + j, line, 0.0)
            par[3 * i + j] = jnp.broadcast_to(jnp.sum(picked, axis=1, keepdims=True), (cs, CL))
    skip_line = jnp.broadcast_to(skip_ref[...], (cs, cs))
    skip_col = jnp.sum(
        jnp.where(iota((cs, cs), 0) == iota((cs, cs), 1), skip_line, 0.0), axis=1, keepdims=True
    )

    stage("kv", 2, 1)
    stage("kv", 2, 0)
    stage("q", 1, 1)
    stage("q", 1, 0)
    lay_out(8, 16)
    decay_k = [jnp.exp(-lam * float(CL * k)) for k in range(nk)]
    rf = r.astype(f32)
    block = lam * float(length)
    w_own = jnp.exp(-block * (ROW - 1 - rf))
    w_before = [
        jnp.where(r >= k, jnp.exp(-block * float(k - 1)), 0.0) for k in range(1, ROW)
    ]
    w_row = [
        jnp.exp(-block * (ROW - 1 - lax.rem(r + ROW - k, ROW).astype(f32))) for k in range(1, ROW)
    ]
    w_rows = [
        jnp.where(row_y >= k, jnp.exp(-block * (rf + float(ROW * (k - 1)))), 0.0)
        for k in range(1, n_y)
    ]
    stage("kv", 3, 1)
    stage("kv", 3, 0)
    stage("q", 2, 1)
    stage("q", 2, 0)
    stage("kv", 4, 1)

    def tail(kind, i, row0, n):
        halo_s[row0 : row0 + n] = tot[row0 : row0 + n, length - CL : length].astype(bf16)
        remote(
            ("halo", i),
            halo_s.at[pl.ds(row0, n)],
            halo_r.at[pl.ds(row0, n)],
            halo_ss.at[i],
            halo_rs.at[i],
            (after, z),
        )

    def tail_in(i, row0, n):
        arrived(("halo", i), halo_r.at[pl.ds(row0, n)], halo_ss.at[i], halo_rs.at[i])

    tail("kv", 0, 0, 2 * cs)
    stage("kv", 4, 0)

    def short(row0, j):
        edge = jnp.where(p > 0, halo_r[row0 : row0 + cs].astype(f32), 0.0)
        x = tot[row0 : row0 + cs]
        ext = jnp.concatenate([edge, x], axis=1)
        one = pltpu.roll(ext, 1, 1)[:, CL:]
        two = pltpu.roll(ext, 2, 1)[:, CL:]
        t = [par[3 * i + j][:, 0:1] for i in range(3)]
        return t[0] * x + t[1] * one + t[2] * two

    tail_in(0, 0, 2 * cs)
    driven = (short(0, 1) * short(cs, 2)).astype(bf16)
    stacked = jnp.concatenate([driven[:, CL * k : CL * (k + 1)] for k in range(nk)], axis=0)
    dscr[...] = stacked.astype(f32)
    states = mm(stacked, e_hl[0]) + mm(stacked, e_hl[1])
    carry = jnp.zeros((cs, st), f32)
    for k in range(nk):
        xscr[cs * k : cs * (k + 1)] = carry
        carry = decay_k[1] * carry + jnp.where(mine, states[cs * k : cs * (k + 1)], 0.0)
    total = jnp.sum(carry, axis=0, keepdims=True)
    st0[0] = total
    for k in range(1, ROW):
        remote(
            ("st1", k),
            st0.at[0],
            st1.at[k - 1],
            st1_ss.at[k - 1],
            st1_rs.at[k - 1],
            (mates[k - 1], z),
        )

    stage("q", 3, 1)
    stage("q", 3, 0)
    for c in range(cs):
        line = dscr[pl.ds(c, nk, stride=cs), :].astype(bf16)
        yscr[pl.ds(c, nk, stride=cs), :] = mm(jnp.concatenate([line, line], axis=1), tcat[c])

    into = jnp.zeros((1, st), f32)
    whole = w_own * total
    for k in range(1, ROW):
        arrived(("st1", k), st1.at[k - 1], st1_ss.at[k - 1], st1_rs.at[k - 1])
        got = st1[k - 1]
        into = into + w_before[k - 1] * got
        whole = whole + w_row[k - 1] * got
    st0[1] = whole
    for k in range(1, n_y):
        remote(
            ("st2", k),
            st0.at[1],
            st2.at[k - 1],
            st2_ss.at[k - 1],
            st2_rs.at[k - 1],
            (peers[k - 1], z),
        )
    stage("q", 4, 1)
    tail("q", 1, 2 * cs, cs)
    stage("q", 4, 0)
    tail_in(1, 2 * cs, cs)
    query = short(2 * cs, 0)
    for k in range(1, n_y):
        arrived(("st2", k), st2.at[k - 1], st2_ss.at[k - 1], st2_rs.at[k - 1])
        into = into + w_rows[k - 1] * st2[k - 1]
    wide = jnp.where(mine, into, 0.0)
    x = jnp.concatenate(
        [xscr[cs * k : cs * (k + 1)] + decay_k[k] * wide for k in range(nk)], axis=0
    )
    x_hi, x_lo = halves(x)
    y = yscr[...] + mm(x_hi, p_hl[0], NT) + mm(x_lo, p_hl[0], NT) + mm(x_hi, p_hl[1], NT)
    for k in range(nk):
        sl = slice(cs * k, cs * (k + 1))
        tok = slice(CL * k, CL * (k + 1))
        value = query[:, tok] * (y[sl] + skip_col * dscr[sl])
        gath[z, :, tok] = value.astype(bf16)

    hand_on = ((0, 2, None), (0, 1, None), (2, 1, None), (2, 2, 0))

    def piece(i, d, dist):
        part_of = hand_on[i][2]
        tok = slice(None) if part_of is None else toks[part_of if d == 0 else 1 - part_of]
        return gath.at[zz(-dist if d == 0 else dist), :, tok]

    def hand(i, d):
        hold, step, _ = hand_on[i]
        ref = piece(i, d, hold)
        target = (p, zz(step if d == 0 else -step))
        remote(("ag", d, i), ref, ref, ag_ss.at[d, i], ag_rs.at[d, i], target)

    def handed(i, d):
        hold, step, _ = hand_on[i]
        arrived(("ag", d, i), piece(i, d, hold + step), ag_ss.at[d, i], ag_rs.at[d, i])

    for i in (0, 1):
        for d in (0, 1):
            hand(i, d)
    for d in (0, 1):
        handed(0, d)
        hand(2, d)
        hand(3, d)
    for i in (1, 2, 3):
        for d in (0, 1):
            handed(i, d)
    out_ref[...] = gath[...]
    for cp in sends:
        cp.wait_send()


def project_kernel(w_ref, x_ref, out, rows_ref, sem):
    count = sem.shape[0]
    tile = out.shape[0] // count
    copies = []
    for i in range(count):
        at = pl.ds(i * tile, tile)
        rows_ref[at] = mm(w_ref[at], x_ref[...]).astype(bf16)
        cp = pltpu.make_async_copy(rows_ref.at[at], out.at[at], sem.at[i])
        cp.start()
        copies.append(cp)
    for cp in copies:
        cp.wait()


def solution(mesh):
    n_seq, n_ch = mesh.shape["seq"], mesh.shape["ch"]

    def body(hidden_in, w_in, short_taps, rates, residues, skip_gain, w_out):
        depth, length = hidden_in.shape
        rows = w_in.shape[1]
        per = rows // n_ch
        cs = per // 3
        st = cs * rates.shape[1]
        half = length // 2
        nk = length // CL
        n_y = n_seq // ROW
        vmem = pl.BlockSpec(memory_space=pltpu.VMEM)
        dma = pltpu.SemaphoreType.DMA
        gathered = pl.pallas_call(
            functools.partial(conv_kernel, n_seq, n_ch),
            out_shape=jax.ShapeDtypeStruct((n_ch, cs, length), bf16),
            in_specs=[pl.BlockSpec(memory_space=pltpu.HBM)] * 6,
            out_specs=vmem,
            scratch_shapes=[
                pltpu.VMEM(w_in.shape, bf16),
                pltpu.VMEM(short_taps.shape, f32),
                pltpu.VMEM(rates.shape, f32),
                pltpu.VMEM(residues.shape, f32),
                pltpu.VMEM((1, cs), f32),
                pltpu.VMEM((depth, length), bf16),
                pltpu.VMEM((rows, depth), bf16),
                pltpu.VMEM((n_ch, per, length), f32),
                pltpu.VMEM((2, 4, 2, 2 * cs, half), bf16),
                pltpu.VMEM((2, 4, 2, 2 * cs, half), bf16),
                pltpu.VMEM((2, 4, 2, cs, half), bf16),
                pltpu.VMEM((2, 4, 2, cs, half), bf16),
                pltpu.VMEM((per, length), f32),
                pltpu.VMEM((per, CL), bf16),
                pltpu.VMEM((per, CL), bf16),
                pltpu.VMEM((n_ch, cs, length), bf16),
                pltpu.VMEM((2, 1, st), f32),
                pltpu.VMEM((ROW - 1, 1, st), f32),
                pltpu.VMEM((n_y - 1, 1, st), f32),
                pltpu.VMEM((9, cs, CL), f32),
                pltpu.VMEM((2, CL, st), bf16),
                pltpu.VMEM((2, CL, st), bf16),
                pltpu.VMEM((cs, 2 * CL, CL), bf16),
                pltpu.VMEM((nk * cs, CL), f32),
                pltpu.VMEM((nk * cs, CL), f32),
                pltpu.VMEM((nk * cs, st), f32),
                dma((4,)),
                dma((5,)),
                dma((2, 4, 2)),
                dma((2, 4, 2)),
                dma((2, 4, 2)),
                dma((2, 4, 2)),
                dma((2,)),
                dma((2,)),
                dma((ROW - 1,)),
                dma((ROW - 1,)),
                dma((n_y - 1,)),
                dma((n_y - 1,)),
                dma((2, 4)),
                dma((2, 4)),
            ],
            compiler_params=pltpu.CompilerParams(
                collective_id=0, has_side_effects=True, vmem_limit_bytes=40 * 1024 * 1024
            ),
        )(
            *(
                pltpu.with_memory_space_constraint(x, pltpu.HBM)
                for x in (hidden_in, w_in, short_taps, rates, residues, skip_gain.reshape(1, cs))
            )
        )
        slab = n_ch * cs
        return pl.pallas_call(
            project_kernel,
            out_shape=jax.ShapeDtypeStruct((w_out.shape[0], length), bf16),
            in_specs=[vmem] * 2,
            out_specs=pl.BlockSpec(memory_space=pl.ANY),
            scratch_shapes=[pltpu.VMEM((w_out.shape[0], length), bf16), dma((8,))],
            compiler_params=pltpu.CompilerParams(vmem_limit_bytes=16 * 1024 * 1024),
        )(w_out, gathered.reshape(slab, length))

    in_specs = (
        P("ch", "seq"),
        P("ch", None),
        P(None, "ch"),
        P("ch", None),
        P("ch", None),
        P("ch"),
        P("ch", None),
    )
    return jax.shard_map(
        body, mesh=mesh, in_specs=in_specs, out_specs=P("ch", "seq"), check_vma=False
    )
```

```python
import functools

import jax
import jax.numpy as jnp
from jax import lax
from jax.experimental import pallas as pl
from jax.experimental.pallas import tpu as pltpu
from jax.sharding import PartitionSpec as P

MESH = pl.DeviceIdType.MESH
f32 = jnp.float32
bf16 = jnp.bfloat16
HIGH = lax.Precision.HIGHEST
NT = (((1,), (1,)), ((), ()))
NN = (((1,), (0,)), ((), ()))
CL = 128


def mm(a, b, dims=NN, precision=None):
    return lax.dot_general(a, b, dims, precision=precision, preferred_element_type=f32)


def halves(x):
    hi = x.astype(bf16)
    return hi, (x - hi.astype(f32)).astype(bf16)


def iota(shape, dim):
    return lax.broadcasted_iota(jnp.int32, shape, dim)


def conv_kernel(
    n_seq,
    n_ch,
    hid,
    w_in,
    taps_in,
    rates_in,
    res_in,
    skip_in,
    out_ref,
    w_ref,
    taps_ref,
    rates_ref,
    res_ref,
    skip_ref,
    hidv,
    wt,
    part,
    kv_s,
    kv_r,
    q_s,
    q_r,
    tot,
    halo_s,
    halo_r,
    gath,
    st0,
    st1,
    par,
    e_hl,
    p_hl,
    tcat,
    dscr,
    yscr,
    xscr,
    load_sem,
    small_sem,
    kv_ss,
    kv_rs,
    q_ss,
    q_rs,
    halo_ss,
    halo_rs,
    st_ss,
    st_rs,
    ag_ss,
    ag_rs,
):
    p = lax.axis_index("seq")
    z = lax.axis_index("ch")
    depth, length = hid.shape
    rows = w_ref.shape[1]
    per = rows // n_ch
    cs = per // 3
    nm = rates_ref.shape[1]
    st = cs * nm
    half = length // 2
    nk = length // CL
    quarter = length // 4
    py, px, pc = p // 8, p // 2 % 4, p % 2
    n_y = n_seq // 8

    def zz(k):
        return lax.rem(z + (k + n_ch), n_ch)

    ring = (zz(1), zz(-1))
    ring2 = (zz(2), zz(-2))
    sends = []
    pending = {}

    smalls = []
    pairs = ((w_in, w_ref), (rates_in, rates_ref), (res_in, res_ref), (taps_in, taps_ref), (skip_in, skip_ref))
    for i, (src, dst) in enumerate(pairs):
        cp = pltpu.make_async_copy(src, dst, small_sem.at[i])
        smalls.append(cp)
    smalls[0].start()
    loads = []
    for i in (3, 2, 1, 0):
        cp = pltpu.make_async_copy(
            hid.at[:, pl.ds(i * quarter, quarter)],
            hidv.at[:, pl.ds(i * quarter, quarter)],
            load_sem.at[i],
        )
        cp.start()
        loads.append((i, cp))
    for cp in smalls[1:]:
        cp.start()

    def place(dy, dx, dc):
        return lax.rem(py + dy + n_y, n_y) * 8 + lax.rem(px + dx + 4, 4) * 2 + lax.rem(pc + dc, 2)

    moves = [(dy, dx, dc) for dy in range(n_y) for dx in range(4) for dc in range(2)][1:]
    moves.sort(key=lambda m: (-min(m[0], n_y - m[0]) - min(m[1], 4 - m[1]), -m[2]))
    after = lax.rem(p + 1, n_seq)
    barrier = pltpu.get_barrier_semaphore()
    for s in ring + ring2:
        pl.semaphore_signal(barrier, inc=1, device_id=(p, s), device_id_type=MESH)
    for s in [place(*move) for move in moves]:
        pl.semaphore_signal(barrier, inc=1, device_id=(s, z), device_id_type=MESH)

    new = iota((rows, rows), 0)
    blk = (new * 1366) >> 16
    comp = (new - blk * per) >> 4
    old = blk * per + 3 * (new & (cs - 1)) + jnp.where(comp == 2, 0, comp + 1)
    perm = jnp.where(old == iota((rows, rows), 1), 1.0, 0.0).astype(bf16)
    smalls[0].wait()
    wt[...] = mm(perm, w_ref[...], NT).astype(bf16)

    def remote(key, src, dst, ssem, rsem, dev):
        cp = pltpu.make_async_remote_copy(
            src_ref=src,
            dst_ref=dst,
            send_sem=ssem,
            recv_sem=rsem,
            device_id=dev,
            device_id_type=MESH,
        )
        cp.start()
        sends.append(cp)
        pending[key] = (dst, ssem, rsem)

    def arrived(key, dst, ssem, rsem):
        pending.pop(key)
        pltpu.make_async_remote_copy(
            src_ref=dst,
            dst_ref=dst,
            send_sem=ssem,
            recv_sem=rsem,
            device_id=(p, ring[0]),
            device_id_type=MESH,
        ).wait_recv()

    bufs = {
        "kv": (kv_s, kv_r, kv_ss, kv_rs, 0, 2 * cs),
        "q": (q_s, q_r, q_ss, q_rs, 2 * cs, cs),
    }
    toks = (pl.ds(0, half), pl.ds(half, half))

    def own(kind, h, d, dist):
        row0, n = bufs[kind][4:]
        dest = zz(dist if d == 0 else -dist)
        return part[dest, row0 : row0 + n, toks[h]]

    def send(kind, h, d, m, value):
        sbuf, rbuf, ss, rs = bufs[kind][:4]
        sbuf[d, m, h] = value.astype(bf16)
        remote(
            (kind, d, m, h),
            sbuf.at[d, m, h],
            rbuf.at[d, m, h],
            ss.at[d, m, h],
            rs.at[d, m, h],
            (p, (ring, ring2)[m in (0, 2)][d]),
        )

    def far(kind, h):
        send(kind, h, 0 if h == 1 else 1, 0, own(kind, h, 0 if h == 1 else 1, 4))
        for d in (0, 1):
            send(kind, h, d, 1, own(kind, h, d, 3))

    def near(kind, h):
        for d in (0, 1):
            send(kind, h, d, 3, own(kind, h, d, 1))

    def take(kind, h, d, m):
        _, rbuf, ss, rs = bufs[kind][:4]
        arrived((kind, d, m, h), rbuf.at[d, m, h], ss.at[d, m, h], rs.at[d, m, h])
        return rbuf[d, m, h].astype(f32)

    def merge(kind, h):
        long = 0 if h == 1 else 1
        for d in (1 - long, long):
            value = own(kind, h, d, 2) + take(kind, h, d, 1)
            if d == long:
                value = value + take(kind, h, d, 0)
            send(kind, h, d, 2, value)

    def total_of(kind, h):
        row0, n = bufs[kind][4:]
        value = part[z, row0 : row0 + n, toks[h]]
        for m in (3, 2):
            for d in (0, 1):
                value = value + take(kind, h, d, m)
        tot[row0 : row0 + n, toks[h]] = value

    for n, (i, cp) in enumerate(loads):
        cp.wait()
        tok = pl.ds(i * quarter, quarter)
        part[:, :, tok] = mm(wt[...], hidv[:, tok]).reshape(n_ch, per, quarter)
        if n == 1:
            pl.semaphore_wait(barrier, 4 + len(moves))
            far("kv", 1)
        if n == 3:
            far("kv", 0)
            far("q", 1)
            far("q", 0)

    lane_st = iota((cs, st), 1)
    mine = (lane_st >> 4) == iota((cs, st), 0)
    rep = jnp.where((iota((nm, st), 1) & (nm - 1)) == iota((nm, st), 0), 1.0, 0.0)

    def as_row(x):
        return jnp.sum(jnp.where(mine, mm(x, rep, precision=HIGH), 0.0), axis=0, keepdims=True)

    for cp in smalls[1:]:
        cp.wait()
    lam = as_row(rates_ref[...])
    gain = as_row(res_ref[...] * jnp.sqrt(rates_ref[...]))
    steps = iota((CL, st), 0).astype(f32)
    e_hi, e_lo = halves(jnp.exp(-lam * (CL - 1 - steps)))
    e_hl[0] = e_hi
    e_hl[1] = e_lo
    p_hi, p_lo = halves(gain * jnp.exp(-lam * (steps + 1.0)))
    p_hl[0] = p_hi
    p_hl[1] = p_lo

    for h in (1, 0):
        merge("kv", h)
        near("kv", h)

    spread = jnp.where(mine, gain, 0.0)
    taps0 = mm(spread, jnp.exp(-lam * steps), NT, HIGH)
    causal = iota((CL, CL), 1) >= iota((CL, CL), 0)

    def lay_out(c0, c1):
        for c in range(c0, c1):
            line = jnp.broadcast_to(taps0[c : c + 1, :], (CL, CL))
            tri = jnp.where(causal, pltpu.roll(line, 0, 1, stride=1, stride_axis=0), 0.0)
            hi, lo = halves(tri)
            tcat[c, 0:CL] = hi
            tcat[c, CL : 2 * CL] = lo

    lay_out(0, 8)
    lane_per = iota((cs, per), 1)
    row_per = iota((cs, per), 0)
    for i in range(3):
        line = jnp.broadcast_to(taps_ref[i : i + 1, :], (cs, per))
        for j in range(3):
            picked = jnp.where(lane_per == 3 * row_per + j, line, 0.0)
            par[3 * i + j] = jnp.broadcast_to(jnp.sum(picked, axis=1, keepdims=True), (cs, CL))
    skip_line = jnp.broadcast_to(skip_ref[...], (cs, cs))
    skip_col = jnp.sum(
        jnp.where(iota((cs, cs), 0) == iota((cs, cs), 1), skip_line, 0.0), axis=1, keepdims=True
    )

    for h in (1, 0):
        merge("q", h)
        near("q", h)
    lay_out(8, 16)
    decay_k = [jnp.exp(-lam * float(CL * k)) for k in range(nk)]
    block = lam * float(length)
    weight = []
    for dy, dx, dc in moves:
        src = place(-dy, -dx, dc)
        weight.append(
            jnp.where(src < p, jnp.exp(-block * jnp.maximum(p - 1 - src, 0).astype(f32)), 0.0)
        )
    total_of("kv", 1)

    def tail(kind, i, row0, n):
        halo_s[row0 : row0 + n] = tot[row0 : row0 + n, length - CL : length].astype(bf16)
        remote(
            ("halo", i),
            halo_s.at[pl.ds(row0, n)],
            halo_r.at[pl.ds(row0, n)],
            halo_ss.at[i],
            halo_rs.at[i],
            (after, z),
        )

    def tail_in(i, row0, n):
        arrived(("halo", i), halo_r.at[pl.ds(row0, n)], halo_ss.at[i], halo_rs.at[i])

    tail("kv", 0, 0, 2 * cs)
    total_of("kv", 0)

    def short(row0, j):
        edge = jnp.where(p > 0, halo_r[row0 : row0 + cs].astype(f32), 0.0)
        x = tot[row0 : row0 + cs]
        ext = jnp.concatenate([edge, x], axis=1)
        one = pltpu.roll(ext, 1, 1)[:, CL:]
        two = pltpu.roll(ext, 2, 1)[:, CL:]
        t = [par[3 * i + j][:, 0:1] for i in range(3)]
        return t[0] * x + t[1] * one + t[2] * two

    tail_in(0, 0, 2 * cs)
    driven = (short(0, 1) * short(cs, 2)).astype(bf16)
    stacked = jnp.concatenate([driven[:, CL * k : CL * (k + 1)] for k in range(nk)], axis=0)
    dscr[...] = stacked.astype(f32)
    states = mm(stacked, e_hl[0]) + mm(stacked, e_hl[1])
    carry = jnp.zeros((cs, st), f32)
    for k in range(nk):
        xscr[cs * k : cs * (k + 1)] = carry
        carry = decay_k[1] * carry + jnp.where(mine, states[cs * k : cs * (k + 1)], 0.0)
    total = jnp.sum(carry, axis=0, keepdims=True)
    st0[...] = total
    for i, move in enumerate(moves):
        remote(
            ("st", i), st0, st1.at[i], st_ss.at[i], st_rs.at[i], (place(*move), z)
        )

    for c in range(cs):
        line = dscr[pl.ds(c, nk, stride=cs), :].astype(bf16)
        yscr[pl.ds(c, nk, stride=cs), :] = mm(jnp.concatenate([line, line], axis=1), tcat[c])

    total_of("q", 1)
    tail("q", 1, 2 * cs, cs)
    total_of("q", 0)
    tail_in(1, 2 * cs, cs)
    query = short(2 * cs, 0)
    into = jnp.zeros((1, st), f32)
    for i in reversed(range(len(moves))):
        arrived(("st", i), st1.at[i], st_ss.at[i], st_rs.at[i])
        into = into + weight[i] * st1[i]
    wide = jnp.where(mine, into, 0.0)
    x = jnp.concatenate(
        [xscr[cs * k : cs * (k + 1)] + decay_k[k] * wide for k in range(nk)], axis=0
    )
    x_hi, x_lo = halves(x)
    y = yscr[...] + mm(x_hi, p_hl[0], NT) + mm(x_lo, p_hl[0], NT) + mm(x_hi, p_hl[1], NT)
    for k in range(nk):
        sl = slice(cs * k, cs * (k + 1))
        tok = slice(CL * k, CL * (k + 1))
        value = query[:, tok] * (y[sl] + skip_col * dscr[sl])
        gath[z, :, tok] = value.astype(bf16)

    hand_on = ((0, 2, None), (0, 1, None), (2, 1, None), (2, 2, 0))

    def piece(i, d, dist):
        part_of = hand_on[i][2]
        tok = slice(None) if part_of is None else toks[part_of if d == 0 else 1 - part_of]
        return gath.at[zz(-dist if d == 0 else dist), :, tok]

    def hand(i, d):
        hold, step, _ = hand_on[i]
        ref = piece(i, d, hold)
        target = (p, zz(step if d == 0 else -step))
        remote(("ag", d, i), ref, ref, ag_ss.at[d, i], ag_rs.at[d, i], target)

    def handed(i, d):
        hold, step, _ = hand_on[i]
        arrived(("ag", d, i), piece(i, d, hold + step), ag_ss.at[d, i], ag_rs.at[d, i])

    for i in (0, 1):
        for d in (0, 1):
            hand(i, d)
    for d in (0, 1):
        handed(0, d)
        hand(2, d)
        hand(3, d)
    for i in (1, 2, 3):
        for d in (0, 1):
            handed(i, d)
    out_ref[...] = gath[...]
    for cp in sends:
        cp.wait_send()


def project_kernel(w_ref, x_ref, out, rows_ref, sem):
    count = sem.shape[0]
    tile = out.shape[0] // count
    copies = []
    for i in range(count):
        at = pl.ds(i * tile, tile)
        rows_ref[at] = mm(w_ref[at], x_ref[...]).astype(bf16)
        cp = pltpu.make_async_copy(rows_ref.at[at], out.at[at], sem.at[i])
        cp.start()
        copies.append(cp)
    for cp in copies:
        cp.wait()


def solution(mesh):
    n_seq, n_ch = mesh.shape["seq"], mesh.shape["ch"]

    def body(hidden_in, w_in, short_taps, rates, residues, skip_gain, w_out):
        depth, length = hidden_in.shape
        rows = w_in.shape[1]
        per = rows // n_ch
        cs = per // 3
        st = cs * rates.shape[1]
        half = length // 2
        nk = length // CL
        vmem = pl.BlockSpec(memory_space=pltpu.VMEM)
        dma = pltpu.SemaphoreType.DMA
        gathered = pl.pallas_call(
            functools.partial(conv_kernel, n_seq, n_ch),
            out_shape=jax.ShapeDtypeStruct((n_ch, cs, length), bf16),
            in_specs=[pl.BlockSpec(memory_space=pltpu.HBM)] * 6,
            out_specs=vmem,
            scratch_shapes=[
                pltpu.VMEM(w_in.shape, bf16),
                pltpu.VMEM(short_taps.shape, f32),
                pltpu.VMEM(rates.shape, f32),
                pltpu.VMEM(residues.shape, f32),
                pltpu.VMEM((1, cs), f32),
                pltpu.VMEM((depth, length), bf16),
                pltpu.VMEM((rows, depth), bf16),
                pltpu.VMEM((n_ch, per, length), f32),
                pltpu.VMEM((2, 4, 2, 2 * cs, half), bf16),
                pltpu.VMEM((2, 4, 2, 2 * cs, half), bf16),
                pltpu.VMEM((2, 4, 2, cs, half), bf16),
                pltpu.VMEM((2, 4, 2, cs, half), bf16),
                pltpu.VMEM((per, length), f32),
                pltpu.VMEM((per, CL), bf16),
                pltpu.VMEM((per, CL), bf16),
                pltpu.VMEM((n_ch, cs, length), bf16),
                pltpu.VMEM((1, st), f32),
                pltpu.VMEM((n_seq - 1, 1, st), f32),
                pltpu.VMEM((9, cs, CL), f32),
                pltpu.VMEM((2, CL, st), bf16),
                pltpu.VMEM((2, CL, st), bf16),
                pltpu.VMEM((cs, 2 * CL, CL), bf16),
                pltpu.VMEM((nk * cs, CL), f32),
                pltpu.VMEM((nk * cs, CL), f32),
                pltpu.VMEM((nk * cs, st), f32),
                dma((4,)),
                dma((5,)),
                dma((2, 4, 2)),
                dma((2, 4, 2)),
                dma((2, 4, 2)),
                dma((2, 4, 2)),
                dma((2,)),
                dma((2,)),
                dma((n_seq - 1,)),
                dma((n_seq - 1,)),
                dma((2, 4)),
                dma((2, 4)),
            ],
            compiler_params=pltpu.CompilerParams(
                collective_id=0, has_side_effects=True, vmem_limit_bytes=40 * 1024 * 1024
            ),
        )(
            *(
                pltpu.with_memory_space_constraint(x, pltpu.HBM)
                for x in (hidden_in, w_in, short_taps, rates, residues, skip_gain.reshape(1, cs))
            )
        )
        slab = n_ch * cs
        return pl.pallas_call(
            project_kernel,
            out_shape=jax.ShapeDtypeStruct((w_out.shape[0], length), bf16),
            in_specs=[vmem] * 2,
            out_specs=pl.BlockSpec(memory_space=pl.ANY),
            scratch_shapes=[pltpu.VMEM((w_out.shape[0], length), bf16), dma((8,))],
            compiler_params=pltpu.CompilerParams(vmem_limit_bytes=16 * 1024 * 1024),
        )(w_out, gathered.reshape(slab, length))

    in_specs = (
        P("ch", "seq"),
        P("ch", None),
        P(None, "ch"),
        P("ch", None),
        P("ch", None),
        P("ch"),
        P("ch", None),
    )
    return jax.shard_map(
        body, mesh=mesh, in_specs=in_specs, out_specs=P("ch", "seq"), check_vma=False
    )
```

```python
import functools

import jax
import jax.numpy as jnp
from jax import lax
from jax.experimental import pallas as pl
from jax.experimental.pallas import tpu as pltpu
from jax.sharding import PartitionSpec as P

MESH = pl.DeviceIdType.MESH
f32 = jnp.float32
bf16 = jnp.bfloat16
HIGH = lax.Precision.HIGHEST
NT = (((1,), (1,)), ((), ()))
NN = (((1,), (0,)), ((), ()))
CL = 128


def mm(a, b, dims=NN, precision=None):
    return lax.dot_general(a, b, dims, precision=precision, preferred_element_type=f32)


def halves(x):
    hi = x.astype(bf16)
    return hi, (x - hi.astype(f32)).astype(bf16)


def iota(shape, dim):
    return lax.broadcasted_iota(jnp.int32, shape, dim)


def conv_kernel(
    n_seq,
    n_ch,
    hid,
    w_in,
    taps_in,
    rates_in,
    res_in,
    skip_in,
    out_ref,
    w_ref,
    taps_ref,
    rates_ref,
    res_ref,
    skip_ref,
    hidv,
    wt,
    part,
    kv_s,
    kv_r,
    q_s,
    q_r,
    tot,
    halo_s,
    halo_r,
    gath,
    st0,
    st1,
    par,
    e_hl,
    p_hl,
    tcat,
    dscr,
    yscr,
    xscr,
    load_sem,
    small_sem,
    sent,
    kv_rs,
    q_rs,
    halo_rs,
    st_rs,
    ag_rs,
):
    p = lax.axis_index("seq")
    z = lax.axis_index("ch")
    depth, length = hid.shape
    rows = w_ref.shape[1]
    per = rows // n_ch
    cs = per // 3
    nm = rates_ref.shape[1]
    st = cs * nm
    half = length // 2
    nk = length // CL
    quarter = length // 4

    def zz(k):
        return lax.rem(z + (k + n_ch), n_ch)

    ring = (zz(1), zz(-1))
    ring2 = (zz(2), zz(-2))
    pending = {}

    smalls = []
    pairs = ((w_in, w_ref), (rates_in, rates_ref), (res_in, res_ref), (taps_in, taps_ref), (skip_in, skip_ref))
    for i, (src, dst) in enumerate(pairs):
        cp = pltpu.make_async_copy(src, dst, small_sem.at[i])
        smalls.append(cp)
    smalls[0].start()
    loads = []
    for i in (3, 2, 1, 0):
        cp = pltpu.make_async_copy(
            hid.at[:, pl.ds(i * quarter, quarter)],
            hidv.at[:, pl.ds(i * quarter, quarter)],
            load_sem.at[i],
        )
        cp.start()
        loads.append((i, cp))
    for cp in smalls[1:]:
        cp.start()

    def hops(k):
        return (0, 1, 2, 1)[k >> 1 & 3] + (0, 1, 2, 1)[k >> 3]

    moves = sorted(range(1, n_seq), key=lambda k: -hops(k))
    after = lax.rem(p + 1, n_seq)
    barrier = pltpu.get_barrier_semaphore()
    for s in ring + ring2:
        pl.semaphore_signal(barrier, inc=1, device_id=(p, s), device_id_type=MESH)
    for k in moves:
        pl.semaphore_signal(barrier, inc=1, device_id=(p ^ k, z), device_id_type=MESH)

    new = iota((rows, rows), 0)
    blk = (new * 1366) >> 16
    comp = (new - blk * per) >> 4
    old = blk * per + 3 * (new & (cs - 1)) + jnp.where(comp == 2, 0, comp + 1)
    perm = jnp.where(old == iota((rows, rows), 1), 1.0, 0.0).astype(bf16)
    smalls[0].wait()
    wt[...] = mm(perm, w_ref[...], NT).astype(bf16)

    def remote(key, src, dst, ssem, rsem, dev):
        pltpu.make_async_remote_copy(
            src_ref=src,
            dst_ref=dst,
            send_sem=ssem,
            recv_sem=rsem,
            device_id=dev,
            device_id_type=MESH,
        ).start()
        pending[key] = (dst, rsem)

    def waiter(ref, sem):
        return pltpu.make_async_remote_copy(
            src_ref=ref,
            dst_ref=ref,
            send_sem=sem,
            recv_sem=sem,
            device_id=(p, ring[0]),
            device_id_type=MESH,
        )

    def arrived(keys, ref, sem):
        for key in keys:
            pending.pop(key)
        waiter(ref, sem).wait_recv()

    bufs = {
        "kv": (kv_s, kv_r, sent.at[0], kv_rs, 0, 2 * cs),
        "q": (q_s, q_r, sent.at[1], q_rs, 2 * cs, cs),
    }
    toks = (pl.ds(0, half), pl.ds(half, half))

    def own(kind, h, d, dist):
        row0, n = bufs[kind][4:]
        dest = zz(dist if d == 0 else -dist)
        return part[dest, row0 : row0 + n, toks[h]]

    def long_way(h):
        return 0 if h == 1 else 1

    def send(kind, h, d, m, value):
        sbuf, rbuf, ss, rs = bufs[kind][:4]
        slot = (0, 1, 3, 5)[m] if d == long_way(h) else (None, 2, 4, 6)[m]
        sbuf[h, slot] = value.astype(bf16)
        to = (ring2, ring)[m % 2][d]
        got = rs.at[h, (0, 0, 1, 2, 2, 2, 2)[slot]]
        remote((kind, h, slot), sbuf.at[h, slot], rbuf.at[h, slot], ss, got, (p, to))

    def take(kind, h, group, first, count):
        _, rbuf, _, rs = bufs[kind][:4]
        keys = [(kind, h, first + i) for i in range(count)]
        arrived(keys, rbuf.at[h, pl.ds(first, count)], rs.at[h, group])
        return [rbuf[h, first + i].astype(f32) for i in range(count)]

    def far(kind, h):
        send(kind, h, long_way(h), 0, own(kind, h, long_way(h), 4))
        for d in (0, 1):
            send(kind, h, d, 1, own(kind, h, d, 3))

    def near(kind, h):
        for d in (0, 1):
            send(kind, h, d, 3, own(kind, h, d, 1))

    def merge_short(kind, h):
        d = 1 - long_way(h)
        (got,) = take(kind, h, 1, 2, 1)
        send(kind, h, d, 2, own(kind, h, d, 2) + got)

    def merge_long(kind, h):
        d = long_way(h)
        four, three = take(kind, h, 0, 0, 2)
        send(kind, h, d, 2, own(kind, h, d, 2) + three + four)

    def total_of(kind, h):
        row0, n = bufs[kind][4:]
        value = part[z, row0 : row0 + n, toks[h]]
        for got in take(kind, h, 2, 3, 4):
            value = value + got
        tot[row0 : row0 + n, toks[h]] = value

    for n, (i, cp) in enumerate(loads):
        cp.wait()
        tok = pl.ds(i * quarter, quarter)
        part[:, :, tok] = mm(wt[...], hidv[:, tok]).reshape(n_ch, per, quarter)
        if n == 1:
            pl.semaphore_wait(barrier, 4 + len(moves))
            far("kv", 1)
        if n == 3:
            far("kv", 0)
            far("q", 1)
            far("q", 0)

    lane_st = iota((cs, st), 1)
    mine = (lane_st >> 4) == iota((cs, st), 0)
    rep = jnp.where((iota((nm, st), 1) & (nm - 1)) == iota((nm, st), 0), 1.0, 0.0)

    def as_row(x):
        return jnp.sum(jnp.where(mine, mm(x, rep, precision=HIGH), 0.0), axis=0, keepdims=True)

    for cp in smalls[1:]:
        cp.wait()
    lam = as_row(rates_ref[...])
    gain = as_row(res_ref[...] * jnp.sqrt(rates_ref[...]))
    steps = iota((CL, st), 0).astype(f32)
    e_hi, e_lo = halves(jnp.exp(-lam * (CL - 1 - steps)))
    e_hl[0] = e_hi
    e_hl[1] = e_lo
    p_hi, p_lo = halves(gain * jnp.exp(-lam * (steps + 1.0)))
    p_hl[0] = p_hi
    p_hl[1] = p_lo

    for h in (1, 0):
        merge_short("kv", h)
    for h in (1, 0):
        merge_long("kv", h)
    for h in (1, 0):
        near("kv", h)

    spread = jnp.where(mine, gain, 0.0)
    taps0 = mm(spread, jnp.exp(-lam * steps), NT, HIGH)
    causal = iota((CL, CL), 1) >= iota((CL, CL), 0)

    def lay_out(c0, c1):
        for c in range(c0, c1):
            line = jnp.broadcast_to(taps0[c : c + 1, :], (CL, CL))
            tri = jnp.where(causal, pltpu.roll(line, 0, 1, stride=1, stride_axis=0), 0.0)
            hi, lo = halves(tri)
            tcat[c, 0:CL] = hi
            tcat[c, CL : 2 * CL] = lo

    lay_out(0, 8)
    lane_per = iota((cs, per), 1)
    row_per = iota((cs, per), 0)
    for i in range(3):
        line = jnp.broadcast_to(taps_ref[i : i + 1, :], (cs, per))
        for j in range(3):
            picked = jnp.where(lane_per == 3 * row_per + j, line, 0.0)
            par[3 * i + j] = jnp.broadcast_to(jnp.sum(picked, axis=1, keepdims=True), (cs, CL))
    skip_line = jnp.broadcast_to(skip_ref[...], (cs, cs))
    skip_col = jnp.sum(
        jnp.where(iota((cs, cs), 0) == iota((cs, cs), 1), skip_line, 0.0), axis=1, keepdims=True
    )

    for h in (1, 0):
        merge_short("q", h)
    for h in (1, 0):
        merge_long("q", h)
    for h in (1, 0):
        near("q", h)
    lay_out(8, 16)
    decay_k = [jnp.exp(-lam * float(CL * k)) for k in range(nk)]
    block = lam * float(length)
    weight = []
    for k in moves:
        src = p ^ k
        weight.append(
            jnp.where(src < p, jnp.exp(-block * jnp.maximum(p - 1 - src, 0).astype(f32)), 0.0)
        )
    total_of("kv", 1)

    def tail(kind, i, row0, n):
        halo_s[row0 : row0 + n] = tot[row0 : row0 + n, length - CL : length].astype(bf16)
        remote(
            ("halo", i),
            halo_s.at[pl.ds(row0, n)],
            halo_r.at[pl.ds(row0, n)],
            sent.at[3],
            halo_rs.at[i],
            (after, z),
        )

    def tail_in(i, row0, n):
        arrived([("halo", i)], halo_r.at[pl.ds(row0, n)], halo_rs.at[i])

    tail("kv", 0, 0, 2 * cs)
    total_of("kv", 0)

    def short(row0, j):
        edge = jnp.where(p > 0, halo_r[row0 : row0 + cs].astype(f32), 0.0)
        x = tot[row0 : row0 + cs]
        ext = jnp.concatenate([edge, x], axis=1)
        one = pltpu.roll(ext, 1, 1)[:, CL:]
        two = pltpu.roll(ext, 2, 1)[:, CL:]
        t = [par[3 * i + j][:, 0:1] for i in range(3)]
        return t[0] * x + t[1] * one + t[2] * two

    tail_in(0, 0, 2 * cs)
    driven = (short(0, 1) * short(cs, 2)).astype(bf16)
    stacked = jnp.concatenate([driven[:, CL * k : CL * (k + 1)] for k in range(nk)], axis=0)
    dscr[...] = stacked.astype(f32)
    states = mm(stacked, e_hl[0]) + mm(stacked, e_hl[1])
    carry = jnp.zeros((cs, st), f32)
    for k in range(nk):
        xscr[cs * k : cs * (k + 1)] = carry
        carry = decay_k[1] * carry + jnp.where(mine, states[cs * k : cs * (k + 1)], 0.0)
    total = jnp.sum(carry, axis=0, keepdims=True)
    st0[...] = total
    for i, k in enumerate(moves):
        remote(("st", i), st0, st1.at[i], sent.at[2], st_rs, (p ^ k, z))

    for c in range(cs):
        line = dscr[pl.ds(c, nk, stride=cs), :].astype(bf16)
        yscr[pl.ds(c, nk, stride=cs), :] = mm(jnp.concatenate([line, line], axis=1), tcat[c])

    total_of("q", 1)
    tail("q", 1, 2 * cs, cs)
    total_of("q", 0)
    tail_in(1, 2 * cs, cs)
    query = short(2 * cs, 0)
    into = jnp.zeros((1, st), f32)
    arrived([("st", i) for i in range(len(moves))], st1, st_rs)
    for i in range(len(moves)):
        into = into + weight[i] * st1[i]
    wide = jnp.where(mine, into, 0.0)
    x = jnp.concatenate(
        [xscr[cs * k : cs * (k + 1)] + decay_k[k] * wide for k in range(nk)], axis=0
    )
    x_hi, x_lo = halves(x)
    y = yscr[...] + mm(x_hi, p_hl[0], NT) + mm(x_lo, p_hl[0], NT) + mm(x_hi, p_hl[1], NT)
    for k in range(nk):
        sl = slice(cs * k, cs * (k + 1))
        tok = slice(CL * k, CL * (k + 1))
        value = query[:, tok] * (y[sl] + skip_col * dscr[sl])
        gath[z, :, tok] = value.astype(bf16)

    hand_on = ((0, 2, None), (0, 1, None), (2, 1, None), (2, 2, 0))

    def piece(i, d, dist):
        part_of = hand_on[i][2]
        tok = slice(None) if part_of is None else toks[part_of if d == 0 else 1 - part_of]
        return gath.at[zz(-dist if d == 0 else dist), :, tok]

    def hand(i, d):
        hold, step, _ = hand_on[i]
        ref = piece(i, d, hold)
        target = (p, zz(step if d == 0 else -step))
        remote(("ag", i, d), ref, ref, sent.at[4], ag_rs.at[d if i == 0 else 2], target)

    for i in (0, 1):
        for d in (0, 1):
            hand(i, d)
    for d in (0, 1):
        arrived([("ag", 0, d)], piece(0, d, 2), ag_rs.at[d])
        hand(2, d)
        hand(3, d)
    arrived([("ag", i, d) for i in (1, 2, 3) for d in (0, 1)], gath.at[pl.ds(0, 5)], ag_rs.at[2])
    out_ref[...] = gath[...]
    assert not pending
    for i, ref in enumerate((kv_s, q_s, st1, halo_s, gath.at[pl.ds(0, n_ch - 1)])):
        waiter(ref, sent.at[i]).wait_send()


def project_kernel(w_ref, x_ref, out, rows_ref, sem):
    count = sem.shape[0]
    tile = out.shape[0] // count
    copies = []
    for i in range(count):
        at = pl.ds(i * tile, tile)
        rows_ref[at] = mm(w_ref[at], x_ref[...]).astype(bf16)
        cp = pltpu.make_async_copy(rows_ref.at[at], out.at[at], sem.at[i])
        cp.start()
        copies.append(cp)
    for cp in copies:
        cp.wait()


def solution(mesh):
    n_seq, n_ch = mesh.shape["seq"], mesh.shape["ch"]

    def body(hidden_in, w_in, short_taps, rates, residues, skip_gain, w_out):
        depth, length = hidden_in.shape
        rows = w_in.shape[1]
        per = rows // n_ch
        cs = per // 3
        st = cs * rates.shape[1]
        half = length // 2
        nk = length // CL
        vmem = pl.BlockSpec(memory_space=pltpu.VMEM)
        dma = pltpu.SemaphoreType.DMA
        gathered = pl.pallas_call(
            functools.partial(conv_kernel, n_seq, n_ch),
            out_shape=jax.ShapeDtypeStruct((n_ch, cs, length), bf16),
            in_specs=[pl.BlockSpec(memory_space=pltpu.HBM)] * 6,
            out_specs=vmem,
            scratch_shapes=[
                pltpu.VMEM(w_in.shape, bf16),
                pltpu.VMEM(short_taps.shape, f32),
                pltpu.VMEM(rates.shape, f32),
                pltpu.VMEM(residues.shape, f32),
                pltpu.VMEM((1, cs), f32),
                pltpu.VMEM((depth, length), bf16),
                pltpu.VMEM((rows, depth), bf16),
                pltpu.VMEM((n_ch, per, length), f32),
                pltpu.VMEM((2, 7, 2 * cs, half), bf16),
                pltpu.VMEM((2, 7, 2 * cs, half), bf16),
                pltpu.VMEM((2, 7, cs, half), bf16),
                pltpu.VMEM((2, 7, cs, half), bf16),
                pltpu.VMEM((per, length), f32),
                pltpu.VMEM((per, CL), bf16),
                pltpu.VMEM((per, CL), bf16),
                pltpu.VMEM((n_ch, cs, length), bf16),
                pltpu.VMEM((1, st), f32),
                pltpu.VMEM((n_seq - 1, 1, st), f32),
                pltpu.VMEM((9, cs, CL), f32),
                pltpu.VMEM((2, CL, st), bf16),
                pltpu.VMEM((2, CL, st), bf16),
                pltpu.VMEM((cs, 2 * CL, CL), bf16),
                pltpu.VMEM((nk * cs, CL), f32),
                pltpu.VMEM((nk * cs, CL), f32),
                pltpu.VMEM((nk * cs, st), f32),
                dma((4,)),
                dma((5,)),
                dma((5,)),
                dma((2, 3)),
                dma((2, 3)),
                dma((2,)),
                dma,
                dma((3,)),
            ],
            compiler_params=pltpu.CompilerParams(
                collective_id=0, has_side_effects=True, vmem_limit_bytes=40 * 1024 * 1024
            ),
        )(
            *(
                pltpu.with_memory_space_constraint(x, pltpu.HBM)
                for x in (hidden_in, w_in, short_taps, rates, residues, skip_gain.reshape(1, cs))
            )
        )
        slab = n_ch * cs
        return pl.pallas_call(
            project_kernel,
            out_shape=jax.ShapeDtypeStruct((w_out.shape[0], length), bf16),
            in_specs=[vmem] * 2,
            out_specs=pl.BlockSpec(memory_space=pl.ANY),
            scratch_shapes=[pltpu.VMEM((w_out.shape[0], length), bf16), dma((8,))],
            compiler_params=pltpu.CompilerParams(vmem_limit_bytes=16 * 1024 * 1024),
        )(w_out, gathered.reshape(slab, length))

    in_specs = (
        P("ch", "seq"),
        P("ch", None),
        P(None, "ch"),
        P("ch", None),
        P("ch", None),
        P("ch"),
        P("ch", None),
    )
    return jax.shard_map(
        body, mesh=mesh, in_specs=in_specs, out_specs=P("ch", "seq"), check_vma=False
    )
```

```python
import functools

import jax
import jax.numpy as jnp
from jax import lax
from jax.experimental import pallas as pl
from jax.experimental.pallas import tpu as pltpu
from jax.sharding import PartitionSpec as P

MESH = pl.DeviceIdType.MESH
f32 = jnp.float32
bf16 = jnp.bfloat16
HIGH = lax.Precision.HIGHEST
NT = (((1,), (1,)), ((), ()))
NN = (((1,), (0,)), ((), ()))
TN = (((0,), (0,)), ((), ()))
CL = 128


def mm(a, b, dims=NN, precision=None):
    return lax.dot_general(a, b, dims, precision=precision, preferred_element_type=f32)


def halves(x):
    hi = x.astype(bf16)
    return hi, (x - hi.astype(f32)).astype(bf16)


def iota(shape, dim):
    return lax.broadcasted_iota(jnp.int32, shape, dim)


def conv_kernel(
    n_seq,
    n_ch,
    hid,
    w_in,
    taps_in,
    rates_in,
    res_in,
    skip_in,
    out_ref,
    w_ref,
    taps_ref,
    rates_ref,
    res_ref,
    skip_ref,
    hidv,
    part,
    kv_s,
    kv_r,
    q_s,
    q_r,
    tot,
    halo_s,
    halo_r,
    gath,
    st0,
    st1,
    par,
    e_hl,
    p_hl,
    tcat,
    dscr,
    yscr,
    xscr,
    load_sem,
    small_sem,
    sent,
    kv_rs,
    q_rs,
    halo_rs,
    st_rs,
    ag_rs,
):
    p = lax.axis_index("seq")
    z = lax.axis_index("ch")
    depth, length = hid.shape
    rows = w_ref.shape[1]
    per = rows // n_ch
    cs = per // 3
    nm = rates_ref.shape[1]
    st = cs * nm
    half = length // 2
    nk = length // CL
    quarter = length // 4

    def zz(k):
        return lax.rem(z + (k + n_ch), n_ch)

    ring = (zz(1), zz(-1))
    ring2 = (zz(2), zz(-2))
    pending = {}

    smalls = []
    pairs = ((w_in, w_ref), (rates_in, rates_ref), (res_in, res_ref), (taps_in, taps_ref), (skip_in, skip_ref))
    for i, (src, dst) in enumerate(pairs):
        cp = pltpu.make_async_copy(src, dst, small_sem.at[i])
        smalls.append(cp)
    smalls[0].start()
    loads = []
    for i in (3, 2, 1, 0):
        cp = pltpu.make_async_copy(
            hid.at[:, pl.ds(i * quarter, quarter)],
            hidv.at[:, pl.ds(i * quarter, quarter)],
            load_sem.at[i],
        )
        cp.start()
        loads.append((i, cp))
    for cp in smalls[1:]:
        cp.start()

    def hops(k):
        return (0, 1, 2, 1)[k >> 1 & 3] + (0, 1, 2, 1)[k >> 3]

    moves = sorted(range(1, n_seq), key=lambda k: -hops(k))
    after = lax.rem(p + 1, n_seq)
    barrier = pltpu.get_barrier_semaphore()
    for s in ring + ring2:
        pl.semaphore_signal(barrier, inc=1, device_id=(p, s), device_id_type=MESH)
    for k in moves:
        pl.semaphore_signal(barrier, inc=1, device_id=(p ^ k, z), device_id_type=MESH)

    smalls[0].wait()

    def remote(key, src, dst, ssem, rsem, dev):
        pltpu.make_async_remote_copy(
            src_ref=src,
            dst_ref=dst,
            send_sem=ssem,
            recv_sem=rsem,
            device_id=dev,
            device_id_type=MESH,
        ).start()
        pending[key] = (dst, rsem)

    def waiter(ref, sem):
        return pltpu.make_async_remote_copy(
            src_ref=ref,
            dst_ref=ref,
            send_sem=sem,
            recv_sem=sem,
            device_id=(p, ring[0]),
            device_id_type=MESH,
        )

    def arrived(keys, ref, sem):
        for key in keys:
            pending.pop(key)
        waiter(ref, sem).wait_recv()

    bufs = {
        "kv": (kv_s, kv_r, sent.at[0], kv_rs, 0, 2 * cs),
        "q": (q_s, q_r, sent.at[1], q_rs, 2 * cs, cs),
    }
    toks = (pl.ds(0, half), pl.ds(half, half))

    def rows_of(kind, dest, h):
        comps = (1, 2) if kind == "kv" else (0,)
        picked = []
        for j in comps:
            pieces = [
                part[k, dest, pl.ds(j, cs, stride=3), :]
                for k in range(h * nk // 2, (h + 1) * nk // 2)
            ]
            picked.append(jnp.concatenate(pieces, axis=1))
        return jnp.concatenate(picked, axis=0)

    def own(kind, h, d, dist):
        return rows_of(kind, zz(dist if d == 0 else -dist), h)

    def long_way(h):
        return 0 if h == 1 else 1

    def send(kind, h, d, m, value):
        sbuf, rbuf, ss, rs = bufs[kind][:4]
        slot = (0, 1, 3, 5)[m] if d == long_way(h) else (None, 2, 4, 6)[m]
        sbuf[h, slot] = value.astype(bf16)
        to = (ring2, ring)[m % 2][d]
        got = rs.at[h, (0, 0, 1, 2, 2, 2, 2)[slot]]
        remote((kind, h, slot), sbuf.at[h, slot], rbuf.at[h, slot], ss, got, (p, to))

    def take(kind, h, group, first, count):
        _, rbuf, _, rs = bufs[kind][:4]
        keys = [(kind, h, first + i) for i in range(count)]
        arrived(keys, rbuf.at[h, pl.ds(first, count)], rs.at[h, group])
        return [rbuf[h, first + i].astype(f32) for i in range(count)]

    def far(kind, h):
        send(kind, h, long_way(h), 0, own(kind, h, long_way(h), 4))
        for d in (0, 1):
            send(kind, h, d, 1, own(kind, h, d, 3))

    def near(kind, h):
        for d in (0, 1):
            send(kind, h, d, 3, own(kind, h, d, 1))

    def merge_short(kind, h):
        d = 1 - long_way(h)
        (got,) = take(kind, h, 1, 2, 1)
        send(kind, h, d, 2, own(kind, h, d, 2) + got)

    def merge_long(kind, h):
        d = long_way(h)
        four, three = take(kind, h, 0, 0, 2)
        send(kind, h, d, 2, own(kind, h, d, 2) + three + four)

    def total_of(kind, h):
        row0, n = bufs[kind][4:]
        value = rows_of(kind, z, h)
        for got in take(kind, h, 2, 3, 4):
            value = value + got
        tot[row0 : row0 + n, toks[h]] = value

    for n, (i, cp) in enumerate(loads):
        cp.wait()
        tok = pl.ds(i * quarter, quarter)
        sums = mm(w_ref[...], hidv[:, tok], TN)
        for k in range(quarter // CL):
            piece = sums[:, CL * k : CL * (k + 1)].reshape(n_ch, per, CL)
            part[i * quarter // CL + k] = piece
        if n == 1:
            pl.semaphore_wait(barrier, 4 + len(moves))
            far("kv", 1)
        if n == 3:
            far("kv", 0)
            far("q", 1)
            far("q", 0)

    lane_st = iota((cs, st), 1)
    mine = (lane_st >> 4) == iota((cs, st), 0)
    rep = jnp.where((iota((nm, st), 1) & (nm - 1)) == iota((nm, st), 0), 1.0, 0.0)

    def as_row(x):
        return jnp.sum(jnp.where(mine, mm(x, rep, precision=HIGH), 0.0), axis=0, keepdims=True)

    for cp in smalls[1:]:
        cp.wait()
    lam = as_row(rates_ref[...])
    gain = as_row(res_ref[...] * jnp.sqrt(rates_ref[...]))
    steps = iota((CL, st), 0).astype(f32)
    e_hi, e_lo = halves(jnp.exp(-lam * (CL - 1 - steps)))
    e_hl[0:CL] = e_hi
    e_hl[CL : 2 * CL] = e_lo
    p_hi, p_lo = halves(gain * jnp.exp(-lam * (steps + 1.0)))
    p_hl[:, 0:st] = p_hi
    p_hl[:, st : 2 * st] = p_hi
    p_hl[:, 2 * st : 3 * st] = p_lo

    for h in (1, 0):
        merge_short("kv", h)
    for h in (1, 0):
        merge_long("kv", h)
    for h in (1, 0):
        near("kv", h)

    spread = jnp.where(mine, gain, 0.0)
    taps0 = mm(spread, jnp.exp(-lam * steps), NT, HIGH)
    causal = iota((CL, CL), 1) >= iota((CL, CL), 0)

    def lay_out(c0, c1):
        for c in range(c0, c1):
            line = jnp.broadcast_to(taps0[c : c + 1, :], (CL, CL))
            tri = jnp.where(causal, pltpu.roll(line, 0, 1, stride=1, stride_axis=0), 0.0)
            hi, lo = halves(tri)
            tcat[c, 0:CL] = hi
            tcat[c, CL : 2 * CL] = lo

    lay_out(0, 8)
    lane_per = iota((cs, per), 1)
    row_per = iota((cs, per), 0)
    for i in range(3):
        line = jnp.broadcast_to(taps_ref[i : i + 1, :], (cs, per))
        for j in range(3):
            picked = jnp.where(lane_per == 3 * row_per + j, line, 0.0)
            par[3 * i + j] = jnp.broadcast_to(jnp.sum(picked, axis=1, keepdims=True), (cs, CL))
    skip_line = jnp.broadcast_to(skip_ref[...], (cs, cs))
    skip_col = jnp.sum(
        jnp.where(iota((cs, cs), 0) == iota((cs, cs), 1), skip_line, 0.0), axis=1, keepdims=True
    )

    for h in (1, 0):
        merge_short("q", h)
    for h in (1, 0):
        merge_long("q", h)
    for h in (1, 0):
        near("q", h)

    lay_out(8, 16)
    decay_k = [jnp.exp(-lam * float(CL * k)) for k in range(nk)]
    block = lam * float(length)
    weight = []
    for k in moves:
        src = p ^ k
        weight.append(
            jnp.where(src < p, jnp.exp(-block * jnp.maximum(p - 1 - src, 0).astype(f32)), 0.0)
        )

    total_of("kv", 1)

    def tail(kind, i, row0, n):
        halo_s[row0 : row0 + n] = tot[row0 : row0 + n, length - CL : length].astype(bf16)
        remote(
            ("halo", i),
            halo_s.at[pl.ds(row0, n)],
            halo_r.at[pl.ds(row0, n)],
            sent.at[3],
            halo_rs.at[i],
            (after, z),
        )

    def tail_in(i, row0, n):
        arrived([("halo", i)], halo_r.at[pl.ds(row0, n)], halo_rs.at[i])

    tail("kv", 0, 0, 2 * cs)
    total_of("kv", 0)

    def short(row0, j):
        edge = jnp.where(p > 0, halo_r[row0 : row0 + cs].astype(f32), 0.0)
        x = tot[row0 : row0 + cs]
        ext = jnp.concatenate([edge, x], axis=1)
        one = pltpu.roll(ext, 1, 1)[:, CL:]
        two = pltpu.roll(ext, 2, 1)[:, CL:]
        t = [par[3 * i + j][:, 0:1] for i in range(3)]
        return t[0] * x + t[1] * one + t[2] * two

    tail_in(0, 0, 2 * cs)

    driven = (short(0, 1) * short(cs, 2)).astype(bf16)
    stacked = jnp.concatenate([driven[:, CL * k : CL * (k + 1)] for k in range(nk)], axis=0)
    dscr[...] = stacked.astype(f32)
    states = mm(jnp.concatenate([stacked, stacked], axis=1), e_hl[...])
    carry = jnp.zeros((cs, st), f32)
    for k in range(nk):
        xscr[cs * k : cs * (k + 1)] = carry
        carry = decay_k[1] * carry + jnp.where(mine, states[cs * k : cs * (k + 1)], 0.0)
    total = jnp.sum(carry, axis=0, keepdims=True)
    st0[...] = total
    for i, k in enumerate(moves):
        remote(("st", i), st0, st1.at[i], sent.at[2], st_rs, (p ^ k, z))

    total_of("q", 1)
    tail("q", 1, 2 * cs, cs)
    total_of("q", 0)

    for c in range(cs):
        line = dscr[pl.ds(c, nk, stride=cs), :].astype(bf16)
        yscr[pl.ds(c, nk, stride=cs), :] = mm(jnp.concatenate([line, line], axis=1), tcat[c])

    tail_in(1, 2 * cs, cs)
    query = short(2 * cs, 0)

    arrived([("st", i) for i in range(len(moves))], st1, st_rs)
    terms = [weight[i] * st1[i] for i in range(len(moves))]
    while len(terms) > 1:
        terms = [sum(terms[i : i + 2]) for i in range(0, len(terms), 2)]
    into = terms[0]

    wide = jnp.where(mine, into, 0.0)
    x = jnp.concatenate(
        [xscr[cs * k : cs * (k + 1)] + decay_k[k] * wide for k in range(nk)], axis=0
    )
    x_hi, x_lo = halves(x)
    y = yscr[...] + mm(jnp.concatenate([x_hi, x_lo, x_hi], axis=1), p_hl[...], NT)
    for k in range(nk):
        sl = slice(cs * k, cs * (k + 1))
        tok = slice(CL * k, CL * (k + 1))
        value = query[:, tok] * (y[sl] + skip_col * dscr[sl])
        gath[z, :, tok] = value.astype(bf16)

    hand_on = ((0, 2, 0), (0, 2, 1), (0, 1, None), (2, 2, 0), (2, 1, 0), (2, 1, 1))

    def piece(i, d, dist):
        part_of = hand_on[i][2]
        tok = slice(None) if part_of is None else toks[part_of if d == 0 else 1 - part_of]
        return gath.at[zz(-dist if d == 0 else dist), :, tok]

    def hand(i, d):
        hold, step, _ = hand_on[i]
        ref = piece(i, d, hold)
        target = (p, zz(step if d == 0 else -step))
        remote(("ag", i, d), ref, ref, sent.at[4], ag_rs.at[2 * i + d if i < 2 else 4], target)

    for i in (0, 1, 2):
        for d in (0, 1):
            hand(i, d)
    for i in (0, 1):
        for d in (0, 1):
            arrived([("ag", i, d)], piece(i, d, 2), ag_rs.at[2 * i + d])
            if i == 0:
                hand(3, d)
            hand(4 + i, d)
    arrived([("ag", i, d) for i in range(2, 6) for d in (0, 1)], gath.at[pl.ds(0, 5)], ag_rs.at[4])
    out_ref[...] = gath[...]

    assert not pending
    for i, ref in enumerate((kv_s, q_s, st1, halo_s, gath.at[pl.ds(0, n_ch - 1)])):
        waiter(ref, sent.at[i]).wait_send()


def project_kernel(w_ref, x_ref, out, rows_ref, sem):
    count = sem.shape[0]
    tile = out.shape[0] // count
    copies = []
    for i in range(count):
        at = pl.ds(i * tile, tile)
        rows_ref[at] = mm(w_ref[at], x_ref[...]).astype(bf16)
        cp = pltpu.make_async_copy(rows_ref.at[at], out.at[at], sem.at[i])
        cp.start()
        copies.append(cp)
    for cp in copies:
        cp.wait()


def solution(mesh):
    n_seq, n_ch = mesh.shape["seq"], mesh.shape["ch"]

    def body(hidden_in, w_in, short_taps, rates, residues, skip_gain, w_out):
        depth, length = hidden_in.shape
        rows = w_in.shape[1]
        per = rows // n_ch
        cs = per // 3
        st = cs * rates.shape[1]
        half = length // 2
        nk = length // CL
        vmem = pl.BlockSpec(memory_space=pltpu.VMEM)
        dma = pltpu.SemaphoreType.DMA
        gathered = pl.pallas_call(
            functools.partial(conv_kernel, n_seq, n_ch),
            out_shape=jax.ShapeDtypeStruct((n_ch, cs, length), bf16),
            in_specs=[pl.BlockSpec(memory_space=pltpu.HBM)] * 6,
            out_specs=vmem,
            scratch_shapes=[
                pltpu.VMEM(w_in.shape, bf16),
                pltpu.VMEM(short_taps.shape, f32),
                pltpu.VMEM(rates.shape, f32),
                pltpu.VMEM(residues.shape, f32),
                pltpu.VMEM((1, cs), f32),
                pltpu.VMEM((depth, length), bf16),
                pltpu.VMEM((nk, n_ch, per, CL), f32),
                pltpu.VMEM((2, 7, 2 * cs, half), bf16),
                pltpu.VMEM((2, 7, 2 * cs, half), bf16),
                pltpu.VMEM((2, 7, cs, half), bf16),
                pltpu.VMEM((2, 7, cs, half), bf16),
                pltpu.VMEM((per, length), f32),
                pltpu.VMEM((per, CL), bf16),
                pltpu.VMEM((per, CL), bf16),
                pltpu.VMEM((n_ch, cs, length), bf16),
                pltpu.VMEM((1, st), f32),
                pltpu.VMEM((n_seq - 1, 1, st), f32),
                pltpu.VMEM((9, cs, CL), f32),
                pltpu.VMEM((2 * CL, st), bf16),
                pltpu.VMEM((CL, 3 * st), bf16),
                pltpu.VMEM((cs, 2 * CL, CL), bf16),
                pltpu.VMEM((nk * cs, CL), f32),
                pltpu.VMEM((nk * cs, CL), f32),
                pltpu.VMEM((nk * cs, st), f32),
                dma((4,)),
                dma((5,)),
                dma((5,)),
                dma((2, 3)),
                dma((2, 3)),
                dma((2,)),
                dma,
                dma((5,)),
            ],
            compiler_params=pltpu.CompilerParams(
                collective_id=0, has_side_effects=True, vmem_limit_bytes=40 * 1024 * 1024
            ),
        )(
            *(
                pltpu.with_memory_space_constraint(x, pltpu.HBM)
                for x in (hidden_in, w_in, short_taps, rates, residues, skip_gain.reshape(1, cs))
            )
        )
        slab = n_ch * cs
        return pl.pallas_call(
            project_kernel,
            out_shape=jax.ShapeDtypeStruct((w_out.shape[0], length), bf16),
            in_specs=[vmem] * 2,
            out_specs=pl.BlockSpec(memory_space=pl.ANY),
            scratch_shapes=[pltpu.VMEM((w_out.shape[0], length), bf16), dma((8,))],
            compiler_params=pltpu.CompilerParams(vmem_limit_bytes=16 * 1024 * 1024),
        )(w_out, gathered.reshape(slab, length))

    in_specs = (
        P("ch", "seq"),
        P("ch", None),
        P(None, "ch"),
        P("ch", None),
        P("ch", None),
        P("ch"),
        P("ch", None),
    )
    return jax.shard_map(
        body, mesh=mesh, in_specs=in_specs, out_specs=P("ch", "seq"), check_vma=False
    )
```

```python
import functools

import jax
import jax.numpy as jnp
from jax import lax
from jax.experimental import pallas as pl
from jax.experimental.pallas import tpu as pltpu
from jax.sharding import PartitionSpec as P

MESH = pl.DeviceIdType.MESH
f32 = jnp.float32
bf16 = jnp.bfloat16
HIGH = lax.Precision.HIGHEST
NT = (((1,), (1,)), ((), ()))
NN = (((1,), (0,)), ((), ()))
TN = (((0,), (0,)), ((), ()))
CL = 128


def mm(a, b, dims=NN, precision=None):
    return lax.dot_general(a, b, dims, precision=precision, preferred_element_type=f32)


def halves(x):
    hi = x.astype(bf16)
    return hi, (x - hi.astype(f32)).astype(bf16)


def iota(shape, dim):
    return lax.broadcasted_iota(jnp.int32, shape, dim)


def conv_kernel(
    n_seq,
    n_ch,
    hid,
    w_in,
    taps_in,
    rates_in,
    res_in,
    skip_in,
    out_ref,
    w_ref,
    taps_ref,
    rates_ref,
    res_ref,
    skip_ref,
    hidv,
    part,
    kv_s,
    kv_r,
    q_s,
    q_r,
    tot,
    halo_s,
    halo_r,
    gath,
    st0,
    st1,
    weight,
    into,
    par,
    e_hl,
    p_hl,
    tcat,
    dscr,
    yscr,
    xscr,
    load_sem,
    small_sem,
    sent,
    kv_rs,
    q_rs,
    halo_rs,
    st_ss,
    st_rs,
    ready,
    ag_rs,
):
    p = lax.axis_index("seq")
    z = lax.axis_index("ch")
    depth, length = hid.shape
    rows = w_ref.shape[1]
    per = rows // n_ch
    cs = per // 3
    nm = rates_ref.shape[1]
    st = cs * nm
    half = length // 2
    nk = length // CL
    quarter = length // 4

    def zz(k):
        return lax.rem(z + (k + n_ch), n_ch)

    ring = (zz(1), zz(-1))
    ring2 = (zz(2), zz(-2))
    pending = {}

    smalls = []
    pairs = ((w_in, w_ref), (rates_in, rates_ref), (res_in, res_ref), (taps_in, taps_ref), (skip_in, skip_ref))
    for i, (src, dst) in enumerate(pairs):
        cp = pltpu.make_async_copy(src, dst, small_sem.at[i])
        smalls.append(cp)
    smalls[0].start()
    loads = []
    for i in (3, 2, 1, 0):
        cp = pltpu.make_async_copy(
            hid.at[:, pl.ds(i * quarter, quarter)],
            hidv.at[:, pl.ds(i * quarter, quarter)],
            load_sem.at[i],
        )
        cp.start()
        loads.append((i, cp))
    for cp in smalls[1:]:
        cp.start()

    def hops(k):
        return (0, 1, 2, 1)[k >> 1 & 3] + (0, 1, 2, 1)[k >> 3]

    bits = n_seq.bit_length() - 1
    groups = [sorted(range(1 << b, 2 << b), key=lambda k: -hops(k)) for b in range(bits)]

    def to_later(b):
        return pl.when((p >> b) & 1 == 0)

    def to_earlier(b):
        return pl.when((p >> b) & 1 == 1)

    after = lax.rem(p + 1, n_seq)
    barrier = pltpu.get_barrier_semaphore()
    for s in ring + ring2:
        pl.semaphore_signal(barrier, inc=1, device_id=(p, s), device_id_type=MESH)
    for b in reversed(range(bits)):

        @to_later(b)
        def _():
            for k in groups[b]:
                pl.semaphore_signal(barrier, inc=1, device_id=(p ^ k, z), device_id_type=MESH)

    smalls[0].wait()

    def remote(key, src, dst, ssem, rsem, dev):
        pltpu.make_async_remote_copy(
            src_ref=src,
            dst_ref=dst,
            send_sem=ssem,
            recv_sem=rsem,
            device_id=dev,
            device_id_type=MESH,
        ).start()
        pending[key] = (dst, rsem)

    def waiter(ref, sem):
        return pltpu.make_async_remote_copy(
            src_ref=ref,
            dst_ref=ref,
            send_sem=sem,
            recv_sem=sem,
            device_id=(p, ring[0]),
            device_id_type=MESH,
        )

    def arrived(keys, ref, sem):
        for key in keys:
            pending.pop(key)
        waiter(ref, sem).wait_recv()

    bufs = {
        "kv": (kv_s, kv_r, sent.at[0], kv_rs, 0, 2 * cs),
        "q": (q_s, q_r, sent.at[1], q_rs, 2 * cs, cs),
    }
    toks = (pl.ds(0, half), pl.ds(half, half))

    def rows_of(kind, dest, h):
        comps = (1, 2) if kind == "kv" else (0,)
        picked = []
        for j in comps:
            pieces = [
                part[k, dest, pl.ds(j, cs, stride=3), :]
                for k in range(h * nk // 2, (h + 1) * nk // 2)
            ]
            picked.append(jnp.concatenate(pieces, axis=1))
        return jnp.concatenate(picked, axis=0)

    def own(kind, h, d, dist):
        return rows_of(kind, zz(dist if d == 0 else -dist), h)

    def long_way(h):
        return 0 if h == 1 else 1

    def send(kind, h, d, m, value):
        sbuf, rbuf, ss, rs = bufs[kind][:4]
        slot = (0, 1, 3, 5)[m] if d == long_way(h) else (None, 2, 4, 6)[m]
        sbuf[h, slot] = value.astype(bf16)
        to = (ring2, ring)[m % 2][d]
        got = rs.at[h, (0, 0, 1, 2, 2, 2, 2)[slot]]
        remote((kind, h, slot), sbuf.at[h, slot], rbuf.at[h, slot], ss, got, (p, to))

    def take(kind, h, group, first, count):
        _, rbuf, _, rs = bufs[kind][:4]
        keys = [(kind, h, first + i) for i in range(count)]
        arrived(keys, rbuf.at[h, pl.ds(first, count)], rs.at[h, group])
        return [rbuf[h, first + i].astype(f32) for i in range(count)]

    def far(kind, h):
        send(kind, h, long_way(h), 0, own(kind, h, long_way(h), 4))
        for d in (0, 1):
            send(kind, h, d, 1, own(kind, h, d, 3))

    def near(kind, h):
        for d in (0, 1):
            send(kind, h, d, 3, own(kind, h, d, 1))

    def merge_short(kind, h):
        d = 1 - long_way(h)
        (got,) = take(kind, h, 1, 2, 1)
        send(kind, h, d, 2, own(kind, h, d, 2) + got)

    def merge_long(kind, h):
        d = long_way(h)
        four, three = take(kind, h, 0, 0, 2)
        send(kind, h, d, 2, own(kind, h, d, 2) + three + four)

    def total_of(kind, h):
        row0, n = bufs[kind][4:]
        value = rows_of(kind, z, h)
        for got in take(kind, h, 2, 3, 4):
            value = value + got
        tot[row0 : row0 + n, toks[h]] = value

    for n, (i, cp) in enumerate(loads):
        cp.wait()
        tok = pl.ds(i * quarter, quarter)
        sums = mm(w_ref[...], hidv[:, tok], TN)
        for k in range(quarter // CL):
            piece = sums[:, CL * k : CL * (k + 1)].reshape(n_ch, per, CL)
            part[i * quarter // CL + k] = piece
        if n == 1:
            pl.semaphore_wait(barrier, 4 + p)
            far("kv", 1)
        if n == 3:
            far("kv", 0)
            far("q", 1)
            far("q", 0)
    for b in reversed(range(bits)):

        @to_earlier(b)
        def _():
            for k in groups[b]:
                pl.semaphore_signal(ready, inc=1, device_id=(p ^ k, z), device_id_type=MESH)

    @pl.when(p == 0)
    def _():
        halo_r[...] = jnp.zeros_like(halo_r)

    lane_st = iota((cs, st), 1)
    mine = (lane_st >> 4) == iota((cs, st), 0)
    rep = jnp.where((iota((nm, st), 1) & (nm - 1)) == iota((nm, st), 0), 1.0, 0.0)

    def as_row(x):
        return jnp.sum(jnp.where(mine, mm(x, rep, precision=HIGH), 0.0), axis=0, keepdims=True)

    for cp in smalls[1:]:
        cp.wait()
    lam = as_row(rates_ref[...])
    gain = as_row(res_ref[...] * jnp.sqrt(rates_ref[...]))
    steps = iota((CL, st), 0).astype(f32)
    e_hi, e_lo = halves(jnp.exp(-lam * (CL - 1 - steps)))
    e_hl[0:CL] = e_hi
    e_hl[CL : 2 * CL] = e_lo
    p_hi, p_lo = halves(gain * jnp.exp(-lam * (steps + 1.0)))
    p_hl[:, 0:st] = p_hi
    p_hl[:, st : 2 * st] = p_hi
    p_hl[:, 2 * st : 3 * st] = p_lo

    for h in (1, 0):
        merge_short("kv", h)
    for h in (1, 0):
        merge_long("kv", h)
    for h in (1, 0):
        near("kv", h)

    spread = jnp.where(mine, gain, 0.0)
    taps0 = mm(spread, jnp.exp(-lam * steps), NT, HIGH)
    causal = iota((CL, CL), 1) >= iota((CL, CL), 0)

    def lay_out(c0, c1):
        for c in range(c0, c1):
            line = jnp.broadcast_to(taps0[c : c + 1, :], (CL, CL))
            tri = jnp.where(causal, pltpu.roll(line, 0, 1, stride=1, stride_axis=0), 0.0)
            hi, lo = halves(tri)
            tcat[c, 0:CL] = hi
            tcat[c, CL : 2 * CL] = lo

    lay_out(0, 8)
    lane_per = iota((cs, per), 1)
    row_per = iota((cs, per), 0)
    for i in range(3):
        line = jnp.broadcast_to(taps_ref[i : i + 1, :], (cs, per))
        for j in range(3):
            picked = jnp.where(lane_per == 3 * row_per + j, line, 0.0)
            par[3 * i + j] = jnp.broadcast_to(jnp.sum(picked, axis=1, keepdims=True), (cs, CL))
    skip_line = jnp.broadcast_to(skip_ref[...], (cs, cs))
    skip_col = jnp.sum(
        jnp.where(iota((cs, cs), 0) == iota((cs, cs), 1), skip_line, 0.0), axis=1, keepdims=True
    )

    for h in (1, 0):
        merge_short("q", h)
    for h in (1, 0):
        merge_long("q", h)
    for h in (1, 0):
        near("q", h)
    lay_out(8, 16)
    decay_k = [jnp.exp(-lam * float(CL * k)) for k in range(nk)]
    block = lam * float(length)
    for k in range(1, n_seq):
        apart = jnp.maximum(p - 1 - (p ^ k), 0)
        weight[k] = jnp.exp(-block * apart.astype(f32))
    total_of("kv", 1)

    def tail(i, row0, n):
        halo_s[row0 : row0 + n] = tot[row0 : row0 + n, length - CL : length].astype(bf16)
        at = pl.ds(row0, n)

        @pl.when(p < n_seq - 1)
        def _():
            remote(
                ("halo", i), halo_s.at[at], halo_r.at[at], sent.at[2], halo_rs.at[i], (after, z)
            )

    def tail_in(i, row0, n):
        @pl.when(p > 0)
        def _():
            arrived([("halo", i)], halo_r.at[pl.ds(row0, n)], halo_rs.at[i])

    @pl.when(p < n_seq - 1)
    def _():
        pl.semaphore_wait(ready, n_seq - 1 - p)

    tail(0, 0, 2 * cs)
    total_of("kv", 0)

    def short(row0, j):
        edge = halo_r[row0 : row0 + cs].astype(f32)
        x = tot[row0 : row0 + cs]
        ext = jnp.concatenate([edge, x], axis=1)
        one = pltpu.roll(ext, 1, 1)[:, CL:]
        two = pltpu.roll(ext, 2, 1)[:, CL:]
        t = [par[3 * i + j][:, 0:1] for i in range(3)]
        return t[0] * x + t[1] * one + t[2] * two

    tail_in(0, 0, 2 * cs)
    driven = (short(0, 1) * short(cs, 2)).astype(bf16)
    stacked = jnp.concatenate([driven[:, CL * k : CL * (k + 1)] for k in range(nk)], axis=0)
    dscr[...] = stacked.astype(f32)
    states = mm(jnp.concatenate([stacked, stacked], axis=1), e_hl[...])
    carry = jnp.zeros((cs, st), f32)
    for k in range(nk):
        xscr[cs * k : cs * (k + 1)] = carry
        carry = decay_k[1] * carry + jnp.where(mine, states[cs * k : cs * (k + 1)], 0.0)
    total = jnp.sum(carry, axis=0, keepdims=True)
    st0[...] = total
    for b in reversed(range(bits)):

        @to_later(b)
        def _():
            for k in groups[b]:
                remote(("st", k), st0, st1.at[k], st_ss.at[b], st_rs.at[b], (p ^ k, z))

    total_of("q", 1)
    tail(1, 2 * cs, cs)
    total_of("q", 0)
    for c in range(cs):
        line = dscr[pl.ds(c, nk, stride=cs), :].astype(bf16)
        yscr[pl.ds(c, nk, stride=cs), :] = mm(jnp.concatenate([line, line], axis=1), tcat[c])

    tail_in(1, 2 * cs, cs)
    query = short(2 * cs, 0)
    into[...] = jnp.zeros_like(into)
    for b in reversed(range(bits)):

        @to_earlier(b)
        def _():
            group = pl.ds(1 << b, 1 << b)
            arrived([("st", k) for k in groups[b]], st1.at[group], st_rs.at[b])
            into[...] += jnp.sum(weight[group] * st1[group], axis=0)

    wide = jnp.where(mine, into[...], 0.0)
    x = jnp.concatenate(
        [xscr[cs * k : cs * (k + 1)] + decay_k[k] * wide for k in range(nk)], axis=0
    )
    x_hi, x_lo = halves(x)
    y = yscr[...] + mm(jnp.concatenate([x_hi, x_lo, x_hi], axis=1), p_hl[...], NT)
    for k in range(nk):
        sl = slice(cs * k, cs * (k + 1))
        tok = slice(CL * k, CL * (k + 1))
        value = query[:, tok] * (y[sl] + skip_col * dscr[sl])
        gath[z, :, tok] = value.astype(bf16)

    hand_on = ((0, 2, 0), (0, 2, 1), (0, 1, None), (2, 2, 0), (2, 1, 0), (2, 1, 1))

    def piece(i, d, dist):
        part_of = hand_on[i][2]
        tok = slice(None) if part_of is None else toks[part_of if d == 0 else 1 - part_of]
        return gath.at[zz(-dist if d == 0 else dist), :, tok]

    def hand(i, d):
        hold, step, _ = hand_on[i]
        ref = piece(i, d, hold)
        target = (p, zz(step if d == 0 else -step))
        remote(("ag", i, d), ref, ref, sent.at[3], ag_rs.at[2 * i + d if i < 2 else 4], target)

    for i in (0, 1, 2):
        for d in (0, 1):
            hand(i, d)
    for i in (0, 1):
        for d in (0, 1):
            arrived([("ag", i, d)], piece(i, d, 2), ag_rs.at[2 * i + d])
            if i == 0:
                hand(3, d)
            hand(4 + i, d)
    arrived([("ag", i, d) for i in range(2, 6) for d in (0, 1)], gath.at[pl.ds(0, 5)], ag_rs.at[4])
    out_ref[...] = gath[...]
    assert not pending
    for i, ref in ((0, kv_s), (1, q_s), (3, gath.at[pl.ds(0, n_ch - 1)])):
        waiter(ref, sent.at[i]).wait_send()

    @pl.when(p < n_seq - 1)
    def _():
        waiter(halo_s, sent.at[2]).wait_send()

    for b in range(bits):

        @to_later(b)
        def _():
            waiter(st1.at[pl.ds(1 << b, 1 << b)], st_ss.at[b]).wait_send()


def project_kernel(w_ref, x_ref, out, rows_ref, sem):
    count = sem.shape[0]
    tile = out.shape[0] // count
    copies = []
    for i in range(count):
        at = pl.ds(i * tile, tile)
        rows_ref[at] = mm(w_ref[at], x_ref[...]).astype(bf16)
        cp = pltpu.make_async_copy(rows_ref.at[at], out.at[at], sem.at[i])
        cp.start()
        copies.append(cp)
    for cp in copies:
        cp.wait()


def solution(mesh):
    n_seq, n_ch = mesh.shape["seq"], mesh.shape["ch"]

    def body(hidden_in, w_in, short_taps, rates, residues, skip_gain, w_out):
        depth, length = hidden_in.shape
        rows = w_in.shape[1]
        per = rows // n_ch
        cs = per // 3
        st = cs * rates.shape[1]
        half = length // 2
        nk = length // CL
        bits = n_seq.bit_length() - 1
        vmem = pl.BlockSpec(memory_space=pltpu.VMEM)
        dma = pltpu.SemaphoreType.DMA
        gathered = pl.pallas_call(
            functools.partial(conv_kernel, n_seq, n_ch),
            out_shape=jax.ShapeDtypeStruct((n_ch, cs, length), bf16),
            in_specs=[pl.BlockSpec(memory_space=pltpu.HBM)] * 6,
            out_specs=vmem,
            scratch_shapes=[
                pltpu.VMEM(w_in.shape, bf16),
                pltpu.VMEM(short_taps.shape, f32),
                pltpu.VMEM(rates.shape, f32),
                pltpu.VMEM(residues.shape, f32),
                pltpu.VMEM((1, cs), f32),
                pltpu.VMEM((depth, length), bf16),
                pltpu.VMEM((nk, n_ch, per, CL), f32),
                pltpu.VMEM((2, 7, 2 * cs, half), bf16),
                pltpu.VMEM((2, 7, 2 * cs, half), bf16),
                pltpu.VMEM((2, 7, cs, half), bf16),
                pltpu.VMEM((2, 7, cs, half), bf16),
                pltpu.VMEM((per, length), f32),
                pltpu.VMEM((per, CL), bf16),
                pltpu.VMEM((per, CL), bf16),
                pltpu.VMEM((n_ch, cs, length), bf16),
                pltpu.VMEM((1, st), f32),
                pltpu.VMEM((n_seq, 1, st), f32),
                pltpu.VMEM((n_seq, 1, st), f32),
                pltpu.VMEM((1, st), f32),
                pltpu.VMEM((9, cs, CL), f32),
                pltpu.VMEM((2 * CL, st), bf16),
                pltpu.VMEM((CL, 3 * st), bf16),
                pltpu.VMEM((cs, 2 * CL, CL), bf16),
                pltpu.VMEM((nk * cs, CL), f32),
                pltpu.VMEM((nk * cs, CL), f32),
                pltpu.VMEM((nk * cs, st), f32),
                dma((4,)),
                dma((5,)),
                dma((4,)),
                dma((2, 3)),
                dma((2, 3)),
                dma((2,)),
                dma((bits,)),
                dma((bits,)),
                pltpu.SemaphoreType.REGULAR,
                dma((5,)),
            ],
            compiler_params=pltpu.CompilerParams(
                collective_id=0, has_side_effects=True, vmem_limit_bytes=40 * 1024 * 1024
            ),
        )(
            *(
                pltpu.with_memory_space_constraint(x, pltpu.HBM)
                for x in (hidden_in, w_in, short_taps, rates, residues, skip_gain.reshape(1, cs))
            )
        )
        slab = n_ch * cs
        return pl.pallas_call(
            project_kernel,
            out_shape=jax.ShapeDtypeStruct((w_out.shape[0], length), bf16),
            in_specs=[vmem] * 2,
            out_specs=pl.BlockSpec(memory_space=pl.ANY),
            scratch_shapes=[pltpu.VMEM((w_out.shape[0], length), bf16), dma((8,))],
            compiler_params=pltpu.CompilerParams(vmem_limit_bytes=16 * 1024 * 1024),
        )(w_out, gathered.reshape(slab, length))

    in_specs = (
        P("ch", "seq"),
        P("ch", None),
        P(None, "ch"),
        P("ch", None),
        P("ch", None),
        P("ch"),
        P("ch", None),
    )
    return jax.shard_map(
        body, mesh=mesh, in_specs=in_specs, out_specs=P("ch", "seq"), check_vma=False
    )
```

```python
import functools

import jax
import jax.numpy as jnp
from jax import lax
from jax.experimental import pallas as pl
from jax.experimental.pallas import tpu as pltpu
from jax.sharding import PartitionSpec as P

MESH = pl.DeviceIdType.MESH
f32 = jnp.float32
bf16 = jnp.bfloat16
HIGH = lax.Precision.HIGHEST
NT = (((1,), (1,)), ((), ()))
NN = (((1,), (0,)), ((), ()))
TN = (((0,), (0,)), ((), ()))
CL = 128


def mm(a, b, dims=NN, precision=None):
    return lax.dot_general(a, b, dims, precision=precision, preferred_element_type=f32)


def halves(x):
    hi = x.astype(bf16)
    return hi, (x - hi.astype(f32)).astype(bf16)


def iota(shape, dim):
    return lax.broadcasted_iota(jnp.int32, shape, dim)


def conv_kernel(
    n_seq,
    n_ch,
    hid,
    w_in,
    taps_in,
    rates_in,
    res_in,
    skip_in,
    out_ref,
    w_ref,
    taps_ref,
    rates_ref,
    res_ref,
    skip_ref,
    hidv,
    part,
    kv_s,
    kv_r,
    q_s,
    q_r,
    tot,
    halo_s,
    halo_r,
    gath,
    st0,
    st1,
    weight,
    into,
    par,
    e_hl,
    p_hl,
    tcat,
    dscr,
    yscr,
    xscr,
    load_sem,
    small_sem,
    sent,
    kv_rs,
    q_rs,
    halo_rs,
    st_ss,
    st_rs,
    ready,
    ag_rs,
):
    p = lax.axis_index("seq")
    z = lax.axis_index("ch")
    depth, length = hid.shape
    rows = w_ref.shape[1]
    per = rows // n_ch
    cs = per // 3
    nm = rates_ref.shape[1]
    st = cs * nm
    half = length // 2
    nk = length // CL
    quarter = length // 4

    def zz(k):
        return lax.rem(z + (k + n_ch), n_ch)

    ring = (zz(1), zz(-1))
    ring2 = (zz(2), zz(-2))
    pending = {}

    smalls = []
    pairs = ((w_in, w_ref), (rates_in, rates_ref), (res_in, res_ref), (taps_in, taps_ref), (skip_in, skip_ref))
    for i, (src, dst) in enumerate(pairs):
        cp = pltpu.make_async_copy(src, dst, small_sem.at[i])
        smalls.append(cp)
    smalls[0].start()
    loads = []
    for i in (3, 2, 1, 0):
        cp = pltpu.make_async_copy(
            hid.at[:, pl.ds(i * quarter, quarter)],
            hidv.at[:, pl.ds(i * quarter, quarter)],
            load_sem.at[i],
        )
        cp.start()
        loads.append((i, cp))
    for cp in smalls[1:]:
        cp.start()

    def hops(k):
        return (0, 1, 2, 1)[k >> 1 & 3] + (0, 1, 2, 1)[k >> 3]

    bits = n_seq.bit_length() - 1
    groups = [sorted(range(1 << b, 2 << b), key=lambda k: -hops(k)) for b in range(bits)]

    def to_later(b):
        return pl.when((p >> b) & 1 == 0)

    def to_earlier(b):
        return pl.when((p >> b) & 1 == 1)

    after = lax.rem(p + 1, n_seq)
    barrier = pltpu.get_barrier_semaphore()
    for s in [zz(k) for k in (1, 2, 3, 5, 6, 7)]:
        pl.semaphore_signal(barrier, inc=1, device_id=(p, s), device_id_type=MESH)
    for b in reversed(range(bits)):

        @to_later(b)
        def _():
            for k in groups[b]:
                pl.semaphore_signal(barrier, inc=1, device_id=(p ^ k, z), device_id_type=MESH)

    smalls[0].wait()

    def remote(key, src, dst, ssem, rsem, dev):
        pltpu.make_async_remote_copy(
            src_ref=src,
            dst_ref=dst,
            send_sem=ssem,
            recv_sem=rsem,
            device_id=dev,
            device_id_type=MESH,
        ).start()
        pending[key] = (dst, rsem)

    def waiter(ref, sem):
        return pltpu.make_async_remote_copy(
            src_ref=ref,
            dst_ref=ref,
            send_sem=sem,
            recv_sem=sem,
            device_id=(p, ring[0]),
            device_id_type=MESH,
        )

    def arrived(keys, ref, sem):
        for key in keys:
            pending.pop(key)
        waiter(ref, sem).wait_recv()

    bufs = {
        "kv": (kv_s, kv_r, sent.at[0], kv_rs, 0, 2 * cs),
        "q": (q_s, q_r, sent.at[1], q_rs, 2 * cs, cs),
    }
    toks = (pl.ds(0, half), pl.ds(half, half))

    def rows_of(kind, dest, h):
        comps = (1, 2) if kind == "kv" else (0,)
        picked = []
        for j in comps:
            pieces = [
                part[k, dest, pl.ds(j, cs, stride=3), :]
                for k in range(h * nk // 2, (h + 1) * nk // 2)
            ]
            picked.append(jnp.concatenate(pieces, axis=1))
        return jnp.concatenate(picked, axis=0)

    def own(kind, h, d, dist):
        return rows_of(kind, zz(dist if d == 0 else -dist), h)

    def long_way(h):
        return 0 if h == 1 else 1

    def send(kind, h, d, m, value):
        sbuf, rbuf, ss, rs = bufs[kind][:4]
        slot = (0, 1, 3, 5)[m] if d == long_way(h) else (None, 2, 4, 6)[m]
        sbuf[h, slot] = value.astype(bf16)
        to = (ring2, ring)[m % 2][d]
        got = rs.at[h, (0, 0, 1, 2, 2, 2, 2)[slot]]
        remote((kind, h, slot), sbuf.at[h, slot], rbuf.at[h, slot], ss, got, (p, to))

    def take(kind, h, group, first, count):
        _, rbuf, _, rs = bufs[kind][:4]
        keys = [(kind, h, first + i) for i in range(count)]
        arrived(keys, rbuf.at[h, pl.ds(first, count)], rs.at[h, group])
        return [rbuf[h, first + i].astype(f32) for i in range(count)]

    def far(kind, h):
        send(kind, h, long_way(h), 0, own(kind, h, long_way(h), 4))
        for d in (0, 1):
            send(kind, h, d, 1, own(kind, h, d, 3))

    def near(kind, h):
        for d in (0, 1):
            send(kind, h, d, 3, own(kind, h, d, 1))

    def merge_short(kind, h):
        d = 1 - long_way(h)
        (got,) = take(kind, h, 1, 2, 1)
        send(kind, h, d, 2, own(kind, h, d, 2) + got)

    def merge_long(kind, h):
        d = long_way(h)
        four, three = take(kind, h, 0, 0, 2)
        send(kind, h, d, 2, own(kind, h, d, 2) + three + four)

    def total_of(kind, h):
        row0, n = bufs[kind][4:]
        value = rows_of(kind, z, h)
        for got in take(kind, h, 2, 3, 4):
            value = value + got
        tot[row0 : row0 + n, toks[h]] = value

    for n, (i, cp) in enumerate(loads):
        cp.wait()
        tok = pl.ds(i * quarter, quarter)
        sums = mm(w_ref[...], hidv[:, tok], TN)
        for k in range(quarter // CL):
            piece = sums[:, CL * k : CL * (k + 1)].reshape(n_ch, per, CL)
            part[i * quarter // CL + k] = piece
        if n == 1:
            pl.semaphore_wait(barrier, 6 + p)
            far("kv", 1)
        if n == 3:
            far("kv", 0)
            far("q", 1)
            far("q", 0)
    for b in reversed(range(bits)):

        @to_earlier(b)
        def _():
            for k in groups[b]:
                pl.semaphore_signal(ready, inc=1, device_id=(p ^ k, z), device_id_type=MESH)

    @pl.when(p == 0)
    def _():
        halo_r[...] = jnp.zeros_like(halo_r)

    lane_st = iota((cs, st), 1)
    mine = (lane_st >> 4) == iota((cs, st), 0)
    rep = jnp.where((iota((nm, st), 1) & (nm - 1)) == iota((nm, st), 0), 1.0, 0.0)

    def as_row(x):
        return jnp.sum(jnp.where(mine, mm(x, rep, precision=HIGH), 0.0), axis=0, keepdims=True)

    for cp in smalls[1:]:
        cp.wait()
    lam = as_row(rates_ref[...])
    gain = as_row(res_ref[...] * jnp.sqrt(rates_ref[...]))
    steps = iota((CL, st), 0).astype(f32)
    e_hi, e_lo = halves(jnp.exp(-lam * (CL - 1 - steps)))
    e_hl[0:CL] = e_hi
    e_hl[CL : 2 * CL] = e_lo
    p_hi, p_lo = halves(gain * jnp.exp(-lam * (steps + 1.0)))
    p_hl[:, 0:st] = p_hi
    p_hl[:, st : 2 * st] = p_hi
    p_hl[:, 2 * st : 3 * st] = p_lo

    for h in (1, 0):
        merge_short("kv", h)
    for h in (1, 0):
        merge_long("kv", h)
    for h in (1, 0):
        near("kv", h)

    spread = jnp.where(mine, gain, 0.0)
    taps0 = mm(spread, jnp.exp(-lam * steps), NT, HIGH)
    causal = iota((CL, CL), 1) >= iota((CL, CL), 0)

    def lay_out(c0, c1):
        for c in range(c0, c1):
            line = jnp.broadcast_to(taps0[c : c + 1, :], (CL, CL))
            tri = jnp.where(causal, pltpu.roll(line, 0, 1, stride=1, stride_axis=0), 0.0)
            hi, lo = halves(tri)
            tcat[c, 0:CL] = hi
            tcat[c, CL : 2 * CL] = lo

    lay_out(0, 8)
    lane_per = iota((cs, per), 1)
    row_per = iota((cs, per), 0)
    for i in range(3):
        line = jnp.broadcast_to(taps_ref[i : i + 1, :], (cs, per))
        for j in range(3):
            picked = jnp.where(lane_per == 3 * row_per + j, line, 0.0)
            par[3 * i + j] = jnp.broadcast_to(jnp.sum(picked, axis=1, keepdims=True), (cs, CL))
    skip_line = jnp.broadcast_to(skip_ref[...], (cs, cs))
    skip_col = jnp.sum(
        jnp.where(iota((cs, cs), 0) == iota((cs, cs), 1), skip_line, 0.0), axis=1, keepdims=True
    )

    for h in (1, 0):
        merge_short("q", h)
    for h in (1, 0):
        merge_long("q", h)
    for h in (1, 0):
        near("q", h)
    lay_out(8, 16)
    decay_k = [jnp.exp(-lam * float(CL * k)) for k in range(nk)]
    block = lam * float(length)
    for k in range(1, n_seq):
        apart = jnp.maximum(p - 1 - (p ^ k), 0)
        weight[k] = jnp.exp(-block * apart.astype(f32))
    total_of("kv", 1)

    def tail(i, row0, n):
        halo_s[row0 : row0 + n] = tot[row0 : row0 + n, length - CL : length].astype(bf16)
        at = pl.ds(row0, n)

        @pl.when(p < n_seq - 1)
        def _():
            remote(
                ("halo", i), halo_s.at[at], halo_r.at[at], sent.at[2], halo_rs.at[i], (after, z)
            )

    def tail_in(i, row0, n):
        @pl.when(p > 0)
        def _():
            arrived([("halo", i)], halo_r.at[pl.ds(row0, n)], halo_rs.at[i])

    @pl.when(p < n_seq - 1)
    def _():
        pl.semaphore_wait(ready, n_seq - 1 - p)

    tail(0, 0, 2 * cs)
    total_of("kv", 0)

    def short(row0, j):
        edge = halo_r[row0 : row0 + cs].astype(f32)
        x = tot[row0 : row0 + cs]
        ext = jnp.concatenate([edge, x], axis=1)
        one = pltpu.roll(ext, 1, 1)[:, CL:]
        two = pltpu.roll(ext, 2, 1)[:, CL:]
        t = [par[3 * i + j][:, 0:1] for i in range(3)]
        return t[0] * x + t[1] * one + t[2] * two

    tail_in(0, 0, 2 * cs)
    driven = (short(0, 1) * short(cs, 2)).astype(bf16)
    stacked = jnp.concatenate([driven[:, CL * k : CL * (k + 1)] for k in range(nk)], axis=0)
    dscr[...] = stacked.astype(f32)
    states = mm(jnp.concatenate([stacked, stacked], axis=1), e_hl[...])
    carry = jnp.zeros((cs, st), f32)
    for k in range(nk):
        xscr[cs * k : cs * (k + 1)] = carry
        carry = decay_k[1] * carry + jnp.where(mine, states[cs * k : cs * (k + 1)], 0.0)
    total = jnp.sum(carry, axis=0, keepdims=True)
    st0[...] = total
    for b in reversed(range(bits)):

        @to_later(b)
        def _():
            for k in groups[b]:
                remote(("st", k), st0, st1.at[k], st_ss.at[b], st_rs.at[b], (p ^ k, z))

    total_of("q", 1)
    tail(1, 2 * cs, cs)
    total_of("q", 0)
    for c in range(cs):
        line = dscr[pl.ds(c, nk, stride=cs), :].astype(bf16)
        yscr[pl.ds(c, nk, stride=cs), :] = mm(jnp.concatenate([line, line], axis=1), tcat[c])

    tail_in(1, 2 * cs, cs)
    query = short(2 * cs, 0)
    into[...] = jnp.zeros_like(into)
    for b in reversed(range(bits)):

        @to_earlier(b)
        def _():
            group = pl.ds(1 << b, 1 << b)
            arrived([("st", k) for k in groups[b]], st1.at[group], st_rs.at[b])
            into[...] += jnp.sum(weight[group] * st1[group], axis=0)

    wide = jnp.where(mine, into[...], 0.0)
    x = jnp.concatenate(
        [xscr[cs * k : cs * (k + 1)] + decay_k[k] * wide for k in range(nk)], axis=0
    )
    x_hi, x_lo = halves(x)
    y = yscr[...] + mm(jnp.concatenate([x_hi, x_lo, x_hi], axis=1), p_hl[...], NT)
    for k in range(nk):
        sl = slice(cs * k, cs * (k + 1))
        tok = slice(CL * k, CL * (k + 1))
        value = query[:, tok] * (y[sl] + skip_col * dscr[sl])
        gath[z, :, tok] = value.astype(bf16)

    def piece(move, d, dist):
        tok = slice(None) if move[2] is None else toks[move[2] if d == 0 else 1 - move[2]]
        return gath.at[zz(-dist if d == 0 else dist), :, tok]

    def hand(move, d, sem):
        ref = piece(move, d, move[0])
        target = (p, zz(move[1] if d == 0 else -move[1]))
        remote(("ag", move, d), ref, ref, sent.at[3], ag_rs.at[sem], target)

    def handed(moves, d, sem, ref):
        arrived([("ag", move, way) for move in moves for way in d], ref, ag_rs.at[sem])

    def straight():
        plan = ((0, 3, 0), (0, 1, None), (0, 2, None), (0, 3, 1))
        last = (3, 1, 0)
        for i, move in enumerate(plan):
            for d in (0, 1):
                hand(move, d, d if i == 0 else 4)
        for d in (0, 1):
            handed([plan[0]], (d,), d, piece(plan[0], d, 3))
            hand(last, d, 4)
        handed(plan[1:] + (last,), (0, 1), 4, gath.at[pl.ds(0, n_ch - 2)])

    def relayed():
        plan = ((0, 2, 0), (0, 2, 1), (0, 1, None), (2, 2, 0), (2, 1, 0), (2, 1, 1))
        for i, move in enumerate(plan[:3]):
            for d in (0, 1):
                hand(move, d, 2 * i + d if i < 2 else 4)
        for i in (0, 1):
            for d in (0, 1):
                handed([plan[i]], (d,), 2 * i + d, piece(plan[i], d, 2))
                if i == 0:
                    hand(plan[3], d, 4)
                hand(plan[4 + i], d, 4)
        handed(plan[2:], (0, 1), 4, gath.at[pl.ds(0, n_ch - 3)])

    pl.when(p % 2 == 0)(straight)
    pl.when(p % 2 == 1)(relayed)
    out_ref[...] = gath[...]
    assert not pending
    for i, ref in ((0, kv_s), (1, q_s), (3, gath.at[pl.ds(0, n_ch - 1)])):
        waiter(ref, sent.at[i]).wait_send()

    @pl.when(p < n_seq - 1)
    def _():
        waiter(halo_s, sent.at[2]).wait_send()

    for b in range(bits):

        @to_later(b)
        def _():
            waiter(st1.at[pl.ds(1 << b, 1 << b)], st_ss.at[b]).wait_send()


def project_kernel(w_ref, x_ref, out, rows_ref, sem):
    count = sem.shape[0]
    tile = out.shape[0] // count
    copies = []
    for i in range(count):
        at = pl.ds(i * tile, tile)
        rows_ref[at] = mm(w_ref[at], x_ref[...]).astype(bf16)
        cp = pltpu.make_async_copy(rows_ref.at[at], out.at[at], sem.at[i])
        cp.start()
        copies.append(cp)
    for cp in copies:
        cp.wait()


def solution(mesh):
    n_seq, n_ch = mesh.shape["seq"], mesh.shape["ch"]

    def body(hidden_in, w_in, short_taps, rates, residues, skip_gain, w_out):
        depth, length = hidden_in.shape
        rows = w_in.shape[1]
        per = rows // n_ch
        cs = per // 3
        st = cs * rates.shape[1]
        half = length // 2
        nk = length // CL
        bits = n_seq.bit_length() - 1
        vmem = pl.BlockSpec(memory_space=pltpu.VMEM)
        dma = pltpu.SemaphoreType.DMA
        gathered = pl.pallas_call(
            functools.partial(conv_kernel, n_seq, n_ch),
            out_shape=jax.ShapeDtypeStruct((n_ch, cs, length), bf16),
            in_specs=[pl.BlockSpec(memory_space=pltpu.HBM)] * 6,
            out_specs=vmem,
            scratch_shapes=[
                pltpu.VMEM(w_in.shape, bf16),
                pltpu.VMEM(short_taps.shape, f32),
                pltpu.VMEM(rates.shape, f32),
                pltpu.VMEM(residues.shape, f32),
                pltpu.VMEM((1, cs), f32),
                pltpu.VMEM((depth, length), bf16),
                pltpu.VMEM((nk, n_ch, per, CL), f32),
                pltpu.VMEM((2, 7, 2 * cs, half), bf16),
                pltpu.VMEM((2, 7, 2 * cs, half), bf16),
                pltpu.VMEM((2, 7, cs, half), bf16),
                pltpu.VMEM((2, 7, cs, half), bf16),
                pltpu.VMEM((per, length), f32),
                pltpu.VMEM((per, CL), bf16),
                pltpu.VMEM((per, CL), bf16),
                pltpu.VMEM((n_ch, cs, length), bf16),
                pltpu.VMEM((1, st), f32),
                pltpu.VMEM((n_seq, 1, st), f32),
                pltpu.VMEM((n_seq, 1, st), f32),
                pltpu.VMEM((1, st), f32),
                pltpu.VMEM((9, cs, CL), f32),
                pltpu.VMEM((2 * CL, st), bf16),
                pltpu.VMEM((CL, 3 * st), bf16),
                pltpu.VMEM((cs, 2 * CL, CL), bf16),
                pltpu.VMEM((nk * cs, CL), f32),
                pltpu.VMEM((nk * cs, CL), f32),
                pltpu.VMEM((nk * cs, st), f32),
                dma((4,)),
                dma((5,)),
                dma((4,)),
                dma((2, 3)),
                dma((2, 3)),
                dma((2,)),
                dma((bits,)),
                dma((bits,)),
                pltpu.SemaphoreType.REGULAR,
                dma((5,)),
            ],
            compiler_params=pltpu.CompilerParams(
                collective_id=0, has_side_effects=True, vmem_limit_bytes=40 * 1024 * 1024
            ),
        )(
            *(
                pltpu.with_memory_space_constraint(x, pltpu.HBM)
                for x in (hidden_in, w_in, short_taps, rates, residues, skip_gain.reshape(1, cs))
            )
        )
        slab = n_ch * cs
        return pl.pallas_call(
            project_kernel,
            out_shape=jax.ShapeDtypeStruct((w_out.shape[0], length), bf16),
            in_specs=[vmem] * 2,
            out_specs=pl.BlockSpec(memory_space=pl.ANY),
            scratch_shapes=[pltpu.VMEM((w_out.shape[0], length), bf16), dma((8,))],
            compiler_params=pltpu.CompilerParams(vmem_limit_bytes=16 * 1024 * 1024),
        )(w_out, gathered.reshape(slab, length))

    in_specs = (
        P("ch", "seq"),
        P("ch", None),
        P(None, "ch"),
        P("ch", None),
        P("ch", None),
        P("ch"),
        P("ch", None),
    )
    return jax.shard_map(
        body, mesh=mesh, in_specs=in_specs, out_specs=P("ch", "seq"), check_vma=False
    )
```

```python
import functools

import jax
import jax.numpy as jnp
from jax import lax
from jax.experimental import pallas as pl
from jax.experimental.pallas import tpu as pltpu
from jax.sharding import PartitionSpec as P

MESH = pl.DeviceIdType.MESH
f32 = jnp.float32
bf16 = jnp.bfloat16
HIGH = lax.Precision.HIGHEST
NT = (((1,), (1,)), ((), ()))
NN = (((1,), (0,)), ((), ()))
TN = (((0,), (0,)), ((), ()))
CL = 128


def mm(a, b, dims=NN, precision=None):
    return lax.dot_general(a, b, dims, precision=precision, preferred_element_type=f32)


def halves(x):
    hi = x.astype(bf16)
    return hi, (x - hi.astype(f32)).astype(bf16)


def iota(shape, dim):
    return lax.broadcasted_iota(jnp.int32, shape, dim)


def conv_kernel(
    n_seq,
    n_ch,
    hid,
    w_in,
    taps_in,
    rates_in,
    res_in,
    skip_in,
    out_ref,
    w_ref,
    taps_ref,
    rates_ref,
    res_ref,
    skip_ref,
    hidv,
    part,
    kv_s,
    kv_r,
    q_s,
    q_r,
    tot,
    halo_s,
    halo_r,
    gath,
    st0,
    st1,
    weight,
    into,
    par,
    e_hl,
    p_hl,
    tcat,
    dscr,
    yscr,
    xscr,
    load_sem,
    small_sem,
    sent,
    kv_rs,
    q_rs,
    halo_rs,
    st_ss,
    st_rs,
    ready,
    ag_rs,
):
    p = lax.axis_index("seq")
    z = lax.axis_index("ch")
    depth, length = hid.shape
    rows = w_ref.shape[1]
    per = rows // n_ch
    cs = per // 3
    nm = rates_ref.shape[1]
    st = cs * nm
    half = length // 2
    nk = length // CL
    quarter = length // 4

    def zz(k):
        return lax.rem(z + (k + n_ch), n_ch)

    ring = (zz(1), zz(-1))
    ring2 = (zz(2), zz(-2))
    pending = {}

    smalls = []
    pairs = ((w_in, w_ref), (rates_in, rates_ref), (res_in, res_ref), (taps_in, taps_ref), (skip_in, skip_ref))
    for i, (src, dst) in enumerate(pairs):
        cp = pltpu.make_async_copy(src, dst, small_sem.at[i])
        smalls.append(cp)
    smalls[0].start()
    loads = []
    for i in (3, 2, 1, 0):
        cp = pltpu.make_async_copy(
            hid.at[:, pl.ds(i * quarter, quarter)],
            hidv.at[:, pl.ds(i * quarter, quarter)],
            load_sem.at[i],
        )
        cp.start()
        loads.append((i, cp))
    for cp in smalls[1:]:
        cp.start()

    def hops(k):
        return (0, 1, 2, 1)[k >> 1 & 3] + (0, 1, 2, 1)[k >> 3]

    bits = n_seq.bit_length() - 1
    groups = [sorted(range(1 << b, 2 << b), key=lambda k: -hops(k)) for b in range(bits)]

    def to_later(b):
        return pl.when((p >> b) & 1 == 0)

    def to_earlier(b):
        return pl.when((p >> b) & 1 == 1)

    after = lax.rem(p + 1, n_seq)
    barrier = pltpu.get_barrier_semaphore()
    for s in [zz(k) for k in (1, 2, 3, 5, 6, 7)]:
        pl.semaphore_signal(barrier, inc=1, device_id=(p, s), device_id_type=MESH)
    for b in reversed(range(bits)):

        @to_later(b)
        def _():
            for k in groups[b]:
                pl.semaphore_signal(barrier, inc=1, device_id=(p ^ k, z), device_id_type=MESH)

    smalls[0].wait()

    def remote(key, src, dst, ssem, rsem, dev):
        pltpu.make_async_remote_copy(
            src_ref=src,
            dst_ref=dst,
            send_sem=ssem,
            recv_sem=rsem,
            device_id=dev,
            device_id_type=MESH,
        ).start()
        pending[key] = (dst, rsem)

    def waiter(ref, sem):
        return pltpu.make_async_remote_copy(
            src_ref=ref,
            dst_ref=ref,
            send_sem=sem,
            recv_sem=sem,
            device_id=(p, ring[0]),
            device_id_type=MESH,
        )

    def arrived(keys, ref, sem):
        for key in keys:
            pending.pop(key)
        waiter(ref, sem).wait_recv()

    bufs = {
        "kv": (kv_s, kv_r, sent.at[0], kv_rs, 0, 2 * cs),
        "q": (q_s, q_r, sent.at[1], q_rs, 2 * cs, cs),
    }
    toks = (pl.ds(0, half), pl.ds(half, half))

    def rows_of(kind, dest, h):
        comps = (1, 2) if kind == "kv" else (0,)
        picked = []
        for j in comps:
            pieces = [
                part[k, dest, pl.ds(j, cs, stride=3), :]
                for k in range(h * nk // 2, (h + 1) * nk // 2)
            ]
            picked.append(jnp.concatenate(pieces, axis=1))
        return jnp.concatenate(picked, axis=0)

    def own(kind, h, d, dist):
        return rows_of(kind, zz(dist if d == 0 else -dist), h)

    def long_way(h):
        return 0 if h == 1 else 1

    def send(kind, h, d, m, value):
        sbuf, rbuf, ss, rs = bufs[kind][:4]
        slot = (0, 1, 3, 5)[m] if d == long_way(h) else (None, 2, 4, 6)[m]
        sbuf[h, slot] = value.astype(bf16)
        to = (ring2, ring)[m % 2][d]
        got = rs.at[h, (0, 0, 1, 2, 2, 2, 2)[slot]]
        remote((kind, h, slot), sbuf.at[h, slot], rbuf.at[h, slot], ss, got, (p, to))

    def take(kind, h, group, first, count):
        _, rbuf, _, rs = bufs[kind][:4]
        keys = [(kind, h, first + i) for i in range(count)]
        arrived(keys, rbuf.at[h, pl.ds(first, count)], rs.at[h, group])
        return [rbuf[h, first + i].astype(f32) for i in range(count)]

    def far(kind, h):
        send(kind, h, long_way(h), 0, own(kind, h, long_way(h), 4))
        for d in (0, 1):
            send(kind, h, d, 1, own(kind, h, d, 3))

    def near(kind, h):
        for d in (0, 1):
            send(kind, h, d, 3, own(kind, h, d, 1))

    def merge_short(kind, h):
        d = 1 - long_way(h)
        (got,) = take(kind, h, 1, 2, 1)
        send(kind, h, d, 2, own(kind, h, d, 2) + got)

    def merge_long(kind, h):
        d = long_way(h)
        four, three = take(kind, h, 0, 0, 2)
        send(kind, h, d, 2, own(kind, h, d, 2) + three + four)

    def total_of(kind, h):
        row0, n = bufs[kind][4:]
        value = rows_of(kind, z, h)
        for got in take(kind, h, 2, 3, 4):
            value = value + got
        tot[row0 : row0 + n, toks[h]] = value

    for n, (i, cp) in enumerate(loads):
        cp.wait()
        tok = pl.ds(i * quarter, quarter)
        sums = mm(w_ref[...], hidv[:, tok], TN)
        for k in range(quarter // CL):
            piece = sums[:, CL * k : CL * (k + 1)].reshape(n_ch, per, CL)
            part[i * quarter // CL + k] = piece
        if n == 1:
            pl.semaphore_wait(barrier, 6 + p)
            far("kv", 1)
        if n == 3:
            far("kv", 0)
            far("q", 1)
            far("q", 0)
    for b in reversed(range(bits)):

        @to_earlier(b)
        def _():
            for k in groups[b]:
                pl.semaphore_signal(ready, inc=1, device_id=(p ^ k, z), device_id_type=MESH)

    @pl.when(p == 0)
    def _():
        halo_r[...] = jnp.zeros_like(halo_r)

    lane_st = iota((cs, st), 1)
    mine = (lane_st >> 4) == iota((cs, st), 0)
    rep = jnp.where((iota((nm, st), 1) & (nm - 1)) == iota((nm, st), 0), 1.0, 0.0)

    def as_row(x):
        return jnp.sum(jnp.where(mine, mm(x, rep, precision=HIGH), 0.0), axis=0, keepdims=True)

    for cp in smalls[1:]:
        cp.wait()
    lam = as_row(rates_ref[...])
    gain = as_row(res_ref[...] * jnp.sqrt(rates_ref[...]))
    steps = iota((CL, st), 0).astype(f32)
    e_hi, e_lo = halves(jnp.exp(-lam * (CL - 1 - steps)))
    e_hl[0:CL] = e_hi
    e_hl[CL : 2 * CL] = e_lo
    p_hi, p_lo = halves(gain * jnp.exp(-lam * (steps + 1.0)))
    p_hl[:, 0:st] = p_hi
    p_hl[:, st : 2 * st] = p_hi
    p_hl[:, 2 * st : 3 * st] = p_lo

    for h in (1, 0):
        merge_short("kv", h)
    for h in (1, 0):
        merge_long("kv", h)
    for h in (1, 0):
        near("kv", h)

    spread = jnp.where(mine, gain, 0.0)
    taps0 = mm(spread, jnp.exp(-lam * steps), NT, HIGH)
    causal = iota((CL, CL), 1) >= iota((CL, CL), 0)

    def lay_out(c0, c1):
        for c in range(c0, c1):
            line = jnp.broadcast_to(taps0[c : c + 1, :], (CL, CL))
            tri = jnp.where(causal, pltpu.roll(line, 0, 1, stride=1, stride_axis=0), 0.0)
            hi, lo = halves(tri)
            tcat[c, 0:CL] = hi
            tcat[c, CL : 2 * CL] = lo

    lay_out(0, 8)
    lane_per = iota((cs, per), 1)
    row_per = iota((cs, per), 0)
    for i in range(3):
        line = jnp.broadcast_to(taps_ref[i : i + 1, :], (cs, per))
        for j in range(3):
            picked = jnp.where(lane_per == 3 * row_per + j, line, 0.0)
            par[3 * i + j] = jnp.broadcast_to(jnp.sum(picked, axis=1, keepdims=True), (cs, CL))
    skip_line = jnp.broadcast_to(skip_ref[...], (cs, cs))
    skip_col = jnp.sum(
        jnp.where(iota((cs, cs), 0) == iota((cs, cs), 1), skip_line, 0.0), axis=1, keepdims=True
    )

    for h in (1, 0):
        near("q", h)
    for h in (1, 0):
        merge_short("q", h)
    for h in (1, 0):
        merge_long("q", h)
    lay_out(8, 16)
    decay_k = [jnp.exp(-lam * float(CL * k)) for k in range(nk)]
    block = lam * float(length)
    for k in range(1, n_seq):
        apart = jnp.maximum(p - 1 - (p ^ k), 0)
        weight[k] = jnp.exp(-block * apart.astype(f32))
    total_of("kv", 1)

    def tail(i, row0, n):
        halo_s[row0 : row0 + n] = tot[row0 : row0 + n, length - CL : length].astype(bf16)
        at = pl.ds(row0, n)

        @pl.when(p < n_seq - 1)
        def _():
            remote(
                ("halo", i), halo_s.at[at], halo_r.at[at], sent.at[2], halo_rs.at[i], (after, z)
            )

    def tail_in(i, row0, n):
        @pl.when(p > 0)
        def _():
            arrived([("halo", i)], halo_r.at[pl.ds(row0, n)], halo_rs.at[i])

    @pl.when(p < n_seq - 1)
    def _():
        pl.semaphore_wait(ready, n_seq - 1 - p)

    tail(0, 0, 2 * cs)
    total_of("kv", 0)

    def short(row0, j):
        edge = halo_r[row0 : row0 + cs].astype(f32)
        x = tot[row0 : row0 + cs]
        ext = jnp.concatenate([edge, x], axis=1)
        one = pltpu.roll(ext, 1, 1)[:, CL:]
        two = pltpu.roll(ext, 2, 1)[:, CL:]
        t = [par[3 * i + j][:, 0:1] for i in range(3)]
        return t[0] * x + t[1] * one + t[2] * two

    tail_in(0, 0, 2 * cs)
    driven = (short(0, 1) * short(cs, 2)).astype(bf16)
    stacked = jnp.concatenate([driven[:, CL * k : CL * (k + 1)] for k in range(nk)], axis=0)
    dscr[...] = stacked.astype(f32)
    states = mm(jnp.concatenate([stacked, stacked], axis=1), e_hl[...])
    carry = jnp.zeros((cs, st), f32)
    for k in range(nk):
        xscr[cs * k : cs * (k + 1)] = carry
        carry = decay_k[1] * carry + jnp.where(mine, states[cs * k : cs * (k + 1)], 0.0)
    total = jnp.sum(carry, axis=0, keepdims=True)
    st0[...] = total
    for b in reversed(range(bits)):

        @to_later(b)
        def _():
            for k in groups[b]:
                remote(("st", k), st0, st1.at[k], st_ss.at[b], st_rs.at[b], (p ^ k, z))

    total_of("q", 1)
    tail(1, 2 * cs, cs)
    total_of("q", 0)
    for c in range(cs):
        line = dscr[pl.ds(c, nk, stride=cs), :].astype(bf16)
        yscr[pl.ds(c, nk, stride=cs), :] = mm(jnp.concatenate([line, line], axis=1), tcat[c])

    tail_in(1, 2 * cs, cs)
    query = short(2 * cs, 0)
    into[...] = jnp.zeros_like(into)
    for b in reversed(range(bits)):

        @to_earlier(b)
        def _():
            group = pl.ds(1 << b, 1 << b)
            arrived([("st", k) for k in groups[b]], st1.at[group], st_rs.at[b])
            into[...] += jnp.sum(weight[group] * st1[group], axis=0)

    wide = jnp.where(mine, into[...], 0.0)
    x = jnp.concatenate(
        [xscr[cs * k : cs * (k + 1)] + decay_k[k] * wide for k in range(nk)], axis=0
    )
    x_hi, x_lo = halves(x)
    y = yscr[...] + mm(jnp.concatenate([x_hi, x_lo, x_hi], axis=1), p_hl[...], NT)
    for k in range(nk):
        sl = slice(cs * k, cs * (k + 1))
        tok = slice(CL * k, CL * (k + 1))
        value = query[:, tok] * (y[sl] + skip_col * dscr[sl])
        gath[z, :, tok] = value.astype(bf16)

    def piece(move, d, dist):
        tok = slice(None) if move[2] is None else toks[move[2] if d == 0 else 1 - move[2]]
        return gath.at[zz(-dist if d == 0 else dist), :, tok]

    def hand(move, d, sem):
        ref = piece(move, d, move[0])
        target = (p, zz(move[1] if d == 0 else -move[1]))
        remote(("ag", move, d), ref, ref, sent.at[3], ag_rs.at[sem], target)

    def handed(moves, d, sem, ref):
        arrived([("ag", move, way) for move in moves for way in d], ref, ag_rs.at[sem])

    def straight():
        plan = ((0, 3, 0), (0, 1, None), (0, 2, None), (0, 3, 1))
        last = (3, 1, 0)
        for i, move in enumerate(plan):
            for d in (0, 1):
                hand(move, d, d if i == 0 else 4)
        for d in (0, 1):
            handed([plan[0]], (d,), d, piece(plan[0], d, 3))
            hand(last, d, 4)
        handed(plan[1:] + (last,), (0, 1), 4, gath.at[pl.ds(0, n_ch - 2)])

    def relayed():
        plan = ((0, 2, 0), (0, 2, 1), (0, 1, None), (2, 2, 0), (2, 1, 0), (2, 1, 1))
        for i, move in enumerate(plan[:3]):
            for d in (0, 1):
                hand(move, d, 2 * i + d if i < 2 else 4)
        for i in (0, 1):
            for d in (0, 1):
                handed([plan[i]], (d,), 2 * i + d, piece(plan[i], d, 2))
                if i == 0:
                    hand(plan[3], d, 4)
                hand(plan[4 + i], d, 4)
        handed(plan[2:], (0, 1), 4, gath.at[pl.ds(0, n_ch - 3)])

    pl.when(p % 2 == 0)(straight)
    pl.when(p % 2 == 1)(relayed)
    out_ref[...] = gath[...]
    assert not pending
    for i, ref in ((0, kv_s), (1, q_s), (3, gath.at[pl.ds(0, n_ch - 1)])):
        waiter(ref, sent.at[i]).wait_send()

    @pl.when(p < n_seq - 1)
    def _():
        waiter(halo_s, sent.at[2]).wait_send()

    for b in range(bits):

        @to_later(b)
        def _():
            waiter(st1.at[pl.ds(1 << b, 1 << b)], st_ss.at[b]).wait_send()


def project_kernel(w_ref, x_ref, out, rows_ref, sem):
    count = sem.shape[0]
    tile = out.shape[0] // count
    copies = []
    for i in range(count):
        at = pl.ds(i * tile, tile)
        rows_ref[at] = mm(w_ref[at], x_ref[...]).astype(bf16)
        cp = pltpu.make_async_copy(rows_ref.at[at], out.at[at], sem.at[i])
        cp.start()
        copies.append(cp)
    for cp in copies:
        cp.wait()


def solution(mesh):
    n_seq, n_ch = mesh.shape["seq"], mesh.shape["ch"]

    def body(hidden_in, w_in, short_taps, rates, residues, skip_gain, w_out):
        depth, length = hidden_in.shape
        rows = w_in.shape[1]
        per = rows // n_ch
        cs = per // 3
        st = cs * rates.shape[1]
        half = length // 2
        nk = length // CL
        bits = n_seq.bit_length() - 1
        vmem = pl.BlockSpec(memory_space=pltpu.VMEM)
        dma = pltpu.SemaphoreType.DMA
        gathered = pl.pallas_call(
            functools.partial(conv_kernel, n_seq, n_ch),
            out_shape=jax.ShapeDtypeStruct((n_ch, cs, length), bf16),
            in_specs=[pl.BlockSpec(memory_space=pltpu.HBM)] * 6,
            out_specs=vmem,
            scratch_shapes=[
                pltpu.VMEM(w_in.shape, bf16),
                pltpu.VMEM(short_taps.shape, f32),
                pltpu.VMEM(rates.shape, f32),
                pltpu.VMEM(residues.shape, f32),
                pltpu.VMEM((1, cs), f32),
                pltpu.VMEM((depth, length), bf16),
                pltpu.VMEM((nk, n_ch, per, CL), f32),
                pltpu.VMEM((2, 7, 2 * cs, half), bf16),
                pltpu.VMEM((2, 7, 2 * cs, half), bf16),
                pltpu.VMEM((2, 7, cs, half), bf16),
                pltpu.VMEM((2, 7, cs, half), bf16),
                pltpu.VMEM((per, length), f32),
                pltpu.VMEM((per, CL), bf16),
                pltpu.VMEM((per, CL), bf16),
                pltpu.VMEM((n_ch, cs, length), bf16),
                pltpu.VMEM((1, st), f32),
                pltpu.VMEM((n_seq, 1, st), f32),
                pltpu.VMEM((n_seq, 1, st), f32),
                pltpu.VMEM((1, st), f32),
                pltpu.VMEM((9, cs, CL), f32),
                pltpu.VMEM((2 * CL, st), bf16),
                pltpu.VMEM((CL, 3 * st), bf16),
                pltpu.VMEM((cs, 2 * CL, CL), bf16),
                pltpu.VMEM((nk * cs, CL), f32),
                pltpu.VMEM((nk * cs, CL), f32),
                pltpu.VMEM((nk * cs, st), f32),
                dma((4,)),
                dma((5,)),
                dma((4,)),
                dma((2, 3)),
                dma((2, 3)),
                dma((2,)),
                dma((bits,)),
                dma((bits,)),
                pltpu.SemaphoreType.REGULAR,
                dma((5,)),
            ],
            compiler_params=pltpu.CompilerParams(
                collective_id=0, has_side_effects=True, vmem_limit_bytes=40 * 1024 * 1024
            ),
        )(
            *(
                pltpu.with_memory_space_constraint(x, pltpu.HBM)
                for x in (hidden_in, w_in, short_taps, rates, residues, skip_gain.reshape(1, cs))
            )
        )
        slab = n_ch * cs
        return pl.pallas_call(
            project_kernel,
            out_shape=jax.ShapeDtypeStruct((w_out.shape[0], length), bf16),
            in_specs=[vmem] * 2,
            out_specs=pl.BlockSpec(memory_space=pl.ANY),
            scratch_shapes=[pltpu.VMEM((w_out.shape[0], length), bf16), dma((8,))],
            compiler_params=pltpu.CompilerParams(vmem_limit_bytes=16 * 1024 * 1024),
        )(w_out, gathered.reshape(slab, length))

    in_specs = (
        P("ch", "seq"),
        P("ch", None),
        P(None, "ch"),
        P("ch", None),
        P("ch", None),
        P("ch"),
        P("ch", None),
    )
    return jax.shard_map(
        body, mesh=mesh, in_specs=in_specs, out_specs=P("ch", "seq"), check_vma=False
    )
```

```python
import functools

import jax
import jax.numpy as jnp
from jax import lax
from jax.experimental import pallas as pl
from jax.experimental.pallas import tpu as pltpu
from jax.sharding import PartitionSpec as P

MESH = pl.DeviceIdType.MESH
f32 = jnp.float32
bf16 = jnp.bfloat16
HIGH = lax.Precision.HIGHEST
NT = (((1,), (1,)), ((), ()))
NN = (((1,), (0,)), ((), ()))
TN = (((0,), (0,)), ((), ()))
CL = 128


def mm(a, b, dims=NN, precision=None):
    return lax.dot_general(a, b, dims, precision=precision, preferred_element_type=f32)


def halves(x):
    hi = x.astype(bf16)
    return hi, (x - hi.astype(f32)).astype(bf16)


def iota(shape, dim):
    return lax.broadcasted_iota(jnp.int32, shape, dim)


def conv_kernel(
    n_seq,
    n_ch,
    hid,
    w_in,
    taps_in,
    rates_in,
    res_in,
    skip_in,
    out_ref,
    w_ref,
    taps_ref,
    rates_ref,
    res_ref,
    skip_ref,
    hidv,
    part,
    kv_s,
    kv_r,
    q_s,
    q_r,
    tot,
    halo_s,
    halo_r,
    gath,
    st0,
    st1,
    weight,
    into,
    par,
    e_hl,
    p_hl,
    tcat,
    dscr,
    yscr,
    xscr,
    load_sem,
    small_sem,
    sent,
    kv_rs,
    q_rs,
    halo_rs,
    st_ss,
    st_rs,
    ready,
    ag_rs,
):
    p = lax.axis_index("seq")
    z = lax.axis_index("ch")
    depth, length = hid.shape
    rows = w_ref.shape[1]
    per = rows // n_ch
    cs = per // 3
    nm = rates_ref.shape[1]
    st = cs * nm
    half = length // 2
    nk = length // CL
    quarter = length // 4

    def zz(k):
        return lax.rem(z + (k + n_ch), n_ch)

    ring = (zz(1), zz(-1))
    ring2 = (zz(2), zz(-2))
    pending = {}

    smalls = []
    pairs = ((w_in, w_ref), (rates_in, rates_ref), (res_in, res_ref), (taps_in, taps_ref), (skip_in, skip_ref))
    for i, (src, dst) in enumerate(pairs):
        cp = pltpu.make_async_copy(src, dst, small_sem.at[i])
        smalls.append(cp)
    smalls[0].start()
    loads = []
    for i in (3, 2, 1, 0):
        cp = pltpu.make_async_copy(
            hid.at[:, pl.ds(i * quarter, quarter)],
            hidv.at[:, pl.ds(i * quarter, quarter)],
            load_sem.at[i],
        )
        cp.start()
        loads.append((i, cp))
    for cp in smalls[1:]:
        cp.start()

    def hops(k):
        return (0, 1, 2, 1)[k >> 1 & 3] + (0, 1, 2, 1)[k >> 3]

    bits = n_seq.bit_length() - 1
    groups = [sorted(range(1 << b, 2 << b), key=lambda k: -hops(k)) for b in range(bits)]

    def to_later(b):
        return pl.when((p >> b) & 1 == 0)

    def to_earlier(b):
        return pl.when((p >> b) & 1 == 1)

    after = lax.rem(p + 1, n_seq)
    barrier = pltpu.get_barrier_semaphore()
    for s in [zz(k) for k in (1, 2, 3, 5, 6, 7)]:
        pl.semaphore_signal(barrier, inc=1, device_id=(p, s), device_id_type=MESH)
    for b in reversed(range(bits)):

        @to_later(b)
        def _():
            for k in groups[b]:
                pl.semaphore_signal(barrier, inc=1, device_id=(p ^ k, z), device_id_type=MESH)

    smalls[0].wait()

    def remote(key, src, dst, ssem, rsem, dev):
        pltpu.make_async_remote_copy(
            src_ref=src,
            dst_ref=dst,
            send_sem=ssem,
            recv_sem=rsem,
            device_id=dev,
            device_id_type=MESH,
        ).start()
        pending[key] = (dst, rsem)

    def waiter(ref, sem):
        return pltpu.make_async_remote_copy(
            src_ref=ref,
            dst_ref=ref,
            send_sem=sem,
            recv_sem=sem,
            device_id=(p, ring[0]),
            device_id_type=MESH,
        )

    def arrived(keys, ref, sem):
        for key in keys:
            pending.pop(key)
        waiter(ref, sem).wait_recv()

    bufs = {
        "kv": (kv_s, kv_r, sent.at[0], kv_rs, 0, 2 * cs),
        "q": (q_s, q_r, sent.at[1], q_rs, 2 * cs, cs),
    }
    toks = (pl.ds(0, half), pl.ds(half, half))

    def rows_of(kind, dest, h):
        comps = (1, 2) if kind == "kv" else (0,)
        picked = []
        for j in comps:
            pieces = [
                part[k, dest, pl.ds(j, cs, stride=3), :]
                for k in range(h * nk // 2, (h + 1) * nk // 2)
            ]
            picked.append(jnp.concatenate(pieces, axis=1))
        return jnp.concatenate(picked, axis=0)

    def own(kind, h, d, dist):
        return rows_of(kind, zz(dist if d == 0 else -dist), h)

    def long_way(h):
        return 0 if h == 1 else 1

    def send(kind, h, d, m, value):
        sbuf, rbuf, ss, rs = bufs[kind][:4]
        slot = (0, 1, 3, 5)[m] if d == long_way(h) else (None, 2, 4, 6)[m]
        sbuf[h, slot] = value.astype(bf16)
        to = (ring2, ring)[m % 2][d]
        got = rs.at[h, (0, 0, 1, 2, 2, 2, 2)[slot]]
        remote((kind, h, slot), sbuf.at[h, slot], rbuf.at[h, slot], ss, got, (p, to))

    def take(kind, h, group, first, count):
        _, rbuf, _, rs = bufs[kind][:4]
        keys = [(kind, h, first + i) for i in range(count)]
        arrived(keys, rbuf.at[h, pl.ds(first, count)], rs.at[h, group])
        return [rbuf[h, first + i].astype(f32) for i in range(count)]

    def far(kind, h):
        send(kind, h, long_way(h), 0, own(kind, h, long_way(h), 4))
        for d in (0, 1):
            send(kind, h, d, 1, own(kind, h, d, 3))

    def near(kind, h):
        for d in (0, 1):
            send(kind, h, d, 3, own(kind, h, d, 1))

    def merge_short(kind, h):
        d = 1 - long_way(h)
        (got,) = take(kind, h, 1, 2, 1)
        send(kind, h, d, 2, own(kind, h, d, 2) + got)

    def merge_long(kind, h):
        d = long_way(h)
        four, three = take(kind, h, 0, 0, 2)
        send(kind, h, d, 2, own(kind, h, d, 2) + three + four)

    def total_of(kind, h):
        row0, n = bufs[kind][4:]
        value = rows_of(kind, z, h)
        for got in take(kind, h, 2, 3, 4):
            value = value + got
        tot[row0 : row0 + n, toks[h]] = value

    for n, (i, cp) in enumerate(loads):
        cp.wait()
        tok = pl.ds(i * quarter, quarter)
        sums = mm(w_ref[...], hidv[:, tok], TN)
        for k in range(quarter // CL):
            piece = sums[:, CL * k : CL * (k + 1)].reshape(n_ch, per, CL)
            part[i * quarter // CL + k] = piece
        if n == 1:
            pl.semaphore_wait(barrier, 6 + p)
            far("kv", 1)
        if n == 3:
            far("kv", 0)
            far("q", 1)
            far("q", 0)
    for b in reversed(range(bits)):

        @to_earlier(b)
        def _():
            for k in groups[b]:
                pl.semaphore_signal(ready, inc=1, device_id=(p ^ k, z), device_id_type=MESH)

    @pl.when(p == 0)
    def _():
        halo_r[...] = jnp.zeros_like(halo_r)

    lane_st = iota((cs, st), 1)
    mine = (lane_st >> 4) == iota((cs, st), 0)
    rep = jnp.where((iota((nm, st), 1) & (nm - 1)) == iota((nm, st), 0), 1.0, 0.0)

    def as_row(x):
        return jnp.sum(jnp.where(mine, mm(x, rep, precision=HIGH), 0.0), axis=0, keepdims=True)

    for cp in smalls[1:]:
        cp.wait()
    lam = as_row(rates_ref[...])
    gain = as_row(res_ref[...] * jnp.sqrt(rates_ref[...]))
    steps = iota((CL, st), 0).astype(f32)
    e_hi, e_lo = halves(jnp.exp(-lam * (CL - 1 - steps)))
    e_hl[0:CL] = e_hi
    e_hl[CL : 2 * CL] = e_lo
    p_hi, p_lo = halves(gain * jnp.exp(-lam * (steps + 1.0)))
    p_hl[:, 0:st] = p_hi
    p_hl[:, st : 2 * st] = p_hi
    p_hl[:, 2 * st : 3 * st] = p_lo

    for h in (1, 0):
        merge_short("kv", h)
    for h in (1, 0):
        merge_long("kv", h)
    for h in (1, 0):
        near("kv", h)

    spread = jnp.where(mine, gain, 0.0)
    taps0 = mm(spread, jnp.exp(-lam * steps), NT, HIGH)
    causal = iota((CL, CL), 1) >= iota((CL, CL), 0)

    def lay_out(c0, c1):
        for c in range(c0, c1):
            line = jnp.broadcast_to(taps0[c : c + 1, :], (CL, CL))
            tri = jnp.where(causal, pltpu.roll(line, 0, 1, stride=1, stride_axis=0), 0.0)
            hi, lo = halves(tri)
            tcat[c, 0:CL] = hi
            tcat[c, CL : 2 * CL] = lo

    lay_out(0, 8)
    lane_per = iota((cs, per), 1)
    row_per = iota((cs, per), 0)
    for i in range(3):
        line = jnp.broadcast_to(taps_ref[i : i + 1, :], (cs, per))
        for j in range(3):
            picked = jnp.where(lane_per == 3 * row_per + j, line, 0.0)
            par[3 * i + j] = jnp.broadcast_to(jnp.sum(picked, axis=1, keepdims=True), (cs, CL))
    skip_line = jnp.broadcast_to(skip_ref[...], (cs, cs))
    skip_col = jnp.sum(
        jnp.where(iota((cs, cs), 0) == iota((cs, cs), 1), skip_line, 0.0), axis=1, keepdims=True
    )

    for h in (1, 0):
        near("q", h)
    for h in (1, 0):
        merge_short("q", h)
    for h in (1, 0):
        merge_long("q", h)
    lay_out(8, 16)
    decay_k = [jnp.exp(-lam * float(CL * k)) for k in range(nk)]
    block = lam * float(length)
    for k in range(1, n_seq):
        apart = jnp.maximum(p - 1 - (p ^ k), 0)
        weight[k] = jnp.exp(-block * apart.astype(f32))
    total_of("kv", 1)

    def tail(i, row0, n):
        halo_s[row0 : row0 + n] = tot[row0 : row0 + n, length - CL : length].astype(bf16)
        at = pl.ds(row0, n)

        @pl.when(p < n_seq - 1)
        def _():
            remote(
                ("halo", i), halo_s.at[at], halo_r.at[at], sent.at[2], halo_rs.at[i], (after, z)
            )

    def tail_in(i, row0, n):
        @pl.when(p > 0)
        def _():
            arrived([("halo", i)], halo_r.at[pl.ds(row0, n)], halo_rs.at[i])

    @pl.when(p < n_seq - 1)
    def _():
        pl.semaphore_wait(ready, n_seq - 1 - p)

    tail(0, 0, 2 * cs)
    total_of("kv", 0)

    def short(row0, j, count):
        edge = halo_r[row0 : row0 + cs].astype(f32)
        x = tot[row0 : row0 + cs, 0:count]
        ext = jnp.concatenate([edge, x], axis=1)
        one = pltpu.roll(ext, 1, 1)[:, CL:]
        two = pltpu.roll(ext, 2, 1)[:, CL:]
        t = [par[3 * i + j][:, 0:1] for i in range(3)]
        return t[0] * x + t[1] * one + t[2] * two

    def inner(row0, j):
        x = tot[row0 : row0 + cs]
        one, two = pltpu.roll(x, 1, 1), pltpu.roll(x, 2, 1)
        t = [par[3 * i + j][:, 0:1] for i in range(3)]
        return (t[0] * x + t[1] * one + t[2] * two)[:, CL:]

    def states_of(rows_bf):
        return mm(jnp.concatenate([rows_bf, rows_bf], axis=1), e_hl[...])

    later = (inner(0, 1) * inner(cs, 2)).astype(bf16)
    stacked = jnp.concatenate([later[:, CL * k : CL * (k + 1)] for k in range(nk - 1)], axis=0)
    dscr[cs:] = stacked.astype(f32)
    states = states_of(stacked)
    carry = jnp.zeros((cs, st), f32)
    for k in range(1, nk):
        xscr[cs * k : cs * (k + 1)] = carry
        carry = decay_k[1] * carry + jnp.where(mine, states[cs * (k - 1) : cs * k], 0.0)

    tail_in(0, 0, 2 * cs)
    leading = (short(0, 1, CL) * short(cs, 2, CL)).astype(bf16)
    entry = jnp.where(mine, states_of(leading), 0.0)
    total = jnp.sum(carry + decay_k[nk - 1] * entry, axis=0, keepdims=True)
    st0[...] = total
    for b in reversed(range(bits)):

        @to_later(b)
        def _():
            for k in groups[b]:
                remote(("st", k), st0, st1.at[k], st_ss.at[b], st_rs.at[b], (p ^ k, z))

    dscr[0:cs] = leading.astype(f32)
    xscr[0:cs] = jnp.zeros((cs, st), f32)
    for k in range(1, nk):
        xscr[cs * k : cs * (k + 1)] += decay_k[k - 1] * entry
    total_of("q", 1)
    tail(1, 2 * cs, cs)
    total_of("q", 0)
    for c in range(cs):
        line = dscr[pl.ds(c, nk, stride=cs), :].astype(bf16)
        yscr[pl.ds(c, nk, stride=cs), :] = mm(jnp.concatenate([line, line], axis=1), tcat[c])

    tail_in(1, 2 * cs, cs)
    query = short(2 * cs, 0, length)
    into[...] = jnp.zeros_like(into)
    for b in reversed(range(bits)):

        @to_earlier(b)
        def _():
            group = pl.ds(1 << b, 1 << b)
            arrived([("st", k) for k in groups[b]], st1.at[group], st_rs.at[b])
            into[...] += jnp.sum(weight[group] * st1[group], axis=0)

    wide = jnp.where(mine, into[...], 0.0)
    x = jnp.concatenate(
        [xscr[cs * k : cs * (k + 1)] + decay_k[k] * wide for k in range(nk)], axis=0
    )
    x_hi, x_lo = halves(x)
    y = yscr[...] + mm(jnp.concatenate([x_hi, x_lo, x_hi], axis=1), p_hl[...], NT)
    for k in range(nk):
        sl = slice(cs * k, cs * (k + 1))
        tok = slice(CL * k, CL * (k + 1))
        value = query[:, tok] * (y[sl] + skip_col * dscr[sl])
        gath[z, :, tok] = value.astype(bf16)

    def piece(move, d, dist):
        tok = slice(None) if move[2] is None else toks[move[2] if d == 0 else 1 - move[2]]
        return gath.at[zz(-dist if d == 0 else dist), :, tok]

    def hand(move, d, sem):
        ref = piece(move, d, move[0])
        target = (p, zz(move[1] if d == 0 else -move[1]))
        remote(("ag", move, d), ref, ref, sent.at[3], ag_rs.at[sem], target)

    def handed(moves, d, sem, ref):
        arrived([("ag", move, way) for move in moves for way in d], ref, ag_rs.at[sem])

    def straight():
        plan = ((0, 3, 0), (0, 1, None), (0, 2, None), (0, 3, 1))
        last = (3, 1, 0)
        for i, move in enumerate(plan):
            for d in (0, 1):
                hand(move, d, d if i == 0 else 4)
        for d in (0, 1):
            handed([plan[0]], (d,), d, piece(plan[0], d, 3))
            hand(last, d, 4)
        handed(plan[1:] + (last,), (0, 1), 4, gath.at[pl.ds(0, n_ch - 2)])

    def relayed():
        plan = ((0, 2, 0), (0, 2, 1), (0, 1, None), (2, 2, 0), (2, 1, 0), (2, 1, 1))
        for i, move in enumerate(plan[:3]):
            for d in (0, 1):
                hand(move, d, 2 * i + d if i < 2 else 4)
        for i in (0, 1):
            for d in (0, 1):
                handed([plan[i]], (d,), 2 * i + d, piece(plan[i], d, 2))
                if i == 0:
                    hand(plan[3], d, 4)
                hand(plan[4 + i], d, 4)
        handed(plan[2:], (0, 1), 4, gath.at[pl.ds(0, n_ch - 3)])

    pl.when(p % 2 == 0)(straight)
    pl.when(p % 2 == 1)(relayed)
    out_ref[...] = gath[...]
    assert not pending
    for i, ref in ((0, kv_s), (1, q_s), (3, gath.at[pl.ds(0, n_ch - 1)])):
        waiter(ref, sent.at[i]).wait_send()

    @pl.when(p < n_seq - 1)
    def _():
        waiter(halo_s, sent.at[2]).wait_send()

    for b in range(bits):

        @to_later(b)
        def _():
            waiter(st1.at[pl.ds(1 << b, 1 << b)], st_ss.at[b]).wait_send()


def project_kernel(w_ref, x_ref, out, rows_ref, sem):
    count = sem.shape[0]
    tile = out.shape[0] // count
    copies = []
    for i in range(count):
        at = pl.ds(i * tile, tile)
        rows_ref[at] = mm(w_ref[at], x_ref[...]).astype(bf16)
        cp = pltpu.make_async_copy(rows_ref.at[at], out.at[at], sem.at[i])
        cp.start()
        copies.append(cp)
    for cp in copies:
        cp.wait()


def solution(mesh):
    n_seq, n_ch = mesh.shape["seq"], mesh.shape["ch"]

    def body(hidden_in, w_in, short_taps, rates, residues, skip_gain, w_out):
        depth, length = hidden_in.shape
        rows = w_in.shape[1]
        per = rows // n_ch
        cs = per // 3
        st = cs * rates.shape[1]
        half = length // 2
        nk = length // CL
        bits = n_seq.bit_length() - 1
        vmem = pl.BlockSpec(memory_space=pltpu.VMEM)
        dma = pltpu.SemaphoreType.DMA
        gathered = pl.pallas_call(
            functools.partial(conv_kernel, n_seq, n_ch),
            out_shape=jax.ShapeDtypeStruct((n_ch, cs, length), bf16),
            in_specs=[pl.BlockSpec(memory_space=pltpu.HBM)] * 6,
            out_specs=vmem,
            scratch_shapes=[
                pltpu.VMEM(w_in.shape, bf16),
                pltpu.VMEM(short_taps.shape, f32),
                pltpu.VMEM(rates.shape, f32),
                pltpu.VMEM(residues.shape, f32),
                pltpu.VMEM((1, cs), f32),
                pltpu.VMEM((depth, length), bf16),
                pltpu.VMEM((nk, n_ch, per, CL), f32),
                pltpu.VMEM((2, 7, 2 * cs, half), bf16),
                pltpu.VMEM((2, 7, 2 * cs, half), bf16),
                pltpu.VMEM((2, 7, cs, half), bf16),
                pltpu.VMEM((2, 7, cs, half), bf16),
                pltpu.VMEM((per, length), f32),
                pltpu.VMEM((per, CL), bf16),
                pltpu.VMEM((per, CL), bf16),
                pltpu.VMEM((n_ch, cs, length), bf16),
                pltpu.VMEM((1, st), f32),
                pltpu.VMEM((n_seq, 1, st), f32),
                pltpu.VMEM((n_seq, 1, st), f32),
                pltpu.VMEM((1, st), f32),
                pltpu.VMEM((9, cs, CL), f32),
                pltpu.VMEM((2 * CL, st), bf16),
                pltpu.VMEM((CL, 3 * st), bf16),
                pltpu.VMEM((cs, 2 * CL, CL), bf16),
                pltpu.VMEM((nk * cs, CL), f32),
                pltpu.VMEM((nk * cs, CL), f32),
                pltpu.VMEM((nk * cs, st), f32),
                dma((4,)),
                dma((5,)),
                dma((4,)),
                dma((2, 3)),
                dma((2, 3)),
                dma((2,)),
                dma((bits,)),
                dma((bits,)),
                pltpu.SemaphoreType.REGULAR,
                dma((5,)),
            ],
            compiler_params=pltpu.CompilerParams(
                collective_id=0, has_side_effects=True, vmem_limit_bytes=40 * 1024 * 1024
            ),
        )(
            *(
                pltpu.with_memory_space_constraint(x, pltpu.HBM)
                for x in (hidden_in, w_in, short_taps, rates, residues, skip_gain.reshape(1, cs))
            )
        )
        slab = n_ch * cs
        return pl.pallas_call(
            project_kernel,
            out_shape=jax.ShapeDtypeStruct((w_out.shape[0], length), bf16),
            in_specs=[vmem] * 2,
            out_specs=pl.BlockSpec(memory_space=pl.ANY),
            scratch_shapes=[pltpu.VMEM((w_out.shape[0], length), bf16), dma((8,))],
            compiler_params=pltpu.CompilerParams(vmem_limit_bytes=16 * 1024 * 1024),
        )(w_out, gathered.reshape(slab, length))

    in_specs = (
        P("ch", "seq"),
        P("ch", None),
        P(None, "ch"),
        P("ch", None),
        P("ch", None),
        P("ch"),
        P("ch", None),
    )
    return jax.shard_map(
        body, mesh=mesh, in_specs=in_specs, out_specs=P("ch", "seq"), check_vma=False
    )
```

```python
import functools

import jax
import jax.numpy as jnp
from jax import lax
from jax.experimental import pallas as pl
from jax.experimental.pallas import tpu as pltpu
from jax.sharding import PartitionSpec as P

MESH = pl.DeviceIdType.MESH
f32 = jnp.float32
bf16 = jnp.bfloat16
HIGH = lax.Precision.HIGHEST
NT = (((1,), (1,)), ((), ()))
NN = (((1,), (0,)), ((), ()))
TN = (((0,), (0,)), ((), ()))
CL = 128


def mm(a, b, dims=NN, precision=None):
    return lax.dot_general(a, b, dims, precision=precision, preferred_element_type=f32)


def halves(x):
    hi = x.astype(bf16)
    return hi, (x - hi.astype(f32)).astype(bf16)


def iota(shape, dim):
    return lax.broadcasted_iota(jnp.int32, shape, dim)


def conv_kernel(
    n_seq,
    n_ch,
    hid,
    w_in,
    taps_in,
    rates_in,
    res_in,
    skip_in,
    out_ref,
    w_ref,
    taps_ref,
    rates_ref,
    res_ref,
    skip_ref,
    hidv,
    part,
    kv_s,
    kv_r,
    q_s,
    q_r,
    tot,
    halo_s,
    halo_r,
    gath,
    st0,
    st1,
    weight,
    into,
    par,
    e_hl,
    p_hl,
    tcat,
    dscr,
    yscr,
    xscr,
    load_sem,
    small_sem,
    sent,
    kv_rs,
    q_rs,
    halo_rs,
    st_ss,
    st_rs,
    ready,
    ag_rs,
):
    p = lax.axis_index("seq")
    z = lax.axis_index("ch")
    depth, length = hid.shape
    rows = w_ref.shape[1]
    per = rows // n_ch
    cs = per // 3
    nm = rates_ref.shape[1]
    st = cs * nm
    half = length // 2
    nk = length // CL
    quarter = length // 4

    def zz(k):
        return lax.rem(z + (k + n_ch), n_ch)

    ring = (zz(1), zz(-1))
    ring2 = (zz(2), zz(-2))
    pending = {}

    smalls = []
    pairs = ((w_in, w_ref), (rates_in, rates_ref), (res_in, res_ref), (taps_in, taps_ref), (skip_in, skip_ref))
    for i, (src, dst) in enumerate(pairs):
        cp = pltpu.make_async_copy(src, dst, small_sem.at[i])
        smalls.append(cp)
    smalls[0].start()
    loads = []
    for i in (3, 2, 1, 0):
        cp = pltpu.make_async_copy(
            hid.at[:, pl.ds(i * quarter, quarter)],
            hidv.at[:, pl.ds(i * quarter, quarter)],
            load_sem.at[i],
        )
        cp.start()
        loads.append((i, cp))
    for cp in smalls[1:]:
        cp.start()

    def hops(k):
        return (0, 1, 2, 1)[k >> 1 & 3] + (0, 1, 2, 1)[k >> 3]

    bits = n_seq.bit_length() - 1
    groups = [sorted(range(1 << b, 2 << b), key=lambda k: -hops(k)) for b in range(bits)]

    def to_later(b):
        return pl.when((p >> b) & 1 == 0)

    def to_earlier(b):
        return pl.when((p >> b) & 1 == 1)

    after = lax.rem(p + 1, n_seq)
    barrier = pltpu.get_barrier_semaphore()
    for s in [zz(k) for k in (1, 2, 3, 5, 6, 7)]:
        pl.semaphore_signal(barrier, inc=1, device_id=(p, s), device_id_type=MESH)
    for b in reversed(range(bits)):

        @to_later(b)
        def _():
            for k in groups[b]:
                pl.semaphore_signal(barrier, inc=1, device_id=(p ^ k, z), device_id_type=MESH)

    smalls[0].wait()

    def remote(key, src, dst, ssem, rsem, dev):
        pltpu.make_async_remote_copy(
            src_ref=src,
            dst_ref=dst,
            send_sem=ssem,
            recv_sem=rsem,
            device_id=dev,
            device_id_type=MESH,
        ).start()
        pending[key] = (dst, rsem)

    def waiter(ref, sem):
        return pltpu.make_async_remote_copy(
            src_ref=ref,
            dst_ref=ref,
            send_sem=sem,
            recv_sem=sem,
            device_id=(p, ring[0]),
            device_id_type=MESH,
        )

    def arrived(keys, ref, sem):
        for key in keys:
            pending.pop(key)
        waiter(ref, sem).wait_recv()

    bufs = {
        "kv": (kv_s, kv_r, sent.at[0], kv_rs, 0, 2 * cs),
        "q": (q_s, q_r, sent.at[1], q_rs, 2 * cs, cs),
    }
    toks = (pl.ds(0, half), pl.ds(half, half))

    def rows_of(kind, dest, h):
        comps = (1, 2) if kind == "kv" else (0,)
        picked = []
        for j in comps:
            pieces = [
                part[k, dest, pl.ds(j, cs, stride=3), :]
                for k in range(h * nk // 2, (h + 1) * nk // 2)
            ]
            picked.append(jnp.concatenate(pieces, axis=1))
        return jnp.concatenate(picked, axis=0)

    def own(kind, h, d, dist):
        return rows_of(kind, zz(dist if d == 0 else -dist), h)

    def long_way(h):
        return 0 if h == 1 else 1

    def send(kind, h, d, m, value):
        sbuf, rbuf, ss, rs = bufs[kind][:4]
        slot = (0, 1, 3, 5)[m] if d == long_way(h) else (None, 2, 4, 6)[m]
        sbuf[h, slot] = value.astype(bf16)
        to = (ring2, ring)[m % 2][d]
        got = rs.at[h, (0, 0, 1, 2, 2, 2, 2)[slot]]
        remote((kind, h, slot), sbuf.at[h, slot], rbuf.at[h, slot], ss, got, (p, to))

    def take(kind, h, group, first, count):
        _, rbuf, _, rs = bufs[kind][:4]
        keys = [(kind, h, first + i) for i in range(count)]
        arrived(keys, rbuf.at[h, pl.ds(first, count)], rs.at[h, group])
        return [rbuf[h, first + i].astype(f32) for i in range(count)]

    def far(kind, h):
        send(kind, h, long_way(h), 0, own(kind, h, long_way(h), 4))
        for d in (0, 1):
            send(kind, h, d, 1, own(kind, h, d, 3))

    def near(kind, h):
        for d in (0, 1):
            send(kind, h, d, 3, own(kind, h, d, 1))

    def merge_short(kind, h):
        d = 1 - long_way(h)
        (got,) = take(kind, h, 1, 2, 1)
        send(kind, h, d, 2, own(kind, h, d, 2) + got)

    def merge_long(kind, h):
        d = long_way(h)
        four, three = take(kind, h, 0, 0, 2)
        send(kind, h, d, 2, own(kind, h, d, 2) + three + four)

    def total_of(kind, h):
        row0, n = bufs[kind][4:]
        value = rows_of(kind, z, h)
        for got in take(kind, h, 2, 3, 4):
            value = value + got
        tot[row0 : row0 + n, toks[h]] = value

    for n, (i, cp) in enumerate(loads):
        cp.wait()
        tok = pl.ds(i * quarter, quarter)
        sums = mm(w_ref[...], hidv[:, tok], TN)
        for k in range(quarter // CL):
            piece = sums[:, CL * k : CL * (k + 1)].reshape(n_ch, per, CL)
            part[i * quarter // CL + k] = piece
        if n == 1:
            pl.semaphore_wait(barrier, 6 + p)
            far("kv", 1)
        if n == 3:
            far("kv", 0)
            far("q", 1)
            far("q", 0)
    for b in reversed(range(bits)):

        @to_earlier(b)
        def _():
            for k in groups[b]:
                pl.semaphore_signal(ready, inc=1, device_id=(p ^ k, z), device_id_type=MESH)

    @pl.when(p == 0)
    def _():
        halo_r[...] = jnp.zeros_like(halo_r)

    lane_st = iota((cs, st), 1)
    mine = (lane_st >> 4) == iota((cs, st), 0)
    rep = jnp.where((iota((nm, st), 1) & (nm - 1)) == iota((nm, st), 0), 1.0, 0.0)

    def as_row(x):
        return jnp.sum(jnp.where(mine, mm(x, rep, precision=HIGH), 0.0), axis=0, keepdims=True)

    for cp in smalls[1:]:
        cp.wait()
    lam = as_row(rates_ref[...])
    gain = as_row(res_ref[...] * jnp.sqrt(rates_ref[...]))
    steps = iota((CL, st), 0).astype(f32)
    e_hi, e_lo = halves(jnp.exp(-lam * (CL - 1 - steps)))
    e_hl[0:CL] = e_hi
    e_hl[CL : 2 * CL] = e_lo
    p_hi, p_lo = halves(jnp.transpose(gain * jnp.exp(-lam * (steps + 1.0))))
    p_hl[0:st] = p_hi
    p_hl[st : 2 * st] = p_hi
    p_hl[2 * st : 3 * st] = p_lo

    for h in (1, 0):
        merge_short("kv", h)
    for h in (1, 0):
        merge_long("kv", h)
    for h in (1, 0):
        near("kv", h)

    spread = jnp.where(mine, gain, 0.0)
    taps0 = mm(spread, jnp.exp(-lam * steps), NT, HIGH)
    causal = iota((CL, CL), 1) >= iota((CL, CL), 0)

    def lay_out(c0, c1):
        for c in range(c0, c1):
            line = jnp.broadcast_to(taps0[c : c + 1, :], (CL, CL))
            tri = jnp.where(causal, pltpu.roll(line, 0, 1, stride=1, stride_axis=0), 0.0)
            hi, lo = halves(tri)
            tcat[c, 0:CL] = hi
            tcat[c, CL : 2 * CL] = lo

    lay_out(0, 8)
    lane_per = iota((cs, per), 1)
    row_per = iota((cs, per), 0)
    for i in range(3):
        line = jnp.broadcast_to(taps_ref[i : i + 1, :], (cs, per))
        for j in range(3):
            picked = jnp.where(lane_per == 3 * row_per + j, line, 0.0)
            par[3 * i + j] = jnp.broadcast_to(jnp.sum(picked, axis=1, keepdims=True), (cs, CL))
    skip_line = jnp.broadcast_to(skip_ref[...], (cs, cs))
    skip_col = jnp.sum(
        jnp.where(iota((cs, cs), 0) == iota((cs, cs), 1), skip_line, 0.0), axis=1, keepdims=True
    )

    for h in (1, 0):
        near("q", h)
    for h in (1, 0):
        merge_short("q", h)
    for h in (1, 0):
        merge_long("q", h)
    lay_out(8, 16)
    decay_k = [jnp.exp(-lam * float(CL * k)) for k in range(nk)]
    block = lam * float(length)
    for k in range(1, n_seq):
        apart = jnp.maximum(p - 1 - (p ^ k), 0)
        weight[k] = jnp.exp(-block * apart.astype(f32))
    total_of("kv", 1)

    def tail(i, row0, n):
        halo_s[row0 : row0 + n] = tot[row0 : row0 + n, length - CL : length].astype(bf16)
        at = pl.ds(row0, n)

        @pl.when(p < n_seq - 1)
        def _():
            remote(
                ("halo", i), halo_s.at[at], halo_r.at[at], sent.at[2], halo_rs.at[i], (after, z)
            )

    def tail_in(i, row0, n):
        @pl.when(p > 0)
        def _():
            arrived([("halo", i)], halo_r.at[pl.ds(row0, n)], halo_rs.at[i])

    @pl.when(p < n_seq - 1)
    def _():
        pl.semaphore_wait(ready, n_seq - 1 - p)

    tail(0, 0, 2 * cs)
    total_of("kv", 0)

    def short(row0, j, count):
        edge = halo_r[row0 : row0 + cs].astype(f32)
        x = tot[row0 : row0 + cs, 0:count]
        ext = jnp.concatenate([edge, x], axis=1)
        one = pltpu.roll(ext, 1, 1)[:, CL:]
        two = pltpu.roll(ext, 2, 1)[:, CL:]
        t = [par[3 * i + j][:, 0:1] for i in range(3)]
        return t[0] * x + t[1] * one + t[2] * two

    def inner(row0, j):
        x = tot[row0 : row0 + cs]
        one, two = pltpu.roll(x, 1, 1), pltpu.roll(x, 2, 1)
        t = [par[3 * i + j][:, 0:1] for i in range(3)]
        return (t[0] * x + t[1] * one + t[2] * two)[:, CL:]

    def states_of(rows_bf):
        return mm(jnp.concatenate([rows_bf, rows_bf], axis=1), e_hl[...])

    later = (inner(0, 1) * inner(cs, 2)).astype(bf16)
    stacked = jnp.concatenate([later[:, CL * k : CL * (k + 1)] for k in range(nk - 1)], axis=0)
    dscr[cs:] = stacked.astype(f32)
    states = states_of(stacked)
    carry = jnp.zeros((cs, st), f32)
    for k in range(1, nk):
        xscr[cs * k : cs * (k + 1)] = carry
        carry = decay_k[1] * carry + jnp.where(mine, states[cs * (k - 1) : cs * k], 0.0)

    tail_in(0, 0, 2 * cs)
    leading = (short(0, 1, CL) * short(cs, 2, CL)).astype(bf16)
    entry = jnp.where(mine, states_of(leading), 0.0)
    total = jnp.sum(carry + decay_k[nk - 1] * entry, axis=0, keepdims=True)
    st0[...] = total
    for b in (3, 4, 2, 1, 0):

        @to_later(b)
        def _():
            for k in sorted(groups[b], key=lambda k: -(k >> 3)):
                remote(("st", k), st0, st1.at[k], st_ss.at[b], st_rs.at[b], (p ^ k, z))

    dscr[0:cs] = leading.astype(f32)
    xscr[0:cs] = jnp.zeros((cs, st), f32)
    for k in range(1, nk):
        xscr[cs * k : cs * (k + 1)] += decay_k[k - 1] * entry
    total_of("q", 1)
    tail(1, 2 * cs, cs)
    total_of("q", 0)
    for c in range(cs):
        line = dscr[pl.ds(c, nk, stride=cs), :].astype(bf16)
        yscr[pl.ds(c, nk, stride=cs), :] = mm(jnp.concatenate([line, line], axis=1), tcat[c])

    def carried(x):
        x_hi, x_lo = halves(x)
        return mm(jnp.concatenate([x_hi, x_lo, x_hi], axis=1), p_hl[...])

    yscr[...] += carried(xscr[...])
    tail_in(1, 2 * cs, cs)
    query = short(2 * cs, 0, length)
    into[...] = jnp.zeros_like(into)
    for b in reversed(range(bits)):

        @to_earlier(b)
        def _():
            group = pl.ds(1 << b, 1 << b)
            arrived([("st", k) for k in groups[b]], st1.at[group], st_rs.at[b])
            into[...] += jnp.sum(weight[group] * st1[group], axis=0)

    wide = jnp.where(mine, into[...], 0.0)
    y = yscr[...] + carried(jnp.concatenate([decay_k[k] * wide for k in range(nk)], axis=0))
    for k in range(nk):
        sl = slice(cs * k, cs * (k + 1))
        tok = slice(CL * k, CL * (k + 1))
        value = query[:, tok] * (y[sl] + skip_col * dscr[sl])
        gath[z, :, tok] = value.astype(bf16)

    def piece(move, d, dist):
        tok = slice(None) if move[2] is None else toks[move[2] if d == 0 else 1 - move[2]]
        return gath.at[zz(-dist if d == 0 else dist), :, tok]

    def hand(move, d, sem):
        ref = piece(move, d, move[0])
        target = (p, zz(move[1] if d == 0 else -move[1]))
        remote(("ag", move, d), ref, ref, sent.at[3], ag_rs.at[sem], target)

    def handed(moves, d, sem, ref):
        arrived([("ag", move, way) for move in moves for way in d], ref, ag_rs.at[sem])

    def straight():
        plan = ((0, 3, 0), (0, 1, None), (0, 2, None), (0, 3, 1))
        last = (3, 1, 0)
        for i, move in enumerate(plan):
            for d in (0, 1):
                hand(move, d, d if i == 0 else 4)
        for d in (0, 1):
            handed([plan[0]], (d,), d, piece(plan[0], d, 3))
            hand(last, d, 4)
        handed(plan[1:] + (last,), (0, 1), 4, gath.at[pl.ds(0, n_ch - 2)])

    def relayed():
        plan = ((0, 2, 0), (0, 2, 1), (0, 1, None), (2, 2, 0), (2, 1, 0), (2, 1, 1))
        for i, move in enumerate(plan[:3]):
            for d in (0, 1):
                hand(move, d, 2 * i + d if i < 2 else 4)
        for i in (0, 1):
            for d in (0, 1):
                handed([plan[i]], (d,), 2 * i + d, piece(plan[i], d, 2))
                if i == 0:
                    hand(plan[3], d, 4)
                hand(plan[4 + i], d, 4)
        handed(plan[2:], (0, 1), 4, gath.at[pl.ds(0, n_ch - 3)])

    pl.when(p % 2 == 0)(straight)
    pl.when(p % 2 == 1)(relayed)
    out_ref[...] = gath[...]
    assert not pending
    for i, ref in ((0, kv_s), (1, q_s), (3, gath.at[pl.ds(0, n_ch - 1)])):
        waiter(ref, sent.at[i]).wait_send()

    @pl.when(p < n_seq - 1)
    def _():
        waiter(halo_s, sent.at[2]).wait_send()

    for b in range(bits):

        @to_later(b)
        def _():
            waiter(st1.at[pl.ds(1 << b, 1 << b)], st_ss.at[b]).wait_send()


def project_kernel(w_ref, x_ref, out, rows_ref, sem):
    count = sem.shape[0]
    tile = out.shape[0] // count
    copies = []
    for i in range(count):
        at = pl.ds(i * tile, tile)
        rows_ref[at] = mm(w_ref[at], x_ref[...]).astype(bf16)
        cp = pltpu.make_async_copy(rows_ref.at[at], out.at[at], sem.at[i])
        cp.start()
        copies.append(cp)
    for cp in copies:
        cp.wait()


def solution(mesh):
    n_seq, n_ch = mesh.shape["seq"], mesh.shape["ch"]

    def body(hidden_in, w_in, short_taps, rates, residues, skip_gain, w_out):
        depth, length = hidden_in.shape
        rows = w_in.shape[1]
        per = rows // n_ch
        cs = per // 3
        st = cs * rates.shape[1]
        half = length // 2
        nk = length // CL
        bits = n_seq.bit_length() - 1
        vmem = pl.BlockSpec(memory_space=pltpu.VMEM)
        dma = pltpu.SemaphoreType.DMA
        gathered = pl.pallas_call(
            functools.partial(conv_kernel, n_seq, n_ch),
            out_shape=jax.ShapeDtypeStruct((n_ch, cs, length), bf16),
            in_specs=[pl.BlockSpec(memory_space=pltpu.HBM)] * 6,
            out_specs=vmem,
            scratch_shapes=[
                pltpu.VMEM(w_in.shape, bf16),
                pltpu.VMEM(short_taps.shape, f32),
                pltpu.VMEM(rates.shape, f32),
                pltpu.VMEM(residues.shape, f32),
                pltpu.VMEM((1, cs), f32),
                pltpu.VMEM((depth, length), bf16),
                pltpu.VMEM((nk, n_ch, per, CL), f32),
                pltpu.VMEM((2, 7, 2 * cs, half), bf16),
                pltpu.VMEM((2, 7, 2 * cs, half), bf16),
                pltpu.VMEM((2, 7, cs, half), bf16),
                pltpu.VMEM((2, 7, cs, half), bf16),
                pltpu.VMEM((per, length), f32),
                pltpu.VMEM((per, CL), bf16),
                pltpu.VMEM((per, CL), bf16),
                pltpu.VMEM((n_ch, cs, length), bf16),
                pltpu.VMEM((1, st), f32),
                pltpu.VMEM((n_seq, 1, st), f32),
                pltpu.VMEM((n_seq, 1, st), f32),
                pltpu.VMEM((1, st), f32),
                pltpu.VMEM((9, cs, CL), f32),
                pltpu.VMEM((2 * CL, st), bf16),
                pltpu.VMEM((3 * st, CL), bf16),
                pltpu.VMEM((cs, 2 * CL, CL), bf16),
                pltpu.VMEM((nk * cs, CL), f32),
                pltpu.VMEM((nk * cs, CL), f32),
                pltpu.VMEM((nk * cs, st), f32),
                dma((4,)),
                dma((5,)),
                dma((4,)),
                dma((2, 3)),
                dma((2, 3)),
                dma((2,)),
                dma((bits,)),
                dma((bits,)),
                pltpu.SemaphoreType.REGULAR,
                dma((5,)),
            ],
            compiler_params=pltpu.CompilerParams(
                collective_id=0, has_side_effects=True, vmem_limit_bytes=40 * 1024 * 1024
            ),
        )(
            *(
                pltpu.with_memory_space_constraint(x, pltpu.HBM)
                for x in (hidden_in, w_in, short_taps, rates, residues, skip_gain.reshape(1, cs))
            )
        )
        slab = n_ch * cs
        return pl.pallas_call(
            project_kernel,
            out_shape=jax.ShapeDtypeStruct((w_out.shape[0], length), bf16),
            in_specs=[vmem] * 2,
            out_specs=pl.BlockSpec(memory_space=pl.ANY),
            scratch_shapes=[pltpu.VMEM((w_out.shape[0], length), bf16), dma((8,))],
            compiler_params=pltpu.CompilerParams(vmem_limit_bytes=16 * 1024 * 1024),
        )(w_out, gathered.reshape(slab, length))

    in_specs = (
        P("ch", "seq"),
        P("ch", None),
        P(None, "ch"),
        P("ch", None),
        P("ch", None),
        P("ch"),
        P("ch", None),
    )
    return jax.shard_map(
        body, mesh=mesh, in_specs=in_specs, out_specs=P("ch", "seq"), check_vma=False
    )
```
